512 devices in a mesh: dp: 16 (over x_hi, z), expert: 32 (over y, x_lo, core).
Axes of the slice: x: 4 (x_hi: 2, x_lo: 2; x = x_hi * 2 + x_lo), y: 8, z: 8, core: 2. Of those that a mesh axis runs over, the one named last changes fastest.
Arguments:
- tokens: bfloat16 [32, 128, 2560], P('expert', 'dp'), may hold values from -6 to 6
- teacher_ids: int32 [32, 128, 6], P('expert', 'dp'), may hold values from 0 to 127, all different within a row; in each aligned block of 128 rows (0 to 127, 128 to 255, ..., all dimensions but the last counted through in order) at most 8 rows name the same one
- route_weight: bfloat16 [32, 128, 6], P('expert', 'dp'), may hold values from 0.049804688 to 0.5
- teacher_gate: bfloat16 [128, 768, 2560], P('expert', 'dp'), may hold values from -0.125 to 0.125
- teacher_up: bfloat16 [128, 768, 2560], P('expert', 'dp'), may hold values from -0.125 to 0.125
- teacher_down: bfloat16 [128, 768, 2560], P('expert', 'dp'), may hold values from -0.21875 to 0.21875
- merged_gate: bfloat16 [32, 768, 2560], P('expert', 'dp'), may hold values from -0.125 to 0.125
- merged_up: bfloat16 [32, 768, 2560], P('expert', 'dp'), may hold values from -0.125 to 0.125
- merged_down: bfloat16 [32, 768, 2560], P('expert', 'dp'), may hold values from -0.21875 to 0.21875
Outputs:
- grad_gate: float32 [32, 768, 2560], P('expert', 'dp')
- grad_up: float32 [32, 768, 2560], P('expert', 'dp')
- grad_down: float32 [32, 768, 2560], P('expert', 'dp')
The draws below stay inside these ranges and needn't reach their ends.
Inputs may be any that keep to these rules, and one draw needn't show every extreme that they name: `teacher_ids`: A token's 6 teacher ids differ. Within one group (the 128 tokens of one index of dimension 0) no teacher is named by more than 8 tokens, and in some groups one teacher is named by exactly 8.
All inputs are finite; a program needn't handle non-finite values.
Results may differ from the reference program's by a relative error of at most 0.02.
Values may be sent and summed in bfloat16 or wider, within the bound.
No kernel may reach another device: no remote copies, remote signals or barrier semaphores. Data moves between devices by JAX's collectives and lax.ppermute only.
A program may use at most 128 MiB of HBM per device.

```python
import math
import jax
import jax.numpy as jnp
import numpy as np
from jax import lax

D = 2560
FF = 768
TOP = 6
MERGE = 4
CAP = 8
GROUP_TOK = 128
NT = 128
NS = 32
N_DP = 16
N_EXPERT = 32


def block_levels(rng, dims, pieces, low, top_value):
    loudness = 1.0
    for dim, shards_of in pieces:
        draws = jax.random.uniform(jax.random.fold_in(jax.random.fold_in(rng, 6), dim), (shards_of,), jnp.float32, low / len(pieces), top_value / len(pieces))
        loudness = loudness * jnp.repeat(jnp.exp(draws), dims[dim] // shards_of).reshape((-1,) + (1,) * (len(dims) - 1 - dim))
    return loudness


def assign_block(own_key, own, number, rows, number_of, top, bound, slope):
    ranking = jax.random.permutation(own_key, number_of)
    packed, usual = load_shares(number_of, rows * top, bound, slope, True), load_shares(number_of, rows * top, bound, slope, False)
    places = jnp.arange(number_of)

    def named(lengths, turn):
        used = int((lengths > 0).sum())
        fixed = max(1, used // 4)
        passed = fixed + (places - fixed + turn * (used - fixed)) % max(1, number_of - fixed)
        return jnp.zeros((number_of,), jnp.int32).at[ranking[jnp.where(places < fixed, places, passed)]].set(jnp.asarray(lengths, jnp.int32))

    lengths = jnp.where(number % 4 == 0, named(packed, number // 4), named(usual, number - number // 4 - 1))
    mixed = jax.random.permutation(jax.random.fold_in(own, 3), number_of)
    source_of, sink = mixed[0:number_of // 2 * 2:2], mixed[1:number_of // 2 * 2:2]
    margin = jnp.minimum(lengths[source_of] - 1, bound - lengths[sink]) // 2
    margin = jnp.where((source_of == ranking[0]) | (sink == ranking[0]) | (lengths[sink] == 0), 0, jnp.maximum(margin, 0))
    passed = jax.random.randint(jax.random.fold_in(own, 4), (number_of // 2,), 0, 1 << 20) % (margin + 1)
    lengths = lengths.at[source_of].add(-passed).at[sink].add(passed)
    labels = jnp.searchsorted(jnp.cumsum(lengths), jnp.arange(rows * top), side="right").astype(jnp.int32)
    listing = labels.reshape(top, rows).T
    listing = listing[jax.random.permutation(jax.random.fold_in(own, 1), rows)]
    turn = jax.random.randint(jax.random.fold_in(own, 2), (rows, 1), 0, top)
    return jnp.take_along_axis(listing, (jnp.arange(top)[None, :] + turn) % top, axis=1)


def load_shares(number_of, total, limit, slope, full):
    portions = [(1 << 20) // math.isqrt(standing ** slope) + 1 for standing in range(1, number_of + 1)]
    largest = limit if full else min(limit, max(-(-total // number_of), total * portions[0] // sum(portions)))
    least = 1 if total - largest >= number_of - 1 else 0
    counts, spare = [largest] + [least] * (number_of - 1), total - largest - least * (number_of - 1)
    while spare > 0:
        candidates = [i for i in range(1, number_of) if counts[i] < largest] or [i for i in range(1, number_of) if counts[i] < limit]
        whole, budget = sum([portions[i] for i in candidates]), spare
        for i in candidates:
            extra = min(limit - counts[i], max(1, budget * portions[i] // whole), spare)
            counts[i] = counts[i] + extra
            spare = spare - extra
    return np.array(counts)


def noise(key, dims, spread, limit, pieces=(), held_as=jnp.bfloat16):
    entries = jax.random.normal(key, dims, jnp.float32) * spread
    if len(pieces) > 0:
        entries = block_levels(key, dims, pieces, -0.22, 0.18) * entries
    return jnp.clip(entries, min=-limit, max=limit).astype(held_as)


def setup_inputs(seed: int = 0) -> dict:
    streams_of = jax.random.split(jax.random.key(seed), 10)
    tokens = noise(streams_of[0], (N_EXPERT, GROUP_TOK, D), 1.0, 6.0, ((0, 32), (1, 16)))
    teacher_ids_keys = jax.random.split(jax.random.fold_in(streams_of[1], 1), N_EXPERT * GROUP_TOK // GROUP_TOK)
    teacher_ids_turns = jax.random.permutation(jax.random.fold_in(streams_of[1], 3), N_EXPERT * GROUP_TOK // GROUP_TOK)
    teacher_ids = jax.vmap(lambda own, number: assign_block(jax.random.fold_in(streams_of[1], 2), own, number, GROUP_TOK, MERGE * N_EXPERT, TOP, CAP, 2))(teacher_ids_keys, teacher_ids_turns).reshape((N_EXPERT, GROUP_TOK, TOP))
    route_weight = jnp.clip(0.049804688 + 0.4501953 * jax.random.uniform(streams_of[2], (N_EXPERT, GROUP_TOK, TOP), jnp.float32) ** block_levels(streams_of[2], (N_EXPERT, GROUP_TOK, TOP), ((0, 32), (1, 16)), -0.2, 0.2), 0.049804688, 0.5).astype(jnp.bfloat16)
    teacher_gate = noise(streams_of[3], (NT, FF, D), D ** -0.5, 0.125, ((0, 32), (1, 16)))
    teacher_up = noise(streams_of[4], (NT, FF, D), D ** -0.5, 0.125, ((0, 32), (1, 16)))
    teacher_down = noise(streams_of[5], (NT, FF, D), FF ** -0.5, 0.21875, ((0, 32), (1, 16)))
    merged_gate = noise(streams_of[6], (NS, FF, D), D ** -0.5, 0.125, ((0, 32), (1, 16)))
    merged_up = noise(streams_of[7], (NS, FF, D), D ** -0.5, 0.125, ((0, 32), (1, 16)))
    merged_down = noise(streams_of[8], (NS, FF, D), FF ** -0.5, 0.21875, ((0, 32), (1, 16)))
    return dict(tokens=tokens, teacher_ids=teacher_ids, route_weight=route_weight, teacher_gate=teacher_gate, teacher_up=teacher_up, teacher_down=teacher_down, merged_gate=merged_gate, merged_up=merged_up, merged_down=merged_down)


def silu_split(value):
    logistic = jax.nn.sigmoid(value)
    return value * logistic, logistic * (1.0 + value * (1.0 - logistic))


def slot_layout(group_ids, teachers, capacity, ranks):
    flat_ids = group_ids.reshape(-1).astype(jnp.int32)
    count_all = flat_ids.shape[0]
    hits = (flat_ids[:, None] == jnp.arange(teachers, dtype=jnp.int32)[None, :]).astype(jnp.int32)
    before = jnp.cumsum(hits, axis=0) - hits
    target = flat_ids * capacity + jnp.sum(before * hits, axis=1)
    matches = target[:, None] == jnp.arange(teachers * capacity, dtype=jnp.int32)[None, :]
    source = jnp.sum(jnp.where(matches, jnp.arange(count_all, dtype=jnp.int32)[:, None], 0), axis=0).astype(jnp.int32)
    filled = jnp.any(matches, axis=0)
    return (source // ranks).astype(jnp.int32), source, filled


def group_slots(inputs):
    group_tokens, group_ids, group_weight = inputs
    token_index, slot_index, filled = slot_layout(group_ids, NT, CAP, TOP)
    slot_rows = jnp.where(filled[:, None], jnp.take(group_tokens, token_index, axis=0), jnp.zeros((), group_tokens.dtype))
    slot_weight = jnp.where(filled, jnp.take(group_weight.reshape(-1), slot_index), jnp.zeros((), group_weight.dtype))
    return slot_rows, slot_weight


def column_grads(inputs):
    slot_rows, slot_weight, t_gate, t_up, t_down, m_gate, m_up, m_down = inputs
    row_values = slot_rows.astype(jnp.float32)
    t_gate_value = jnp.einsum('gmcd,mfd->gmcf', row_values, t_gate.astype(jnp.float32))
    t_up_value = jnp.einsum('gmcd,mfd->gmcf', row_values, t_up.astype(jnp.float32))
    t_silu, t_slope = silu_split(t_gate_value)
    teacher_hidden = (t_silu * t_up_value).astype(jnp.bfloat16)
    gate_value = jnp.einsum('gmcd,fd->gmcf', row_values, m_gate.astype(jnp.float32))
    up_value = jnp.einsum('gmcd,fd->gmcf', row_values, m_up.astype(jnp.float32))
    gate_silu, gate_slope = silu_split(gate_value)
    hidden = (gate_silu * up_value).astype(jnp.bfloat16)
    blocks = FF // N_DP
    teacher_blocks = teacher_hidden.astype(jnp.float32).reshape(N_EXPERT, MERGE, CAP, N_DP, blocks)
    hidden_blocks = hidden.astype(jnp.float32).reshape(N_EXPERT, MERGE, CAP, N_DP, blocks)
    t_parts = jnp.einsum('gmcbf,mbfd->bgmcd', teacher_blocks, t_down.astype(jnp.float32).reshape(MERGE, N_DP, blocks, D))
    s_parts = jnp.einsum('gmcbf,bfd->bgmcd', hidden_blocks, m_down.astype(jnp.float32).reshape(N_DP, blocks, D))
    gap_part = (s_parts - t_parts).astype(jnp.bfloat16)
    gap_part = lax.optimization_barrier(gap_part)
    output_gap = jnp.sum(gap_part.astype(jnp.float32), axis=0)
    slot_grad = (slot_weight.astype(jnp.float32)[..., None] * output_gap).astype(jnp.bfloat16)
    slot_grad_f = slot_grad.astype(jnp.float32)
    grad_down = jnp.einsum('gmcf,gmcd->fd', hidden.astype(jnp.float32), slot_grad_f)
    hidden_grad = jnp.einsum('gmcd,fd->gmcf', slot_grad_f, m_down.astype(jnp.float32))
    gate_grad = (hidden_grad * up_value * gate_slope).astype(jnp.bfloat16)
    up_grad = (hidden_grad * gate_silu).astype(jnp.bfloat16)
    grad_gate = jnp.einsum('gmcf,gmcd->fd', gate_grad.astype(jnp.float32), row_values)
    grad_up = jnp.einsum('gmcf,gmcd->fd', up_grad.astype(jnp.float32), row_values)
    return grad_gate, grad_up, grad_down


def by_column(weights):
    return weights.reshape(N_EXPERT, MERGE, FF, D)


def reference(tokens, teacher_ids, route_weight, teacher_gate, teacher_up, teacher_down, merged_gate, merged_up, merged_down):
    slot_rows, slot_weight = lax.map(group_slots, (tokens, teacher_ids, route_weight))
    slot_rows = slot_rows.reshape(N_EXPERT, N_EXPERT, MERGE, CAP, D).transpose(1, 0, 2, 3, 4)
    slot_weight = slot_weight.reshape(N_EXPERT, N_EXPERT, MERGE, CAP).transpose(1, 0, 2, 3)
    grad_gate, grad_up, grad_down = lax.map(column_grads, (slot_rows, slot_weight, by_column(teacher_gate), by_column(teacher_up), by_column(teacher_down), merged_gate, merged_up, merged_down))
    return (grad_gate, grad_up, grad_down)
```

```python
import jax
import jax.numpy as jnp
from jax import lax
from jax.experimental import pallas as pl
from jax.experimental.pallas import tpu as pltpu
from jax.sharding import PartitionSpec as P

HALVES = 2
SIDE = 128
BF16 = jnp.bfloat16
F32 = jnp.float32
NT_DIMS = (((1,), (1,)), ((), ()))
TN_DIMS = (((0,), (0,)), ((), ()))


def dot_nt(a, b):
    return lax.dot_general(a, b, NT_DIMS, preferred_element_type=F32)


def dot_tn(a, b):
    return lax.dot_general(a, b, TN_DIMS, preferred_element_type=F32)


def dot_nn(a, b):
    return jnp.dot(a, b, preferred_element_type=F32)


def call(kernel, outs, args, scalars=0, flops=0):
    specs = [pl.BlockSpec(memory_space=pltpu.SMEM)] * scalars
    specs += [pl.BlockSpec(memory_space=pltpu.VMEM)] * (len(args) - scalars)
    return pl.pallas_call(
        kernel,
        out_shape=outs,
        in_specs=specs,
        out_specs=jax.tree.map(lambda _: pl.BlockSpec(memory_space=pltpu.VMEM), outs),
        compiler_params=pltpu.CompilerParams(vmem_limit_bytes=48 * 1024 * 1024),
        cost_estimate=pl.CostEstimate(
            flops=flops,
            bytes_accessed=sum(a.size * a.dtype.itemsize for a in args),
            transcendentals=0,
        ),
    )(*args)


def slots_kernel(ranks, place_ref, group_ref, out_ref):
    place = place_ref[0]
    features = out_ref.shape[1] - SIDE
    slots = out_ref.shape[0]
    count = group_ref.shape[0]
    side = group_ref[:, features:].astype(F32)
    slot = lax.broadcasted_iota(jnp.int32, (count, SIDE), 1)
    teacher = ((slot // 2) * 4 + place // 4).astype(F32)
    position = (2 * (place % 4) + slot % 2).astype(F32)
    hits = jnp.zeros((count, SIDE), F32)
    weight = jnp.zeros((count, SIDE), F32)
    for k in range(ranks):
        same = side[:, k : k + 1] == teacher
        hits = jnp.where(same, 1.0, hits)
        weight = jnp.where(same, side[:, ranks + k : ranks + k + 1], weight)
    later = lax.broadcasted_iota(jnp.int32, (count, count), 0)
    earlier = lax.broadcasted_iota(jnp.int32, (count, count), 1)
    below = jnp.where(earlier < later, 1.0, 0.0).astype(BF16)
    before = dot_nn(below, hits.astype(BF16))
    chosen = jnp.where((hits > 0.0) & (before == position), 1.0, 0.0)
    rows = dot_tn(chosen.astype(BF16), group_ref[:, :features])
    weights = dot_tn((chosen * weight).astype(BF16), jnp.ones((count, SIDE), BF16))
    out_ref[:, :features] = rows[:slots].astype(BF16)
    out_ref[:, features:] = weights[:slots].astype(BF16)


def silu_split(value):
    logistic = jax.nn.sigmoid(value)
    return value * logistic, logistic * (1.0 + value * (1.0 - logistic))


def hidden_kernel(rows_ref, weights_ref, hidden_ref, silu_ref, slope_ref):
    units = weights_ref.shape[1]
    features = weights_ref.shape[2]
    half = rows_ref.shape[0] // 2
    for m in range(2):
        span = slice(m * half, (m + 1) * half)
        rows = rows_ref[span, :features]
        stack = jnp.concatenate(
            [weights_ref[m], weights_ref[2 + m], weights_ref[4], weights_ref[5]], axis=0
        )
        value = dot_nt(stack, rows)
        t_silu, _ = silu_split(value[:units])
        teacher = t_silu * value[units : 2 * units]
        s_silu, s_slope = silu_split(value[2 * units : 3 * units])
        up = value[3 * units :]
        hidden_ref[:units, span] = (s_silu * up).astype(BF16)
        hidden_ref[units:, span] = teacher.astype(BF16)
        silu_ref[:, span] = s_silu
        slope_ref[:, span] = up * s_slope


def gap_kernel(hidden_ref, side_ref, down_ref, down_t_ref, grad_ref, down_grad_ref):
    ring = hidden_ref.shape[0]
    units = hidden_ref.shape[1] // 2
    rows = hidden_ref.shape[2]
    half = rows // 2
    student = jnp.concatenate([hidden_ref[i, :units] for i in range(ring)], axis=0)
    teacher = jnp.concatenate([hidden_ref[i, units:] for i in range(ring)], axis=0)
    lane = lax.broadcasted_iota(jnp.int32, (8, SIDE), 1)
    first = jnp.where(lane == 0, 1.0, 0.0).astype(BF16)
    weight = dot_nt(first, side_ref[...])[:1]
    gap = dot_nn(down_t_ref[2], student)
    t_gap = jnp.concatenate(
        [dot_nn(down_t_ref[m], teacher[:, m * half : (m + 1) * half]) for m in range(2)], axis=1
    )
    slot_grad = (weight * (gap - t_gap)).astype(BF16)
    grad_ref[...] = dot_nn(down_ref[...], slot_grad).astype(BF16)
    down_grad_ref[...] = dot_nt(student, slot_grad).astype(BF16)


def grads_kernel(parts_ref, silu_ref, slope_ref, rows_ref, own_ref, other_ref):
    features = own_ref.shape[2]
    block = own_ref.shape[1]
    total = parts_ref[0].astype(F32)
    for i in range(1, parts_ref.shape[0]):
        total += parts_ref[i].astype(F32)
    gate = (total * slope_ref[...]).astype(BF16)
    up = (total * silu_ref[...]).astype(BF16)
    stack = jnp.concatenate([gate[:block], up[:block], gate[block:], up[block:]], axis=0)
    grads = dot_nn(stack, rows_ref[:, :features])
    own_ref[0] = grads[:block]
    own_ref[1] = grads[block : 2 * block]
    other_ref[0] = grads[2 * block : 3 * block].astype(BF16)
    other_ref[1] = grads[3 * block :].astype(BF16)


def body(
    tokens,
    teacher_ids,
    route_weight,
    teacher_gate,
    teacher_up,
    teacher_down,
    merged_gate,
    merged_up,
    merged_down,
):
    n_dp = lax.axis_size("dp")
    experts = lax.axis_size("expert")
    ring = n_dp // HALVES
    local, features = tokens.shape[1], tokens.shape[2]
    ranks = teacher_ids.shape[2]
    block = merged_gate.shape[1]
    piece = features // ring
    place = lax.axis_index("dp")
    half = place // ring
    rings = [[a * ring + i for i in range(ring)] for a in range(HALVES)]
    swap = [(a * ring + i, (1 - a) * ring + i) for a in range(HALVES) for i in range(ring)]

    side = jnp.concatenate([teacher_ids[0].astype(BF16), route_weight[0]], axis=1)
    side = jnp.pad(side, ((0, 0), (0, SIDE - 2 * ranks)))
    packet = jnp.concatenate([tokens[0], side], axis=1)
    packets = jnp.broadcast_to(packet[None], (n_dp, *packet.shape))
    group = lax.all_to_all(packets, "dp", split_axis=0, concat_axis=0, tiled=True)
    group = group.reshape(n_dp * local, features + SIDE)

    def take(array, which):
        return lax.dynamic_slice_in_dim(array, 2 * which, 2, axis=0)

    sent = [take(teacher_gate, 1 - half), take(teacher_up, 1 - half), merged_gate, merged_up]
    kept = [take(teacher_gate, half), take(teacher_up, half), merged_gate, merged_up]
    come = lax.ppermute(jnp.concatenate(sent, axis=0), "dp", swap)
    weights = jnp.concatenate([jnp.concatenate(kept, axis=0), come], axis=1)

    pairs = teacher_down.reshape(HALVES, 2, block, ring, piece)
    shared = jnp.broadcast_to(
        merged_down.reshape(1, 1, block, ring, piece), (HALVES, 1, block, ring, piece)
    )
    down = jnp.concatenate([pairs, shared], axis=1).transpose(0, 3, 1, 2, 4)
    down = down.reshape(n_dp, 3, block, piece)
    down = lax.all_to_all(down, "dp", split_axis=0, concat_axis=0, tiled=True)
    down = down.reshape(HALVES, ring, 3, block, piece)
    down = jnp.where(half == 0, down, down[::-1])
    down = down.transpose(2, 1, 0, 3, 4).reshape(3, n_dp * block, piece)
    down_t = down.transpose(0, 2, 1)

    slots = call(
        lambda *refs: slots_kernel(ranks, *refs),
        jax.ShapeDtypeStruct((2 * experts, features + SIDE), BF16),
        (place[None].astype(jnp.int32), group),
        scalars=1,
    )
    slots = slots.reshape(experts, 2, features + SIDE)
    slots = lax.all_to_all(slots, "expert", split_axis=0, concat_axis=0, tiled=True)
    slots = slots.reshape(2 * experts, features + SIDE)
    rows = lax.all_gather(slots, "dp", axis=0, tiled=True, axis_index_groups=rings)
    count = rows.shape[0]

    hidden, silu, slope = call(
        hidden_kernel,
        (
            jax.ShapeDtypeStruct((4 * block, count), BF16),
            jax.ShapeDtypeStruct((2 * block, count), F32),
            jax.ShapeDtypeStruct((2 * block, count), F32),
        ),
        (rows, weights),
    )
    hidden = lax.all_gather(hidden, "dp", axis=0, axis_index_groups=rings)
    hidden_grad, down_grad = call(
        gap_kernel,
        (
            jax.ShapeDtypeStruct((n_dp * block, count), BF16),
            jax.ShapeDtypeStruct((n_dp * block, piece), BF16),
        ),
        (hidden, rows[:, features:], down[2], down_t),
    )
    parts = hidden_grad.reshape(ring, 2 * block, count)
    parts = lax.all_to_all(
        parts, "dp", split_axis=0, concat_axis=0, tiled=True, axis_index_groups=rings
    )
    own, other = call(
        grads_kernel,
        (
            jax.ShapeDtypeStruct((2, block, features), F32),
            jax.ShapeDtypeStruct((2, block, features), BF16),
        ),
        (parts, silu, slope, rows),
    )
    other = lax.ppermute(other, "dp", swap)
    grads = own + other.astype(F32)

    down_grad = down_grad.reshape(ring, HALVES, block, piece)
    down_grad = jnp.where(half == 0, down_grad, down_grad[:, ::-1])
    down_grad = down_grad.transpose(1, 0, 2, 3).reshape(n_dp, block, piece)
    down_grad = lax.all_to_all(down_grad, "dp", split_axis=0, concat_axis=0, tiled=True)
    down_grad = down_grad.reshape(HALVES, ring, block, piece).astype(F32).sum(axis=0)
    down_grad = down_grad.transpose(1, 0, 2).reshape(block, features)
    return grads[:1], grads[1:], down_grad[None]


def solution(mesh):
    placed = (P("expert", "dp", None),) * 9
    return jax.shard_map(
        body,
        mesh=mesh,
        in_specs=placed,
        out_specs=(P("expert", "dp", None),) * 3,
        check_vma=False,
    )
```

```python
import jax
import jax.numpy as jnp
from jax import lax
from jax.experimental import pallas as pl
from jax.experimental.pallas import tpu as pltpu
from jax.sharding import PartitionSpec as P

HALVES = 2
PAIR = 2
SIDE = 128
BF16 = jnp.bfloat16
F32 = jnp.float32


def dot_nn(a, b):
    return jnp.dot(a, b, preferred_element_type=F32)


def dot_nt(a, b):
    return lax.dot_general(a, b, (((1,), (1,)), ((), ())), preferred_element_type=F32)


def dot_tn(a, b):
    return lax.dot_general(a, b, (((0,), (0,)), ((), ())), preferred_element_type=F32)


def call(kernel, outs, args, scalars=0, flops=0):
    specs = [pl.BlockSpec(memory_space=pltpu.SMEM)] * scalars
    specs += [pl.BlockSpec(memory_space=pltpu.VMEM)] * (len(args) - scalars)
    return pl.pallas_call(
        kernel,
        out_shape=outs,
        in_specs=specs,
        out_specs=jax.tree.map(lambda _: pl.BlockSpec(memory_space=pltpu.VMEM), outs),
        compiler_params=pltpu.CompilerParams(vmem_limit_bytes=40 * 1024 * 1024),
        cost_estimate=pl.CostEstimate(
            flops=flops,
            bytes_accessed=sum(a.size * a.dtype.itemsize for a in args),
            transcendentals=0,
        ),
    )(*args)


def columns(total):
    return -(-total // SIDE) * SIDE


def pack_kernel(token_ref, ids_ref, weight_ref, out_ref):
    ring = out_ref.shape[0] // HALVES
    count, ranks = ids_ref.shape
    piece = token_ref.shape[1] // ring
    wide = columns(piece)
    lane = lax.broadcasted_iota(jnp.int32, (count, SIDE), 1)
    ids = ids_ref[...].astype(F32)
    weight = weight_ref[...].astype(F32)
    side = jnp.zeros((count, SIDE), F32)
    for k in range(ranks):
        side = jnp.where(lane == k, ids[:, k : k + 1], side)
        side = jnp.where(lane == ranks + k, weight[:, k : k + 1], side)
    side = side.astype(BF16)
    blank = jnp.zeros((count, wide - piece), BF16)
    for i in range(ring):
        part = token_ref[:, i * piece : (i + 1) * piece]
        row = jnp.concatenate([part, blank, side], axis=1)
        for a in range(HALVES):
            out_ref[a * ring + i] = row


def slots_kernel(ranks, piece, capacity, place_ref, group_ref, out_ref):
    ring = place_ref[1]
    half = place_ref[0] // ring
    wide = columns(piece)
    count = group_ref.shape[0]
    slots = out_ref.shape[0]
    side = group_ref[:, wide:].astype(F32)
    slot = lax.broadcasted_iota(jnp.int32, (count, slots), 1)
    column, inner = slot // (PAIR * capacity), slot % (PAIR * capacity)
    teacher = (column * HALVES * PAIR + half * PAIR + inner // capacity).astype(F32)
    position = (inner % capacity).astype(F32)
    hits = jnp.zeros((count, slots), F32)
    weight = jnp.zeros((count, slots), F32)
    for k in range(ranks):
        same = side[:, k : k + 1] == teacher
        hits = jnp.where(same, 1.0, hits)
        weight = jnp.where(same, side[:, ranks + k : ranks + k + 1], weight)
    later = lax.broadcasted_iota(jnp.int32, (count, count), 0)
    earlier = lax.broadcasted_iota(jnp.int32, (count, count), 1)
    below = jnp.where(earlier < later, 1.0, 0.0).astype(BF16)
    before = dot_nn(below, hits.astype(BF16))
    chosen = jnp.where((hits > 0.0) & (before == position), 1.0, 0.0)
    lane = lax.broadcasted_iota(jnp.int32, (count, wide), 1)
    mark = jnp.where(lane >= piece, 1.0, 0.0).astype(BF16)
    pick = jnp.concatenate([chosen, chosen * weight], axis=0).astype(BF16)
    value = jnp.concatenate([group_ref[:, :wide], mark], axis=0)
    out_ref[...] = dot_tn(pick, value).astype(BF16)


def turn_kernel(piece, capacity, rows_ref, turned_ref, weight_ref):
    count, wide = rows_ref.shape
    source = lax.broadcasted_iota(jnp.int32, (count, count), 0)
    target = lax.broadcasted_iota(jnp.int32, (count, count), 1)
    group, inner = source // (PAIR * capacity), source % (PAIR * capacity)
    goes = (inner // capacity) * (count // PAIR) + group * capacity + inner % capacity
    move = jnp.where(goes == target, 1.0, 0.0).astype(BF16)
    rows = rows_ref[...]
    turned_ref[...] = dot_tn(rows, move)[:piece].astype(BF16)
    weight_ref[...] = dot_tn(move, rows[:, wide - SIDE :]).astype(BF16)


def silu_split(value):
    logistic = jax.nn.sigmoid(value)
    return value * logistic, logistic * (1.0 + value * (1.0 - logistic))


def hidden_kernel(
    place_ref, rows_ref, t_gate_ref, t_up_ref, m_gate_ref, m_up_ref, come_ref, out_ref, silu_ref, slope_ref
):
    ring = place_ref[1]
    half = place_ref[0] // ring
    block = m_gate_ref.shape[1]
    units = 2 * block
    span = rows_ref.shape[1] // PAIR
    places = out_ref.shape[0] // PAIR
    for m in range(PAIR):
        lanes = slice(m * span, (m + 1) * span)
        own = PAIR * half + m
        stack = jnp.concatenate(
            [
                t_gate_ref[own],
                come_ref[m],
                t_up_ref[own],
                come_ref[PAIR + m],
                m_gate_ref[0],
                come_ref[2 * PAIR],
                m_up_ref[0],
                come_ref[2 * PAIR + 1],
            ],
            axis=0,
        )
        value = dot_nn(stack, rows_ref[:, lanes])
        t_silu, _ = silu_split(value[:units])
        teacher = (t_silu * value[units : 2 * units]).astype(BF16)
        s_silu, s_slope = silu_split(value[2 * units : 3 * units])
        up = value[3 * units :]
        student = (s_silu * up).astype(BF16)
        for i in range(places):
            at = m * places + i
            out_ref[at, 0] = student[:block]
            out_ref[at, 1] = student[block:]
            out_ref[at, 2] = teacher[:block]
            out_ref[at, 3] = teacher[block:]
        silu_ref[:, lanes] = s_silu
        slope_ref[:, lanes] = up * s_slope


def gap_kernel(place_ref, hidden_ref, down_ref, weight_ref, grad_ref, down_grad_ref):
    ring = hidden_ref.shape[0]
    block = hidden_ref.shape[2]
    span = hidden_ref.shape[3]
    half = place_ref[0] // ring
    second = (place_ref[0] % ring) // (ring // PAIR)
    piece = down_ref.shape[3]
    order = [(a, i) for a in range(HALVES) for i in range(ring)]
    student = jnp.concatenate([hidden_ref[i, half ^ a] for a, i in order], axis=0)
    teacher = jnp.concatenate([hidden_ref[i, 2 + (half ^ a)] for a, i in order], axis=0)
    t_down = down_ref[:, 0].reshape(HALVES * ring * block, piece)
    m_down = down_ref[:, 1].reshape(HALVES * ring * block, piece)
    gap = dot_tn(student, m_down) - dot_tn(teacher, t_down)
    start = pl.multiple_of(second * span, span)
    weight = weight_ref[pl.ds(start, span), SIDE - 1 : SIDE].astype(F32)
    slot_grad = (weight * gap).astype(BF16)
    grad = dot_nt(m_down, slot_grad).astype(BF16)
    for k, (a, i) in enumerate(order):
        grad_ref[i, half ^ a] = grad[k * block : (k + 1) * block]
    down_grad = dot_nn(student, slot_grad).astype(BF16)
    down_grad_ref[...] = down_grad.reshape(down_grad_ref.shape)


def grads_kernel(parts_ref, silu_ref, slope_ref, rows_ref, own_ref, other_ref):
    block = own_ref.shape[1]
    places = parts_ref.shape[0] // PAIR
    sums = []
    for m in range(PAIR):
        total = parts_ref[m * places].astype(F32)
        for i in range(1, places):
            total += parts_ref[m * places + i].astype(F32)
        sums.append(total)
    total = jnp.concatenate(sums, axis=1)
    gate = (total * slope_ref[...]).astype(BF16)
    up = (total * silu_ref[...]).astype(BF16)
    stack = jnp.concatenate([gate[:block], up[:block], gate[block:], up[block:]], axis=0)
    grads = dot_nt(stack, rows_ref[...])
    own_ref[0] = grads[:block]
    own_ref[1] = grads[block : 2 * block]
    other_ref[0] = grads[2 * block : 3 * block].astype(BF16)
    other_ref[1] = grads[3 * block :].astype(BF16)


def down_sum_kernel(parts_ref, out_ref):
    count, _, piece = parts_ref.shape
    quarters = out_ref.shape[1] // piece
    for q in range(quarters):
        total = parts_ref[q].astype(F32)
        for i in range(q + quarters, count, quarters):
            total += parts_ref[i].astype(F32)
        out_ref[:, q * piece : (q + 1) * piece] = total


def body(
    tokens,
    teacher_ids,
    route_weight,
    teacher_gate,
    teacher_up,
    teacher_down,
    merged_gate,
    merged_up,
    merged_down,
):
    n_dp = lax.axis_size("dp")
    experts = lax.axis_size("expert")
    ring = n_dp // HALVES
    features = tokens.shape[2]
    capacity = tokens.shape[1]
    ranks = teacher_ids.shape[2]
    block = merged_gate.shape[1]
    piece = features // ring
    quarter = features * PAIR // ring
    rows = experts * PAIR * capacity
    axis = lax.axis_index("dp").astype(jnp.int32)
    half = axis // ring
    place = jnp.stack([axis, jnp.int32(ring)])
    rings = [[a * ring + i for i in range(ring)] for a in range(HALVES)]
    swap = [(a * ring + i, (1 - a) * ring + i) for a in range(HALVES) for i in range(ring)]

    def exchange(array, axis_name, groups=None):
        return lax.all_to_all(
            array, axis_name, split_axis=0, concat_axis=0, tiled=True, axis_index_groups=groups
        )

    sent = [
        lax.dynamic_slice_in_dim(a, PAIR * (1 - half), PAIR, axis=0)
        for a in (teacher_gate, teacher_up)
    ]
    come = lax.ppermute(jnp.concatenate([*sent, merged_gate, merged_up], axis=0), "dp", swap)

    packets = call(
        pack_kernel,
        jax.ShapeDtypeStruct((n_dp, capacity, columns(piece) + SIDE), BF16),
        (tokens[0], teacher_ids[0], route_weight[0]),
    )
    group = exchange(packets, "dp").reshape(n_dp * capacity, columns(piece) + SIDE)

    pairs = teacher_down.reshape(HALVES * PAIR, block, ring // PAIR, quarter).transpose(0, 2, 1, 3)
    shared = merged_down.reshape(1, block, ring // PAIR, quarter).transpose(0, 2, 1, 3)
    shared = jnp.broadcast_to(shared, pairs.shape)
    down = jnp.stack([pairs, shared], axis=2).reshape(n_dp, 2, block, quarter)
    down, group = lax.optimization_barrier((down, group))
    down = exchange(down, "dp")

    slots = call(
        lambda *refs: slots_kernel(ranks, piece, capacity, *refs),
        jax.ShapeDtypeStruct((rows, columns(piece)), BF16),
        (place, group),
        scalars=1,
    )
    slots = exchange(slots.reshape(experts, PAIR * capacity, columns(piece)), "expert")
    turned, weight = call(
        lambda *refs: turn_kernel(piece, capacity, *refs),
        (jax.ShapeDtypeStruct((piece, rows), BF16), jax.ShapeDtypeStruct((rows, SIDE), BF16)),
        (slots.reshape(rows, columns(piece)),),
    )
    turned = lax.all_gather(turned, "dp", axis=0, tiled=True, axis_index_groups=rings)

    hidden, silu, slope = call(
        hidden_kernel,
        (
            jax.ShapeDtypeStruct((ring, 4, block, rows // PAIR), BF16),
            jax.ShapeDtypeStruct((2 * block, rows), F32),
            jax.ShapeDtypeStruct((2 * block, rows), F32),
        ),
        (place, turned, teacher_gate, teacher_up, merged_gate, merged_up, come),
        scalars=1,
    )
    hidden = exchange(hidden, "dp", rings)
    hidden_grad, down_grad = call(
        gap_kernel,
        (
            jax.ShapeDtypeStruct((ring, 2, block, rows // PAIR), BF16),
            jax.ShapeDtypeStruct((n_dp, block, quarter), BF16),
        ),
        (place, hidden, down, weight),
        scalars=1,
    )
    parts = exchange(hidden_grad.reshape(ring, 2 * block, rows // PAIR), "dp", rings)
    down_grad = exchange(down_grad, "dp")
    own, other = call(
        grads_kernel,
        (
            jax.ShapeDtypeStruct((2, block, features), F32),
            jax.ShapeDtypeStruct((2, block, features), BF16),
        ),
        (parts, silu, slope, turned),
    )
    other = lax.ppermute(other, "dp", swap)
    grad_down = call(
        down_sum_kernel, jax.ShapeDtypeStruct((block, features), F32), (down_grad,)
    )
    grad_gate = own[:1] + other[:1].astype(F32)
    grad_up = own[1:] + other[1:].astype(F32)
    return grad_gate, grad_up, grad_down[None]


def solution(mesh):
    placed = (P("expert", "dp", None),) * 9
    return jax.shard_map(
        body,
        mesh=mesh,
        in_specs=placed,
        out_specs=(P("expert", "dp", None),) * 3,
        check_vma=False,
    )
```

```python
import jax
import jax.numpy as jnp
from jax import lax
from jax.experimental import pallas as pl
from jax.experimental.pallas import tpu as pltpu
from jax.sharding import PartitionSpec as P

HALVES = 2
PAIR = 2
EARLY = (1, 7, 3, 5)
SIDE = 128
BF16 = jnp.bfloat16
F32 = jnp.float32


def dot_nn(a, b):
    return jnp.dot(a, b, preferred_element_type=F32)


def dot_nt(a, b):
    return lax.dot_general(a, b, (((1,), (1,)), ((), ())), preferred_element_type=F32)


def dot_tn(a, b):
    return lax.dot_general(a, b, (((0,), (0,)), ((), ())), preferred_element_type=F32)


def call(kernel, outs, args, scalars=0, far=(), far_outs=(), scratch=(), mib=60):
    def space(i):
        if i < scalars:
            return pl.BlockSpec(memory_space=pltpu.SMEM)
        return pl.BlockSpec(memory_space=pltpu.HBM if i in far else pltpu.VMEM)

    return pl.pallas_call(
        kernel,
        out_shape=outs,
        in_specs=[space(i) for i in range(len(args))],
        out_specs=[
            pl.BlockSpec(memory_space=pltpu.HBM if i in far_outs else pltpu.VMEM)
            for i in range(len(outs))
        ],
        scratch_shapes=scratch,
        compiler_params=pltpu.CompilerParams(vmem_limit_bytes=mib * 1024 * 1024),
        cost_estimate=pl.CostEstimate(
            flops=0,
            bytes_accessed=sum(a.size * a.dtype.itemsize for a in args),
            transcendentals=0,
        ),
    )(*args)


def start_copies(pairs, sems, first=0):
    copies = [
        pltpu.make_async_copy(source, target, sems.at[first + i])
        for i, (source, target) in enumerate(pairs)
    ]
    for copy in copies:
        copy.start()
    return copies


def wait_copies(copies):
    for copy in copies:
        copy.wait()


def columns(total):
    return -(-total // SIDE) * SIDE


def pack_kernel(
    place_ref, ids_ref, token_hbm, weight_hbm, down_ref, merged_ref, out_ref, sent_ref, token_ref, weight_ref, sems
):
    half = place_ref[0] // place_ref[1]
    pairs = [(down_ref.at[PAIR * (1 - half) + m], sent_ref.at[m]) for m in range(PAIR)]
    inputs = start_copies([(token_hbm, token_ref), (weight_hbm, weight_ref)], sems, PAIR + 1)
    copies = start_copies([*pairs, (merged_ref.at[0], sent_ref.at[PAIR])], sems)
    wait_copies(inputs)
    ring = out_ref.shape[0] // HALVES
    count, ranks = ids_ref.shape
    piece = token_ref.shape[1] // ring
    wide = columns(piece)
    lane = lax.broadcasted_iota(jnp.int32, (count, SIDE), 1)
    ids = ids_ref[...].astype(F32)
    weight = weight_ref[...].astype(F32)
    side = jnp.zeros((count, SIDE), F32)
    for k in range(ranks):
        side = jnp.where(lane == k, ids[:, k : k + 1], side)
        side = jnp.where(lane == ranks + k, weight[:, k : k + 1], side)
    side = side.astype(BF16)
    blank = jnp.zeros((count, wide - piece), BF16)
    for i in range(ring):
        part = token_ref[:, i * piece : (i + 1) * piece]
        row = jnp.concatenate([part, blank, side], axis=1)
        for a in range(HALVES):
            out_ref[a * ring + i] = row
    wait_copies(copies)


def slots_kernel(ranks, piece, capacity, place_ref, group_ref, out_ref):
    ring = place_ref[1]
    half = place_ref[0] // ring
    wide = columns(piece)
    count = group_ref.shape[0]
    slots = out_ref.shape[0]
    side = group_ref[:, wide:].astype(F32)
    slot = lax.broadcasted_iota(jnp.int32, (count, slots), 1)
    column, inner = slot // (PAIR * capacity), slot % (PAIR * capacity)
    teacher = (column * HALVES * PAIR + half * PAIR + inner // capacity).astype(F32)
    position = (inner % capacity).astype(F32)
    hits = jnp.zeros((count, slots), F32)
    weight = jnp.zeros((count, slots), F32)
    for k in range(ranks):
        same = side[:, k : k + 1] == teacher
        hits = jnp.where(same, 1.0, hits)
        weight = jnp.where(same, side[:, ranks + k : ranks + k + 1], weight)
    later = lax.broadcasted_iota(jnp.int32, (count, count), 0)
    earlier = lax.broadcasted_iota(jnp.int32, (count, count), 1)
    below = jnp.where(earlier < later, 1.0, 0.0).astype(BF16)
    before = dot_nn(below, hits.astype(BF16))
    chosen = jnp.where((hits > 0.0) & (before == position), 1.0, 0.0)
    lane = lax.broadcasted_iota(jnp.int32, (count, wide), 1)
    mark = jnp.where(lane >= piece, 1.0, 0.0).astype(BF16)
    pick = jnp.concatenate([chosen, chosen * weight], axis=0).astype(BF16)
    value = jnp.concatenate([group_ref[:, :wide], mark], axis=0)
    out_ref[...] = dot_tn(pick, value).astype(BF16)


def turn_kernel(piece, capacity, rows_ref, turned_hbm, weight_hbm, turned_ref, weight_ref, sems):
    count, wide = rows_ref.shape
    source = lax.broadcasted_iota(jnp.int32, (count, count), 0)
    target = lax.broadcasted_iota(jnp.int32, (count, count), 1)
    group, inner = source // (PAIR * capacity), source % (PAIR * capacity)
    goes = (inner // capacity) * (count // PAIR) + group * capacity + inner % capacity
    move = jnp.where(goes == target, 1.0, 0.0).astype(BF16)
    rows = rows_ref[...]
    turned_ref[...] = dot_tn(rows, move)[:piece].astype(BF16)
    copies = start_copies([(turned_ref, turned_hbm)], sems)
    weight_ref[...] = dot_tn(move, rows[:, wide - SIDE :]).astype(BF16)
    copies += start_copies([(weight_ref, weight_hbm)], sems, 1)
    wait_copies(copies)


def silu_split(value):
    logistic = jax.nn.sigmoid(value)
    return value * logistic, logistic * (1.0 + value * (1.0 - logistic))


def hidden_kernel(
    place_ref,
    rows_ref,
    t_gate_ref,
    t_up_ref,
    m_gate_ref,
    m_up_ref,
    come_ref,
    out_ref,
    silu_ref,
    slope_ref,
    row_buf,
    weight_buf,
    sems,
):
    ring = place_ref[1]
    half = place_ref[0] // ring
    block = m_gate_ref.shape[1]
    units = 2 * block
    span = rows_ref.shape[1] // PAIR
    places = out_ref.shape[0] // PAIR

    def weights(at, own_gate, come_gate, own_up, come_up):
        parts = (own_gate, come_gate, own_up, come_up)
        return [
            (part, weight_buf.at[at, pl.ds(i * block, block)]) for i, part in enumerate(parts)
        ]

    copies = []
    for m in range(PAIR):
        lanes = pl.ds(m * span, span)
        own = PAIR * half + m
        pairs = [(rows_ref.at[:, lanes], row_buf.at[m])]
        pairs += weights(
            m, t_gate_ref.at[own], come_ref.at[m], t_up_ref.at[own], come_ref.at[PAIR + m]
        )
        copies.append(start_copies(pairs, sems, 5 * m))
        if m == 0:
            pairs = weights(
                PAIR,
                m_gate_ref.at[0],
                come_ref.at[2 * PAIR],
                m_up_ref.at[0],
                come_ref.at[2 * PAIR + 1],
            )
            student_copies = start_copies(pairs, sems, 5 * PAIR)
    for m in range(PAIR):
        lanes = slice(m * span, (m + 1) * span)
        wait_copies(copies[m])
        rows = row_buf[m]
        value = dot_nn(weight_buf[m], rows)
        t_silu, _ = silu_split(value[:units])
        teacher = (t_silu * value[units:]).astype(BF16)
        if m == 0:
            wait_copies(student_copies)
        value = dot_nn(weight_buf[PAIR], rows)
        s_silu, s_slope = silu_split(value[:units])
        up = value[units:]
        student = (s_silu * up).astype(BF16)
        for i in range(places):
            at = m * places + i
            out_ref[at, 0] = student[:block]
            out_ref[at, 1] = student[block:]
            out_ref[at, 2] = teacher[:block]
            out_ref[at, 3] = teacher[block:]
        silu_ref[:, lanes] = s_silu
        slope_ref[:, lanes] = up * s_slope


def share_kernel(ring, place_ref, down_ref, merged_ref, came_ref, *refs):
    out_refs, sems = refs[:ring], refs[ring]
    half, at = place_ref[0] // ring, place_ref[0] % ring
    block = merged_ref.shape[1]
    quarter = out_refs[0].shape[2]
    pairs = []
    for k, out_ref in enumerate(out_refs):
        there = (at + k) % ring
        teacher = there // (ring // PAIR)
        start = pl.multiple_of(there % (ring // PAIR) * quarter, SIDE)
        span = pl.ds(start, quarter)
        pairs += [
            (down_ref.at[PAIR * half + teacher, :, span], out_ref.at[0, pl.ds(0, block)]),
            (came_ref.at[teacher, :, span], out_ref.at[0, pl.ds(block, block)]),
            (merged_ref.at[0, :, span], out_ref.at[1, pl.ds(0, block)]),
            (came_ref.at[PAIR, :, span], out_ref.at[1, pl.ds(block, block)]),
        ]
    wait_copies(start_copies(pairs, sems))


def gap_kernel(ring, place_ref, hidden_ref, weight_ref, *refs):
    down_refs = refs[:ring]
    grad_hbm, kept_ref, other_hbm, t_buf, m_buf, grad_ref, other_ref, sems = refs[ring:]
    block = hidden_ref.shape[2]
    units = 2 * block
    copies = []
    for i, buf in enumerate((t_buf, m_buf)):
        pairs = [
            (down_ref.at[i], buf.at[pl.ds(k * units, units)])
            for k, down_ref in enumerate(down_refs)
        ]
        copies.append(start_copies(pairs, sems, ring * i))
    span = hidden_ref.shape[3]
    at = place_ref[0] % ring
    second = at // (ring // PAIR)
    back = [(at + ring - k) % ring for k in range(ring)]
    student = jnp.concatenate([hidden_ref[i, a] for i in back for a in (0, 1)], axis=0)
    teacher = jnp.concatenate([hidden_ref[i, a] for i in back for a in (2, 3)], axis=0)
    wait_copies(copies[0])
    gap = -dot_tn(teacher, t_buf[...])
    wait_copies(copies[1])
    m_down = m_buf[...]
    gap += dot_tn(student, m_down)
    start = pl.multiple_of(second * span, span)
    weight = weight_ref[pl.ds(start, span), SIDE - 1 : SIDE].astype(F32)
    slot_grad = (weight * gap).astype(BF16)
    grad = dot_nt(m_down, slot_grad).astype(BF16)
    for k, i in enumerate(back):
        grad_ref[i] = grad[k * units : (k + 1) * units]
    copies = start_copies([(grad_ref, grad_hbm)], sems, 2 * ring)
    down_grad = dot_nn(student, slot_grad).astype(BF16)
    for k, i in enumerate(back):
        own, other = 2 * k * block, (2 * k + 1) * block
        kept_ref[i] = down_grad[own:other]
        other_ref[i] = down_grad[other : other + block]
    copies += start_copies([(other_ref, other_hbm)], sems, 2 * ring + 1)
    wait_copies(copies)


def grads_kernel(
    parts_ref,
    rows_ref,
    silu_hbm,
    slope_hbm,
    own_hbm,
    other_hbm,
    silu_ref,
    slope_ref,
    own_ref,
    other_ref,
    sems,
):
    block = own_ref.shape[1]
    places = parts_ref.shape[0] // PAIR
    inputs = start_copies([(silu_hbm, silu_ref), (slope_hbm, slope_ref)], sems)
    sums = []
    for m in range(PAIR):
        total = parts_ref[m * places].astype(F32)
        for i in range(1, places):
            total += parts_ref[m * places + i].astype(F32)
        sums.append(total)
    total = jnp.concatenate(sums, axis=1)
    wait_copies(inputs)
    gate = (total * slope_ref[...]).astype(BF16)
    up = (total * silu_ref[...]).astype(BF16)
    rows = rows_ref[...]
    grads = dot_nt(jnp.concatenate([gate[block:], up[block:]], axis=0), rows)
    other_ref[0] = grads[:block].astype(BF16)
    other_ref[1] = grads[block:].astype(BF16)
    copies = start_copies([(other_ref, other_hbm)], sems, 2)
    grads = dot_nt(jnp.concatenate([gate[:block], up[:block]], axis=0), rows)
    own_ref[0] = grads[:block]
    own_ref[1] = grads[block:]
    copies += start_copies([(own_ref, own_hbm)], sems, 3)
    wait_copies(copies)


def down_sum_kernel(parts_ref, out_ref):
    count, _, piece = parts_ref.shape
    quarters = out_ref.shape[1] // piece
    for q in range(quarters):
        total = parts_ref[q].astype(F32)
        for i in range(q + quarters, count, quarters):
            total += parts_ref[i].astype(F32)
        out_ref[:, q * piece : (q + 1) * piece] = total


def body(
    tokens,
    teacher_ids,
    route_weight,
    teacher_gate,
    teacher_up,
    teacher_down,
    merged_gate,
    merged_up,
    merged_down,
):
    n_dp = lax.axis_size("dp")
    experts = lax.axis_size("expert")
    ring = n_dp // HALVES
    features = tokens.shape[2]
    capacity = tokens.shape[1]
    ranks = teacher_ids.shape[2]
    block = merged_gate.shape[1]
    piece = features // ring
    quarter = features * PAIR // ring
    rows = experts * PAIR * capacity
    axis = lax.axis_index("dp").astype(jnp.int32)
    half = axis // ring
    place = jnp.stack([axis, jnp.int32(ring)])
    rings = [[a * ring + i for i in range(ring)] for a in range(HALVES)]
    swap = [(a * ring + i, (1 - a) * ring + i) for a in range(HALVES) for i in range(ring)]

    turns = [
        [(a * ring + i, a * ring + (i + k) % ring) for a in range(HALVES) for i in range(ring)]
        for k in range(ring)
    ]

    def exchange(array, axis_name, groups=None):
        return lax.all_to_all(
            array, axis_name, split_axis=0, concat_axis=0, tiled=True, axis_index_groups=groups
        )

    def halves(array, which):
        return lax.dynamic_slice_in_dim(array, PAIR * which, PAIR, axis=0)

    packets, sent = call(
        pack_kernel,
        (
            jax.ShapeDtypeStruct((n_dp, capacity, columns(piece) + SIDE), BF16),
            jax.ShapeDtypeStruct((PAIR + 1, block, features), BF16),
        ),
        (place, teacher_ids[0], tokens[0], route_weight[0], teacher_down, merged_down),
        scalars=1,
        far=range(2, 6),
        far_outs=(1,),
        scratch=[
            pltpu.VMEM((capacity, features), BF16),
            pltpu.VMEM((capacity, ranks), BF16),
            pltpu.SemaphoreType.DMA((PAIR + 3,)),
        ],
    )
    came = lax.ppermute(sent, "dp", swap)
    group = exchange(packets, "dp").reshape(n_dp * capacity, columns(piece) + SIDE)

    group, came = lax.optimization_barrier((group, came))
    (slots,) = call(
        lambda *refs: slots_kernel(ranks, piece, capacity, *refs),
        (jax.ShapeDtypeStruct((rows, columns(piece)), BF16),),
        (place, group),
        scalars=1,
    )
    slots = exchange(slots.reshape(experts, PAIR * capacity, columns(piece)), "expert")

    shares = call(
        lambda *refs: share_kernel(ring, *refs),
        tuple(jax.ShapeDtypeStruct((2, 2 * block, quarter), BF16) for _ in range(ring)),
        (place, teacher_down, merged_down, came),
        scalars=1,
        far=(1, 2, 3),
        far_outs=range(ring),
        scratch=[pltpu.SemaphoreType.DMA((4 * ring,))],
    )
    down = [
        shares[k] if k == 0 else lax.ppermute(shares[k], "dp", turns[k]) for k in range(ring)
    ]
    early = [down[k] for k in EARLY]
    slots, early = lax.optimization_barrier((slots, early))
    for k, array in zip(EARLY, early):
        down[k] = array

    come = lax.ppermute(
        jnp.concatenate(
            [halves(teacher_gate, 1 - half), halves(teacher_up, 1 - half), merged_gate, merged_up],
            axis=0,
        ),
        "dp",
        swap,
    )
    turned, weight = call(
        lambda *refs: turn_kernel(piece, capacity, *refs),
        (jax.ShapeDtypeStruct((piece, rows), BF16), jax.ShapeDtypeStruct((rows, SIDE), BF16)),
        (slots.reshape(rows, columns(piece)),),
        far_outs=(0, 1),
        scratch=[
            pltpu.VMEM((piece, rows), BF16),
            pltpu.VMEM((rows, SIDE), BF16),
            pltpu.SemaphoreType.DMA((2,)),
        ],
        mib=16,
    )
    turned = lax.all_gather(turned, "dp", axis=0, tiled=True, axis_index_groups=rings)
    late = [k for k in range(1, ring) if k not in EARLY]
    turned, arrays = lax.optimization_barrier((turned, [down[k] for k in late]))
    for k, array in zip(late, arrays):
        down[k] = array

    hidden, silu, slope = call(
        hidden_kernel,
        (
            jax.ShapeDtypeStruct((ring, 4, block, rows // PAIR), BF16),
            jax.ShapeDtypeStruct((2 * block, rows), F32),
            jax.ShapeDtypeStruct((2 * block, rows), F32),
        ),
        (place, turned, teacher_gate, teacher_up, merged_gate, merged_up, come),
        scalars=1,
        far=range(1, 7),
        scratch=[
            pltpu.VMEM((PAIR, features, rows // PAIR), BF16),
            pltpu.VMEM((PAIR + 1, 4 * block, features), BF16),
            pltpu.SemaphoreType.DMA((5 * PAIR + 4,)),
        ],
    )
    hidden = exchange(hidden, "dp", rings)
    hidden_grad, kept_down, other_down = call(
        lambda *refs: gap_kernel(ring, *refs),
        (
            jax.ShapeDtypeStruct((ring, 2 * block, rows // PAIR), BF16),
            jax.ShapeDtypeStruct((ring, block, quarter), BF16),
            jax.ShapeDtypeStruct((ring, block, quarter), BF16),
        ),
        (place, hidden, weight, *down),
        scalars=1,
        far=range(3, 3 + ring),
        far_outs=(0, 2),
        scratch=[
            pltpu.VMEM((n_dp * block, quarter), BF16),
            pltpu.VMEM((n_dp * block, quarter), BF16),
            pltpu.VMEM((ring, 2 * block, rows // PAIR), BF16),
            pltpu.VMEM((ring, block, quarter), BF16),
            pltpu.SemaphoreType.DMA((2 * ring + 2,)),
        ],
    )
    other_down = lax.ppermute(other_down, "dp", swap)
    parts = exchange(hidden_grad, "dp", rings)
    down_grad = exchange((kept_down.astype(F32) + other_down.astype(F32)).astype(BF16), "dp", rings)
    own, other = call(
        grads_kernel,
        (
            jax.ShapeDtypeStruct((2, block, features), F32),
            jax.ShapeDtypeStruct((2, block, features), BF16),
        ),
        (parts, turned, silu, slope),
        far=(2, 3),
        far_outs=(0, 1),
        scratch=[
            pltpu.VMEM((2 * block, rows), F32),
            pltpu.VMEM((2 * block, rows), F32),
            pltpu.VMEM((2, block, features), F32),
            pltpu.VMEM((2, block, features), BF16),
            pltpu.SemaphoreType.DMA((4,)),
        ],
    )
    other = lax.ppermute(other, "dp", swap)
    (grad_down,) = call(
        down_sum_kernel, (jax.ShapeDtypeStruct((block, features), F32),), (down_grad,), mib=16
    )
    grad_gate = own[:1] + other[:1].astype(F32)
    grad_up = own[1:] + other[1:].astype(F32)
    return grad_gate, grad_up, grad_down[None]


def solution(mesh):
    placed = (P("expert", "dp", None),) * 9
    return jax.shard_map(
        body,
        mesh=mesh,
        in_specs=placed,
        out_specs=(P("expert", "dp", None),) * 3,
        check_vma=False,
    )
```

```python
import jax
import jax.numpy as jnp
from jax import lax
from jax.experimental import pallas as pl
from jax.experimental.pallas import tpu as pltpu
from jax.sharding import PartitionSpec as P

HALVES = 2
PAIR = 2
RING = 8
SIDE = 128
BF16 = jnp.bfloat16
F32 = jnp.float32


def dot_nn(a, b):
    return jnp.dot(a, b, preferred_element_type=F32)


def dot_nt(a, b):
    return lax.dot_general(a, b, (((1,), (1,)), ((), ())), preferred_element_type=F32)


def dot_tn(a, b):
    return lax.dot_general(a, b, (((0,), (0,)), ((), ())), preferred_element_type=F32)


def call(kernel, outs, args, far=(), far_outs=(), scratch=(), mib=16):
    def space(i, alone):
        return pl.BlockSpec(memory_space=pltpu.HBM if i in alone else pltpu.VMEM)

    return pl.pallas_call(
        kernel,
        out_shape=outs,
        in_specs=[space(i, far) for i in range(len(args))],
        out_specs=[space(i, far_outs) for i in range(len(outs))],
        scratch_shapes=scratch,
        compiler_params=pltpu.CompilerParams(vmem_limit_bytes=mib * 1024 * 1024),
        cost_estimate=pl.CostEstimate(
            flops=0,
            bytes_accessed=sum(a.size * a.dtype.itemsize for a in args),
            transcendentals=0,
        ),
    )(*args)


def place():
    at = lax.axis_index("dp")
    return at // RING, at % RING


def start_copies(pairs, sems, first=0):
    copies = [
        pltpu.make_async_copy(source, target, sems.at[first + i])
        for i, (source, target) in enumerate(pairs)
    ]
    for copy in copies:
        copy.start()
    return copies


def wait_copies(copies):
    for copy in copies:
        copy.wait()


def columns(total):
    return -(-total // SIDE) * SIDE


def pack_kernel(ids_ref, token_hbm, weight_hbm, down_hbm, out_ref, sent_hbm, token_ref, weight_ref, sent_ref, sems):
    half, _ = place()
    pairs = [(down_hbm.at[PAIR * (1 - half) + m], sent_ref.at[m]) for m in range(PAIR)]
    inputs = start_copies([(token_hbm, token_ref), (weight_hbm, weight_ref)], sems)
    downs = start_copies(pairs, sems, 2)
    ranks, count = ids_ref.shape
    piece = token_ref.shape[1] // RING
    wide = columns(piece)
    lane = lax.broadcasted_iota(jnp.int32, (ranks, SIDE), 1)
    rank = lax.broadcasted_iota(jnp.int32, (ranks, SIDE), 0)
    spread = jnp.where(lane == rank, 1.0, 0.0).astype(BF16)
    side = dot_tn(ids_ref[...].astype(F32).astype(BF16), spread)
    lane = lax.broadcasted_iota(jnp.int32, (count, SIDE), 1)
    wait_copies(inputs)
    weight = weight_ref[...].astype(F32)
    for k in range(ranks):
        side = jnp.where(lane == ranks + k, weight[:, k : k + 1], side)
    side = side.astype(BF16)
    blank = jnp.zeros((count, wide - piece), BF16)
    wait_copies(downs)
    downs = start_copies([(sent_ref, sent_hbm)], sems, 2)
    for i in range(RING):
        part = token_ref[:, i * piece : (i + 1) * piece]
        row = jnp.concatenate([part, blank, side], axis=1)
        for a in range(HALVES):
            out_ref[a * RING + i] = row
    wait_copies(downs)


def slots_kernel(ranks, piece, capacity, group_ref, out_ref):
    half, _ = place()
    wide = columns(piece)
    count = group_ref.shape[0]
    slots = out_ref.shape[0]
    side = group_ref[:, wide:].astype(F32)
    slot = lax.broadcasted_iota(jnp.int32, (count, slots), 1)
    column, inner = slot // (PAIR * capacity), slot % (PAIR * capacity)
    teacher = (column * HALVES * PAIR + half * PAIR + inner // capacity).astype(F32)
    position = (inner % capacity).astype(F32)
    hits = jnp.zeros((count, slots), F32)
    weight = jnp.zeros((count, slots), F32)
    for k in range(ranks):
        same = side[:, k : k + 1] == teacher
        hits = jnp.where(same, 1.0, hits)
        weight = jnp.where(same, side[:, ranks + k : ranks + k + 1], weight)
    later = lax.broadcasted_iota(jnp.int32, (count, count), 0)
    earlier = lax.broadcasted_iota(jnp.int32, (count, count), 1)
    below = jnp.where(earlier < later, 1.0, 0.0).astype(BF16)
    before = dot_nn(below, hits.astype(BF16))
    chosen = jnp.where((hits > 0.0) & (before == position), 1.0, 0.0)
    lane = lax.broadcasted_iota(jnp.int32, (count, wide), 1)
    mark = jnp.where(lane >= piece, 1.0, 0.0).astype(BF16)
    pick = jnp.concatenate([chosen, chosen * weight], axis=0).astype(BF16)
    value = jnp.concatenate([group_ref[:, :wide], mark], axis=0)
    out_ref[...] = dot_tn(pick, value).astype(BF16)


def turn_kernel(piece, capacity, rows_ref, turned_ref, weight_ref):
    count, wide = rows_ref.shape
    source = lax.broadcasted_iota(jnp.int32, (count, count), 0)
    target = lax.broadcasted_iota(jnp.int32, (count, count), 1)
    group, inner = source // (PAIR * capacity), source % (PAIR * capacity)
    goes = (inner // capacity) * (count // PAIR) + group * capacity + inner % capacity
    move = jnp.where(goes == target, 1.0, 0.0).astype(BF16)
    rows = rows_ref[...]
    turned_ref[...] = dot_tn(rows, move)[:piece].astype(BF16)
    weight_ref[...] = dot_tn(move, rows[:, wide - SIDE :]).astype(BF16)


def silu_split(value):
    logistic = jax.nn.sigmoid(value)
    return value * logistic, logistic * (1.0 + value * (1.0 - logistic))


def hidden_kernel(
    rows_ref,
    t_gate_ref,
    t_up_ref,
    m_gate_ref,
    m_up_ref,
    come_ref,
    out_ref,
    silu_ref,
    slope_ref,
    row_buf,
    weight_buf,
    sems,
):
    half, _ = place()
    block = m_gate_ref.shape[1]
    units = 2 * block
    span = rows_ref.shape[1] // PAIR
    places = out_ref.shape[0] // PAIR

    def weights(at, own_gate, come_gate, own_up, come_up):
        parts = (own_gate, come_gate, own_up, come_up)
        return [
            (part, weight_buf.at[at, pl.ds(i * block, block)]) for i, part in enumerate(parts)
        ]

    copies = []
    for m in range(PAIR):
        lanes = pl.ds(m * span, span)
        own = PAIR * half + m
        pairs = [(rows_ref.at[:, lanes], row_buf.at[m])]
        pairs += weights(
            m, t_gate_ref.at[own], come_ref.at[m], t_up_ref.at[own], come_ref.at[PAIR + m]
        )
        copies.append(start_copies(pairs, sems, 5 * m))
        if m == 0:
            pairs = weights(
                PAIR,
                m_gate_ref.at[0],
                come_ref.at[2 * PAIR],
                m_up_ref.at[0],
                come_ref.at[2 * PAIR + 1],
            )
            student_copies = start_copies(pairs, sems, 5 * PAIR)
    for m in range(PAIR):
        lanes = slice(m * span, (m + 1) * span)
        wait_copies(copies[m])
        rows = row_buf[m]
        value = dot_nn(weight_buf[m], rows)
        t_silu, _ = silu_split(value[:units])
        teacher = (t_silu * value[units:]).astype(BF16)
        if m == 0:
            wait_copies(student_copies)
        value = dot_nn(weight_buf[PAIR], rows)
        s_silu, s_slope = silu_split(value[:units])
        up = value[units:]
        student = (s_silu * up).astype(BF16)
        for i in range(places):
            at = m * places + i
            out_ref[at, 0] = student[:block]
            out_ref[at, 1] = student[block:]
            out_ref[at, 2] = teacher[:block]
            out_ref[at, 3] = teacher[block:]
        silu_ref[:, lanes] = s_silu
        slope_ref[:, lanes] = up * s_slope


def share_kernel(down_ref, merged_ref, came_ref, out_ref):
    half, _ = place()
    quarter = out_ref.shape[3]
    for i in range(RING):
        m, q = i // (RING // PAIR), i % (RING // PAIR)
        span = slice(q * quarter, (q + 1) * quarter)
        out_ref[i, 0] = down_ref[PAIR * half + m, :, span]
        out_ref[i, 1] = came_ref[m, :, span]
        out_ref[i, 2] = merged_ref[0, :, span]


def gap_kernel(hidden_ref, weight_ref, down_ref, merged_ref, grad_ref, kept_ref, other_ref):
    block = hidden_ref.shape[2]
    span = hidden_ref.shape[3]
    _, at = place()
    ring = range(RING)
    student = jnp.concatenate([hidden_ref[i, a] for i in ring for a in (0, 1)], axis=0)
    teacher = jnp.concatenate([hidden_ref[i, a] for i in ring for a in (2, 3)], axis=0)
    t_down = jnp.concatenate([down_ref[i, a] for i in ring for a in (0, 1)], axis=0)
    m_down = jnp.concatenate([x for i in ring for x in (down_ref[i, 2], merged_ref[i])], axis=0)
    gap = dot_tn(student, m_down) - dot_tn(teacher, t_down)
    start = pl.multiple_of(at // (RING // PAIR) * span, span)
    weight = weight_ref[pl.ds(start, span), SIDE - 1 : SIDE].astype(F32)
    slot_grad = (weight * gap).astype(BF16)
    grad_ref[...] = dot_nt(m_down, slot_grad).astype(BF16).reshape(grad_ref.shape)
    down_grad = dot_nn(student, slot_grad).astype(BF16)
    for i in ring:
        own, other = 2 * i * block, (2 * i + 1) * block
        kept_ref[i] = down_grad[own:other]
        other_ref[i] = down_grad[other : other + block]


def grads_kernel(parts_ref, silu_ref, slope_ref, rows_ref, own_ref, other_ref):
    block = own_ref.shape[1]
    places = parts_ref.shape[0] // PAIR
    sums = []
    for m in range(PAIR):
        total = parts_ref[m * places].astype(F32)
        for i in range(1, places):
            total += parts_ref[m * places + i].astype(F32)
        sums.append(total)
    total = jnp.concatenate(sums, axis=1)
    gate = (total * slope_ref[...]).astype(BF16)
    up = (total * silu_ref[...]).astype(BF16)
    stack = jnp.concatenate([gate[:block], up[:block], gate[block:], up[block:]], axis=0)
    grads = dot_nt(stack, rows_ref[...])
    own_ref[0] = grads[:block]
    own_ref[1] = grads[block : 2 * block]
    other_ref[0] = grads[2 * block : 3 * block].astype(BF16)
    other_ref[1] = grads[3 * block :].astype(BF16)


def down_sum_kernel(parts_ref, out_ref):
    count, _, piece = parts_ref.shape
    quarters = out_ref.shape[1] // piece
    for q in range(quarters):
        total = parts_ref[q].astype(F32)
        for i in range(q + quarters, count, quarters):
            total += parts_ref[i].astype(F32)
        out_ref[:, q * piece : (q + 1) * piece] = total


def body(
    tokens,
    teacher_ids,
    route_weight,
    teacher_gate,
    teacher_up,
    teacher_down,
    merged_gate,
    merged_up,
    merged_down,
):
    n_dp = HALVES * RING
    experts = lax.axis_size("expert")
    features = tokens.shape[2]
    capacity = tokens.shape[1]
    ranks = teacher_ids.shape[2]
    block = merged_gate.shape[1]
    piece = features // RING
    quarter = features * PAIR // RING
    rows = experts * PAIR * capacity
    span = rows // PAIR
    half = lax.axis_index("dp") // RING
    rings = [[a * RING + i for i in range(RING)] for a in range(HALVES)]
    swap = [(a * RING + i, (1 - a) * RING + i) for a in range(HALVES) for i in range(RING)]

    def exchange(array, axis_name, groups=None):
        return lax.all_to_all(
            array, axis_name, split_axis=0, concat_axis=0, tiled=True, axis_index_groups=groups
        )

    def halves(array, which):
        return lax.dynamic_slice_in_dim(array, PAIR * which, PAIR, axis=0)

    packets, sent = call(
        pack_kernel,
        (
            jax.ShapeDtypeStruct((n_dp, capacity, columns(piece) + SIDE), BF16),
            jax.ShapeDtypeStruct((PAIR, block, features), BF16),
        ),
        (teacher_ids[0].T, tokens[0], route_weight[0], teacher_down),
        far=(1, 2, 3),
        far_outs=(1,),
        scratch=[
            pltpu.VMEM((capacity, features), BF16),
            pltpu.VMEM((capacity, ranks), BF16),
            pltpu.VMEM((PAIR, block, features), BF16),
            pltpu.SemaphoreType.DMA((PAIR + 2,)),
        ],
        mib=60,
    )
    came = lax.ppermute(sent, "dp", swap)
    group = exchange(packets, "dp").reshape(n_dp * capacity, columns(piece) + SIDE)
    group, came = lax.optimization_barrier((group, came))

    (slots,) = call(
        lambda *refs: slots_kernel(ranks, piece, capacity, *refs),
        (jax.ShapeDtypeStruct((rows, columns(piece)), BF16),),
        (group,),
    )
    slots = exchange(slots.reshape(experts, PAIR * capacity, columns(piece)), "expert")

    (down,) = call(
        share_kernel,
        (jax.ShapeDtypeStruct((RING, PAIR + 1, block, quarter), BF16),),
        (teacher_down, merged_down, came),
    )
    down = exchange(down, "dp", rings)
    merged = lax.ppermute(down[:, PAIR], "dp", swap)

    come = lax.ppermute(
        jnp.concatenate(
            [halves(teacher_gate, 1 - half), halves(teacher_up, 1 - half), merged_gate, merged_up],
            axis=0,
        ),
        "dp",
        swap,
    )
    turned, weight = call(
        lambda *refs: turn_kernel(piece, capacity, *refs),
        (jax.ShapeDtypeStruct((piece, rows), BF16), jax.ShapeDtypeStruct((rows, SIDE), BF16)),
        (slots.reshape(rows, columns(piece)),),
    )
    turned = lax.all_gather(turned, "dp", axis=0, tiled=True, axis_index_groups=rings)

    hidden, silu, slope = call(
        hidden_kernel,
        (
            jax.ShapeDtypeStruct((RING, 4, block, span), BF16),
            jax.ShapeDtypeStruct((2 * block, rows), F32),
            jax.ShapeDtypeStruct((2 * block, rows), F32),
        ),
        (turned, teacher_gate, teacher_up, merged_gate, merged_up, come),
        far=range(6),
        scratch=[
            pltpu.VMEM((PAIR, features, span), BF16),
            pltpu.VMEM((PAIR + 1, 4 * block, features), BF16),
            pltpu.SemaphoreType.DMA((5 * PAIR + 4,)),
        ],
        mib=60,
    )
    hidden = exchange(hidden, "dp", rings)
    hidden_grad, kept_down, other_down = call(
        gap_kernel,
        (
            jax.ShapeDtypeStruct((RING, 2 * block, span), BF16),
            jax.ShapeDtypeStruct((RING, block, quarter), BF16),
            jax.ShapeDtypeStruct((RING, block, quarter), BF16),
        ),
        (hidden, weight, down, merged),
    )
    other_down = lax.ppermute(other_down, "dp", swap)
    parts = exchange(hidden_grad, "dp", rings)
    own, other = call(
        grads_kernel,
        (
            jax.ShapeDtypeStruct((2, block, features), F32),
            jax.ShapeDtypeStruct((2, block, features), BF16),
        ),
        (parts, silu, slope, turned),
    )
    other = lax.ppermute(other, "dp", swap)
    down_grad = (kept_down.astype(F32) + other_down.astype(F32)).astype(BF16)
    down_grad = exchange(down_grad, "dp", rings)
    (grad_down,) = call(
        down_sum_kernel, (jax.ShapeDtypeStruct((block, features), F32),), (down_grad,)
    )
    grad_gate = own[:1] + other[:1].astype(F32)
    grad_up = own[1:] + other[1:].astype(F32)
    return grad_gate, grad_up, grad_down[None]


def solution(mesh):
    placed = (P("expert", "dp", None),) * 9
    return jax.shard_map(
        body,
        mesh=mesh,
        in_specs=placed,
        out_specs=(P("expert", "dp", None),) * 3,
        check_vma=False,
    )
```

```python
import jax
import jax.numpy as jnp
from jax import lax
from jax.experimental import pallas as pl
from jax.experimental.pallas import tpu as pltpu
from jax.sharding import PartitionSpec as P

HALVES = 2
PAIR = 2
RING = 8
SIDE = 128
BF16 = jnp.bfloat16
F32 = jnp.float32


def dot_nn(a, b):
    return jnp.dot(a, b, preferred_element_type=F32)


def dot_nt(a, b):
    return lax.dot_general(a, b, (((1,), (1,)), ((), ())), preferred_element_type=F32)


def dot_tn(a, b):
    return lax.dot_general(a, b, (((0,), (0,)), ((), ())), preferred_element_type=F32)


def call(kernel, outs, args, far=(), far_outs=(), scratch=(), mib=16):
    def space(i, alone):
        return pl.BlockSpec(memory_space=pltpu.HBM if i in alone else pltpu.VMEM)

    return pl.pallas_call(
        kernel,
        out_shape=outs,
        in_specs=[space(i, far) for i in range(len(args))],
        out_specs=[space(i, far_outs) for i in range(len(outs))],
        scratch_shapes=scratch,
        compiler_params=pltpu.CompilerParams(vmem_limit_bytes=mib * 1024 * 1024),
        cost_estimate=pl.CostEstimate(
            flops=0,
            bytes_accessed=sum(a.size * a.dtype.itemsize for a in args),
            transcendentals=0,
        ),
    )(*args)


def place():
    at = lax.axis_index("dp")
    return at // RING, at % RING


def start_copies(pairs, sems, first=0):
    copies = [
        pltpu.make_async_copy(source, target, sems.at[first + i])
        for i, (source, target) in enumerate(pairs)
    ]
    for copy in copies:
        copy.start()
    return copies


def wait_copies(copies):
    for copy in copies:
        copy.wait()


def pack_kernel(
    ids_ref, token_hbm, weight_hbm, down_hbm, merged_hbm, out_ref, sent_hbm, token_ref, weight_ref, sent_ref, sems
):
    half, _ = place()
    inputs = start_copies([(token_hbm, token_ref), (weight_hbm, weight_ref)], sems)
    pairs = [(down_hbm.at[PAIR * (1 - half) + m], sent_ref.at[m]) for m in range(PAIR)]
    downs = start_copies([*pairs, (merged_hbm.at[0], sent_ref.at[PAIR])], sems, 2)
    ranks, count = ids_ref.shape
    features = token_ref.shape[1]
    lane = lax.broadcasted_iota(jnp.int32, (ranks, SIDE), 1)
    rank = lax.broadcasted_iota(jnp.int32, (ranks, SIDE), 0)
    spread = jnp.where(lane == rank, 1.0, 0.0).astype(BF16)
    side = dot_tn(ids_ref[...].astype(F32).astype(BF16), spread)
    lane = lax.broadcasted_iota(jnp.int32, (count, SIDE), 1)
    wait_copies(inputs)
    weight = weight_ref[...].astype(F32)
    for k in range(ranks):
        side = jnp.where(lane == ranks + k, weight[:, k : k + 1], side)
    side = side.astype(BF16)
    wait_copies(downs)
    downs = start_copies([(sent_ref, sent_hbm)], sems, 2)
    tokens = token_ref[...]
    for i in range(out_ref.shape[0]):
        out_ref[i, :, :features] = tokens
        out_ref[i, :, features:] = side
    wait_copies(downs)


def slots_kernel(ranks, capacity, group_ref, out_ref):
    half, _ = place()
    wide = group_ref.shape[1] - SIDE
    count = group_ref.shape[0]
    slots = out_ref.shape[0]
    side = group_ref[:, wide:].astype(F32)
    slot = lax.broadcasted_iota(jnp.int32, (count, slots), 1)
    column, inner = slot // (PAIR * capacity), slot % (PAIR * capacity)
    teacher = (column * HALVES * PAIR + half * PAIR + inner // capacity).astype(F32)
    position = (inner % capacity).astype(F32)
    hits = jnp.zeros((count, slots), F32)
    weight = jnp.zeros((count, slots), F32)
    for k in range(ranks):
        same = side[:, k : k + 1] == teacher
        hits = jnp.where(same, 1.0, hits)
        weight = jnp.where(same, side[:, ranks + k : ranks + k + 1], weight)
    later = lax.broadcasted_iota(jnp.int32, (count, count), 0)
    earlier = lax.broadcasted_iota(jnp.int32, (count, count), 1)
    below = jnp.where(earlier < later, 1.0, 0.0).astype(BF16)
    before = dot_nn(below, hits.astype(BF16))
    chosen = jnp.where((hits > 0.0) & (before == position), 1.0, 0.0)
    out_ref[:, :wide] = dot_tn(chosen.astype(BF16), group_ref[:, :wide]).astype(BF16)
    weights = dot_tn((chosen * weight).astype(BF16), jnp.ones((count, SIDE), BF16))
    out_ref[:, wide:] = weights.astype(BF16)


def by_teacher(count, capacity, source_axis):
    source = lax.broadcasted_iota(jnp.int32, (count, count), source_axis)
    target = lax.broadcasted_iota(jnp.int32, (count, count), 1 - source_axis)
    group, inner = source // (PAIR * capacity), source % (PAIR * capacity)
    goes = (inner // capacity) * (count // PAIR) + group * capacity + inner % capacity
    return jnp.where(goes == target, 1.0, 0.0).astype(BF16)


def silu_split(value):
    logistic = jax.nn.sigmoid(value)
    return value * logistic, logistic * (1.0 + value * (1.0 - logistic))


def hidden_kernel(
    capacity,
    rows_hbm,
    t_gate_hbm,
    t_up_hbm,
    m_gate_hbm,
    m_up_hbm,
    come_hbm,
    out_ref,
    silu_ref,
    slope_ref,
    weight_ref,
    raw_buf,
    row_buf,
    weight_buf,
    sems,
):
    half, _ = place()
    block = m_gate_hbm.shape[1]
    units = 2 * block
    count, wide = raw_buf.shape
    features = wide - SIDE
    span = count // PAIR
    places = out_ref.shape[0] // PAIR
    tile = 7 * SIDE
    tiles = [slice(i, i + tile) for i in range(0, wide, tile)]

    def weights(at, own_gate, come_gate, own_up, come_up):
        parts = (own_gate, come_gate, own_up, come_up)
        return [
            (part, weight_buf.at[at, pl.ds(i * block, block)]) for i, part in enumerate(parts)
        ]

    pairs = [(rows_hbm.at[:, pl.ds(t.start, tile)], raw_buf.at[:, pl.ds(t.start, tile)]) for t in tiles]
    row_copies = start_copies(pairs, sems)
    pairs = []
    for m in range(PAIR):
        own = PAIR * half + m
        pairs += weights(
            m, t_gate_hbm.at[own], come_hbm.at[m], t_up_hbm.at[own], come_hbm.at[PAIR + m]
        )
    pairs += weights(
        PAIR,
        m_gate_hbm.at[0],
        come_hbm.at[2 * PAIR],
        m_up_hbm.at[0],
        come_hbm.at[2 * PAIR + 1],
    )
    copies = start_copies(pairs, sems, len(tiles))
    move = by_teacher(count, capacity, 1)
    for t, copy in zip(tiles, row_copies):
        copy.wait()
        row_buf[:, t] = dot_nn(move, raw_buf[:, t]).astype(BF16)
    weight_ref[...] = row_buf[:, features:]
    wait_copies(copies)
    for m in range(PAIR):
        lanes = slice(m * span, (m + 1) * span)
        rows = row_buf[lanes, :features]
        value = dot_nt(weight_buf[m], rows)
        t_silu, _ = silu_split(value[:units])
        teacher = (t_silu * value[units:]).astype(BF16)
        value = dot_nt(weight_buf[PAIR], rows)
        s_silu, s_slope = silu_split(value[:units])
        up = value[units:]
        student = (s_silu * up).astype(BF16)
        for i in range(places):
            at = m * places + i
            out_ref[at, 0] = student[:block]
            out_ref[at, 1] = student[block:]
            out_ref[at, 2] = teacher[:block]
            out_ref[at, 3] = teacher[block:]
        silu_ref[:, lanes] = s_silu
        slope_ref[:, lanes] = up * s_slope


def share_kernel(down_ref, merged_ref, came_ref, *out_refs):
    half, at = place()
    block = merged_ref.shape[1]
    quarter = out_refs[0].shape[2]
    for k, out_ref in enumerate(out_refs):
        there = (at + k) % RING
        m = there // (RING // PAIR)
        span = pl.ds(pl.multiple_of(there % (RING // PAIR) * quarter, SIDE), quarter)
        out_ref[0, :block] = down_ref[PAIR * half + m, :, span]
        out_ref[0, block:] = came_ref[m, :, span]
        out_ref[1, :block] = merged_ref[0, :, span]
        out_ref[1, block:] = came_ref[PAIR, :, span]


def gap_kernel(hidden_ref, weight_ref, *refs):
    down_refs = refs[:RING]
    grad_ref, kept_ref, other_ref = refs[RING:]
    block = hidden_ref.shape[2]
    units = 2 * block
    span = hidden_ref.shape[3]
    _, at = place()
    back = [(at + RING - k) % RING for k in range(RING)]
    student = jnp.concatenate([hidden_ref[i, a] for i in back for a in (0, 1)], axis=0)
    teacher = jnp.concatenate([hidden_ref[i, a] for i in back for a in (2, 3)], axis=0)
    t_down = jnp.concatenate([down_ref[0] for down_ref in down_refs], axis=0)
    m_down = jnp.concatenate([down_ref[1] for down_ref in down_refs], axis=0)
    gap = dot_tn(student, m_down) - dot_tn(teacher, t_down)
    start = pl.multiple_of(at // (RING // PAIR) * span, span)
    weight = weight_ref[pl.ds(start, span), SIDE - 1 : SIDE].astype(F32)
    slot_grad = (weight * gap).astype(BF16)
    grad = dot_nt(m_down, slot_grad).astype(BF16)
    down_grad = dot_nn(student, slot_grad).astype(BF16)
    for k, i in enumerate(back):
        grad_ref[i] = grad[k * units : (k + 1) * units]
        kept_ref[i] = down_grad[k * units : k * units + block]
        other_ref[i] = down_grad[k * units + block : (k + 1) * units]


def grads_kernel(capacity, parts_ref, silu_ref, slope_ref, rows_ref, own_ref, other_ref):
    block = own_ref.shape[1]
    places = parts_ref.shape[0] // PAIR
    sums = []
    for m in range(PAIR):
        total = parts_ref[m * places].astype(F32)
        for i in range(1, places):
            total += parts_ref[m * places + i].astype(F32)
        sums.append(total)
    total = jnp.concatenate(sums, axis=1)
    gate = (total * slope_ref[...]).astype(BF16)
    up = (total * silu_ref[...]).astype(BF16)
    stack = jnp.concatenate([gate[:block], up[:block], gate[block:], up[block:]], axis=0)
    stack = dot_nn(stack, by_teacher(stack.shape[1], capacity, 1)).astype(BF16)
    grads = dot_nn(stack, rows_ref[:, : own_ref.shape[2]])
    own_ref[0] = grads[:block]
    own_ref[1] = grads[block : 2 * block]
    other_ref[0] = grads[2 * block : 3 * block].astype(BF16)
    other_ref[1] = grads[3 * block :].astype(BF16)


def down_sum_kernel(parts_ref, out_ref):
    count, _, piece = parts_ref.shape
    quarters = out_ref.shape[1] // piece
    for q in range(quarters):
        total = parts_ref[q].astype(F32)
        for i in range(q + quarters, count, quarters):
            total += parts_ref[i].astype(F32)
        out_ref[:, q * piece : (q + 1) * piece] = total


def body(
    tokens,
    teacher_ids,
    route_weight,
    teacher_gate,
    teacher_up,
    teacher_down,
    merged_gate,
    merged_up,
    merged_down,
):
    n_dp = HALVES * RING
    experts = lax.axis_size("expert")
    features = tokens.shape[2]
    capacity = tokens.shape[1]
    ranks = teacher_ids.shape[2]
    block = merged_gate.shape[1]
    wide = features + SIDE
    quarter = features * PAIR // RING
    rows = experts * PAIR * capacity
    span = rows // PAIR
    half = lax.axis_index("dp") // RING
    rings = [[a * RING + i for i in range(RING)] for a in range(HALVES)]
    swap = [(a * RING + i, (1 - a) * RING + i) for a in range(HALVES) for i in range(RING)]

    turns = [
        [(a * RING + i, a * RING + (i + k) % RING) for a in range(HALVES) for i in range(RING)]
        for k in range(RING)
    ]

    def exchange(array, axis_name, groups=None):
        return lax.all_to_all(
            array, axis_name, split_axis=0, concat_axis=0, tiled=True, axis_index_groups=groups
        )

    def halves(array, which):
        return lax.dynamic_slice_in_dim(array, PAIR * which, PAIR, axis=0)

    packets, sent = call(
        pack_kernel,
        (
            jax.ShapeDtypeStruct((n_dp, capacity, wide), BF16),
            jax.ShapeDtypeStruct((PAIR + 1, block, features), BF16),
        ),
        (teacher_ids[0].T, tokens[0], route_weight[0], teacher_down, merged_down),
        far=range(1, 5),
        far_outs=(1,),
        scratch=[
            pltpu.VMEM((capacity, features), BF16),
            pltpu.VMEM((capacity, ranks), BF16),
            pltpu.VMEM((PAIR + 1, block, features), BF16),
            pltpu.SemaphoreType.DMA((PAIR + 3,)),
        ],
        mib=60,
    )
    came = lax.ppermute(sent, "dp", swap)
    group = exchange(packets, "dp").reshape(n_dp * capacity, wide)
    group, came = lax.optimization_barrier((group, came))

    (slots,) = call(
        lambda *refs: slots_kernel(ranks, capacity, *refs),
        (jax.ShapeDtypeStruct((rows, wide), BF16),),
        (group,),
        mib=60,
    )
    slots = exchange(slots.reshape(experts, PAIR * capacity, wide), "expert").reshape(rows, wide)

    down = call(
        share_kernel,
        tuple(jax.ShapeDtypeStruct((2, 2 * block, quarter), BF16) for _ in range(RING)),
        (teacher_down, merged_down, came),
    )
    down = [down[k] if k == 0 else lax.ppermute(down[k], "dp", turns[k]) for k in range(RING)]

    come = lax.ppermute(
        jnp.concatenate(
            [halves(teacher_gate, 1 - half), halves(teacher_up, 1 - half), merged_gate, merged_up],
            axis=0,
        ),
        "dp",
        swap,
    )
    slots, come, down = lax.optimization_barrier((slots, come, down))

    hidden, silu, slope, weight = call(
        lambda *refs: hidden_kernel(capacity, *refs),
        (
            jax.ShapeDtypeStruct((RING, 4, block, span), BF16),
            jax.ShapeDtypeStruct((2 * block, rows), F32),
            jax.ShapeDtypeStruct((2 * block, rows), F32),
            jax.ShapeDtypeStruct((rows, SIDE), BF16),
        ),
        (slots, teacher_gate, teacher_up, merged_gate, merged_up, come),
        far=range(6),
        scratch=[
            pltpu.VMEM((rows, wide), BF16),
            pltpu.VMEM((rows, wide), BF16),
            pltpu.VMEM((PAIR + 1, 4 * block, features), BF16),
            pltpu.SemaphoreType.DMA((32,)),
        ],
        mib=24,
    )
    hidden = exchange(hidden, "dp", rings)
    hidden_grad, kept_down, other_down = call(
        gap_kernel,
        (
            jax.ShapeDtypeStruct((RING, 2 * block, span), BF16),
            jax.ShapeDtypeStruct((RING, block, quarter), BF16),
            jax.ShapeDtypeStruct((RING, block, quarter), BF16),
        ),
        (hidden, weight, *down),
    )
    other_down = lax.ppermute(other_down, "dp", swap)
    parts = exchange(hidden_grad, "dp", rings)
    down_grad = (kept_down.astype(F32) + other_down.astype(F32)).astype(BF16)
    parts, down_grad = lax.optimization_barrier((parts, down_grad))
    down_grad = exchange(down_grad, "dp", rings)
    own, other = call(
        lambda *refs: grads_kernel(capacity, *refs),
        (
            jax.ShapeDtypeStruct((2, block, features), F32),
            jax.ShapeDtypeStruct((2, block, features), BF16),
        ),
        (parts, silu, slope, slots),
    )
    other = lax.ppermute(other, "dp", swap)
    (grad_down,) = call(
        down_sum_kernel, (jax.ShapeDtypeStruct((block, features), F32),), (down_grad,)
    )
    grad_gate = own[:1] + other[:1].astype(F32)
    grad_up = own[1:] + other[1:].astype(F32)
    return grad_gate, grad_up, grad_down[None]


def solution(mesh):
    placed = (P("expert", "dp", None),) * 9
    return jax.shard_map(
        body,
        mesh=mesh,
        in_specs=placed,
        out_specs=(P("expert", "dp", None),) * 3,
        check_vma=False,
    )
```

```python
import jax
import jax.numpy as jnp
from jax import lax
from jax.experimental import pallas as pl
from jax.experimental.pallas import tpu as pltpu
from jax.sharding import PartitionSpec as P

HALVES = 2
PAIR = 2
RING = 8
SIDE = 128
BF16 = jnp.bfloat16
F32 = jnp.float32


def dot_nn(a, b):
    return jnp.dot(a, b, preferred_element_type=F32)


def dot_nt(a, b):
    return lax.dot_general(a, b, (((1,), (1,)), ((), ())), preferred_element_type=F32)


def dot_tn(a, b):
    return lax.dot_general(a, b, (((0,), (0,)), ((), ())), preferred_element_type=F32)


def call(kernel, outs, args, mib=16, flops=0):
    space = pl.BlockSpec(memory_space=pltpu.VMEM)
    return pl.pallas_call(
        kernel,
        out_shape=outs,
        in_specs=[space] * len(args),
        out_specs=[space] * len(outs),
        compiler_params=pltpu.CompilerParams(vmem_limit_bytes=mib * 1024 * 1024),
        cost_estimate=pl.CostEstimate(
            flops=flops,
            bytes_accessed=sum(a.size * a.dtype.itemsize for a in args),
            transcendentals=0,
        ),
    )(*args)


def place():
    at = lax.axis_index("dp")
    return at // RING, at % RING


def pack_kernel(ids_ref, token_ref, weight_ref, out_ref):
    ranks, count = ids_ref.shape
    features = token_ref.shape[1]
    lane = lax.broadcasted_iota(jnp.int32, (ranks, SIDE), 1)
    rank = lax.broadcasted_iota(jnp.int32, (ranks, SIDE), 0)
    spread = jnp.where(lane == rank, 1.0, 0.0).astype(BF16)
    side = dot_tn(ids_ref[...].astype(F32).astype(BF16), spread)
    lane = lax.broadcasted_iota(jnp.int32, (count, SIDE), 1)
    weight = weight_ref[...].astype(F32)
    for k in range(ranks):
        side = jnp.where(lane == ranks + k, weight[:, k : k + 1], side)
    side = side.astype(BF16)
    tokens = token_ref[...]
    for i in range(out_ref.shape[0]):
        out_ref[i, :, :features] = tokens
        out_ref[i, :, features:] = side


def slots_kernel(ranks, capacity, group_ref, out_ref):
    half, _ = place()
    wide = group_ref.shape[1] - SIDE
    count = group_ref.shape[0]
    slots = out_ref.shape[0]
    side = group_ref[:, wide:].astype(F32)
    slot = lax.broadcasted_iota(jnp.int32, (count, slots), 1)
    column, inner = slot // (PAIR * capacity), slot % (PAIR * capacity)
    teacher = (column * HALVES * PAIR + half * PAIR + inner // capacity).astype(F32)
    position = (inner % capacity).astype(F32)
    hits = jnp.zeros((count, slots), F32)
    weight = jnp.zeros((count, slots), F32)
    for k in range(ranks):
        same = side[:, k : k + 1] == teacher
        hits = jnp.where(same, 1.0, hits)
        weight = jnp.where(same, side[:, ranks + k : ranks + k + 1], weight)
    later = lax.broadcasted_iota(jnp.int32, (count, count), 0)
    earlier = lax.broadcasted_iota(jnp.int32, (count, count), 1)
    below = jnp.where(earlier < later, 1.0, 0.0).astype(BF16)
    before = dot_nn(below, hits.astype(BF16))
    chosen = jnp.where((hits > 0.0) & (before == position), 1.0, 0.0)
    out_ref[:, :wide] = dot_tn(chosen.astype(BF16), group_ref[:, :wide]).astype(BF16)
    weights = dot_tn((chosen * weight).astype(BF16), jnp.ones((count, SIDE), BF16))
    out_ref[:, wide:] = weights.astype(BF16)


def by_teacher(count, capacity, source_axis):
    source = lax.broadcasted_iota(jnp.int32, (count, count), source_axis)
    target = lax.broadcasted_iota(jnp.int32, (count, count), 1 - source_axis)
    group, inner = source // (PAIR * capacity), source % (PAIR * capacity)
    goes = (inner // capacity) * (count // PAIR) + group * capacity + inner % capacity
    return jnp.where(goes == target, 1.0, 0.0).astype(BF16)


def silu_split(value):
    logistic = jax.nn.sigmoid(value)
    return value * logistic, logistic * (1.0 + value * (1.0 - logistic))


def hidden_kernel(
    capacity,
    rows_ref,
    t_gate_ref,
    t_up_ref,
    m_gate_ref,
    m_up_ref,
    t_come_ref,
    m_come_ref,
    out_ref,
    silu_ref,
    slope_ref,
    weight_ref,
):
    half, _ = place()
    block = m_gate_ref.shape[1]
    units = 2 * block
    count = rows_ref.shape[0]
    features = rows_ref.shape[1] - SIDE
    span = count // PAIR
    places = out_ref.shape[0] // PAIR
    rows = rows_ref[:, :features]

    def gate_up(*parts):
        value = dot_nt(jnp.concatenate(parts, axis=0), rows)
        return value[:units], value[units:]

    gate, up = gate_up(m_gate_ref[0], m_come_ref[0], m_up_ref[0], m_come_ref[1])
    silu, slope = silu_split(gate)
    silu_ref[...] = silu
    slope_ref[...] = up * slope
    hidden = [(silu * up).astype(BF16)]
    for m in range(PAIR):
        own = PAIR * half + m
        gate, up = gate_up(t_gate_ref[own], t_come_ref[m], t_up_ref[own], t_come_ref[PAIR + m])
        silu, _ = silu_split(gate)
        hidden.append((silu * up).astype(BF16))
    move = by_teacher(count, capacity, 0)
    hidden = dot_nn(jnp.concatenate(hidden, axis=0), move).astype(BF16)
    weight_ref[...] = dot_tn(move, rows_ref[:, features:]).astype(BF16)
    for m in range(PAIR):
        lanes = slice(m * span, (m + 1) * span)
        first = (1 + m) * units
        for i in range(places):
            at = m * places + i
            out_ref[at, 0] = hidden[:block, lanes]
            out_ref[at, 1] = hidden[block:units, lanes]
            out_ref[at, 2] = hidden[first : first + block, lanes]
            out_ref[at, 3] = hidden[first + block : first + units, lanes]


def share_kernel(down_ref, merged_ref, *out_refs):
    half, at = place()
    quarter = out_refs[0].shape[2]
    for k, out_ref in enumerate(out_refs):
        there = (at + k) % RING
        m = there // (RING // PAIR)
        span = pl.ds(pl.multiple_of(there % (RING // PAIR) * quarter, SIDE), quarter)
        out_ref[0] = down_ref[PAIR * half + m, :, span]
        out_ref[1] = down_ref[PAIR * (1 - half) + m, :, span]
        out_ref[2] = merged_ref[0, :, span]


def pass_kernel(*refs):
    out_ref = refs[-1]
    for k, down_ref in enumerate(refs[:-1]):
        out_ref[k] = down_ref[1:]


def gap_kernel(hidden_ref, weight_ref, came_ref, *refs):
    down_refs = refs[:RING]
    grad_ref, student_ref, slot_grad_ref = refs[RING:]
    block = hidden_ref.shape[2]
    units = 2 * block
    span = hidden_ref.shape[3]
    _, at = place()
    back = [(at + RING - k) % RING for k in range(RING)]
    student = jnp.concatenate([hidden_ref[i, a] for i in back for a in (0, 1)], axis=0)
    teacher = jnp.concatenate([hidden_ref[i, a] for i in back for a in (2, 3)], axis=0)
    t_down = jnp.concatenate([x for k in range(RING) for x in (down_refs[k][0], came_ref[k, 0])], axis=0)
    m_down = jnp.concatenate([x for k in range(RING) for x in (down_refs[k][2], came_ref[k, 1])], axis=0)
    gap = dot_tn(student, m_down) - dot_tn(teacher, t_down)
    start = pl.multiple_of(at // (RING // PAIR) * span, span)
    weight = weight_ref[pl.ds(start, span), SIDE - 1 : SIDE].astype(F32)
    slot_grad = (weight * gap).astype(BF16)
    grad = dot_nt(m_down, slot_grad).astype(BF16)
    for k, i in enumerate(back):
        grad_ref[i] = grad[k * units : (k + 1) * units]
    student_ref[...] = student
    slot_grad_ref[...] = slot_grad


def down_grad_kernel(student_ref, slot_grad_ref, kept_ref, other_ref):
    block = kept_ref.shape[1]
    units = 2 * block
    _, at = place()
    down_grad = dot_nn(student_ref[...], slot_grad_ref[...]).astype(BF16)
    for k in range(RING):
        i = (at + RING - k) % RING
        kept_ref[i] = down_grad[k * units : k * units + block]
        other_ref[i] = down_grad[k * units + block : (k + 1) * units]


def grads_kernel(capacity, parts_ref, silu_ref, slope_ref, rows_ref, own_ref, other_ref):
    block = own_ref.shape[1]
    places = parts_ref.shape[0] // PAIR
    units = parts_ref.shape[1]
    count = rows_ref.shape[0]
    parts = jnp.concatenate(
        [
            jnp.concatenate([parts_ref[m * places + i] for i in range(places)], axis=0)
            for m in range(PAIR)
        ],
        axis=1,
    )
    parts = dot_nn(parts, by_teacher(count, capacity, 1))
    total = parts[:units]
    for i in range(1, places):
        total += parts[i * units : (i + 1) * units]
    gate = (total * slope_ref[...]).astype(BF16)
    up = (total * silu_ref[...]).astype(BF16)
    stack = jnp.concatenate([gate[:block], up[:block], gate[block:], up[block:]], axis=0)
    grads = dot_nn(stack, rows_ref[:, : own_ref.shape[2]])
    own_ref[0] = grads[:block]
    own_ref[1] = grads[block : 2 * block]
    other_ref[0] = grads[2 * block : 3 * block].astype(BF16)
    other_ref[1] = grads[3 * block :].astype(BF16)


def down_sum_kernel(parts_ref, out_ref):
    count, _, piece = parts_ref.shape
    quarters = out_ref.shape[1] // piece
    for q in range(quarters):
        total = parts_ref[q].astype(F32)
        for i in range(q + quarters, count, quarters):
            total += parts_ref[i].astype(F32)
        out_ref[:, q * piece : (q + 1) * piece] = total


def body(
    tokens,
    teacher_ids,
    route_weight,
    teacher_gate,
    teacher_up,
    teacher_down,
    merged_gate,
    merged_up,
    merged_down,
):
    n_dp = HALVES * RING
    experts = lax.axis_size("expert")
    features = tokens.shape[2]
    capacity = tokens.shape[1]
    ranks = teacher_ids.shape[2]
    block = merged_gate.shape[1]
    wide = features + SIDE
    quarter = features * PAIR // RING
    rows = experts * PAIR * capacity
    span = rows // PAIR
    half = lax.axis_index("dp") // RING
    rings = [[a * RING + i for i in range(RING)] for a in range(HALVES)]
    swap = [(a * RING + i, (1 - a) * RING + i) for a in range(HALVES) for i in range(RING)]

    turns = [
        [(a * RING + i, a * RING + (i + k) % RING) for a in range(HALVES) for i in range(RING)]
        for k in range(RING)
    ]

    def exchange(array, axis_name, groups=None):
        return lax.all_to_all(
            array, axis_name, split_axis=0, concat_axis=0, tiled=True, axis_index_groups=groups
        )

    def halves(array, which):
        return lax.dynamic_slice_in_dim(array, PAIR * which, PAIR, axis=0)

    (packets,) = call(
        pack_kernel,
        (jax.ShapeDtypeStruct((n_dp, capacity, wide), BF16),),
        (teacher_ids[0].T, tokens[0], route_weight[0]),
    )
    group = exchange(packets, "dp").reshape(n_dp * capacity, wide)

    m_come = lax.ppermute(jnp.concatenate([merged_gate, merged_up], axis=0), "dp", swap)
    group, m_come = lax.optimization_barrier((group, m_come))
    (slots,) = call(
        lambda *refs: slots_kernel(ranks, capacity, *refs),
        (jax.ShapeDtypeStruct((rows, wide), BF16),),
        (group,),
        mib=60,
    )
    slots = exchange(slots.reshape(experts, PAIR * capacity, wide), "expert").reshape(rows, wide)

    down = call(
        share_kernel,
        tuple(jax.ShapeDtypeStruct((PAIR + 1, block, quarter), BF16) for _ in range(RING)),
        (teacher_down, merged_down),
    )
    down = [down[k] if k == 0 else lax.ppermute(down[k], "dp", turns[k]) for k in range(RING)]

    t_sent = jnp.concatenate([halves(teacher_gate, 1 - half), halves(teacher_up, 1 - half)], axis=0)
    t_sent, down[3], down[5] = lax.optimization_barrier((t_sent, down[3], down[5]))
    t_come = lax.ppermute(t_sent, "dp", swap)
    slots, t_come, down = lax.optimization_barrier((slots, t_come, down))

    (passed,) = call(
        pass_kernel, (jax.ShapeDtypeStruct((RING, PAIR, block, quarter), BF16),), tuple(down)
    )
    came = lax.ppermute(passed, "dp", swap)

    hidden, silu, slope, weight = call(
        lambda *refs: hidden_kernel(capacity, *refs),
        (
            jax.ShapeDtypeStruct((RING, 4, block, span), BF16),
            jax.ShapeDtypeStruct((2 * block, rows), F32),
            jax.ShapeDtypeStruct((2 * block, rows), F32),
            jax.ShapeDtypeStruct((rows, SIDE), BF16),
        ),
        (slots, teacher_gate, teacher_up, merged_gate, merged_up, t_come, m_come),
        mib=60,
    )
    hidden = exchange(hidden, "dp", rings)
    hidden_grad, student, slot_grad = call(
        gap_kernel,
        (
            jax.ShapeDtypeStruct((RING, 2 * block, span), BF16),
            jax.ShapeDtypeStruct((n_dp * block, span), BF16),
            jax.ShapeDtypeStruct((span, quarter), BF16),
        ),
        (hidden, weight, came, *down),
    )
    parts = exchange(hidden_grad, "dp", rings)
    kept_down, other_down = call(
        down_grad_kernel,
        (
            jax.ShapeDtypeStruct((RING, block, quarter), BF16),
            jax.ShapeDtypeStruct((RING, block, quarter), BF16),
        ),
        (student, slot_grad),
    )
    other_down = lax.ppermute(other_down, "dp", swap)
    down_grad = (kept_down.astype(F32) + other_down.astype(F32)).astype(BF16)
    own, other = call(
        lambda *refs: grads_kernel(capacity, *refs),
        (
            jax.ShapeDtypeStruct((2, block, features), F32),
            jax.ShapeDtypeStruct((2, block, features), BF16),
        ),
        (parts, silu, slope, slots),
        flops=0,
    )
    other, down_grad = lax.optimization_barrier((other, down_grad))
    down_grad = exchange(down_grad, "dp", rings)
    other = lax.ppermute(other, "dp", swap)
    (grad_down,) = call(
        down_sum_kernel, (jax.ShapeDtypeStruct((block, features), F32),), (down_grad,)
    )
    grad_gate = own[:1] + other[:1].astype(F32)
    grad_up = own[1:] + other[1:].astype(F32)
    return grad_gate, grad_up, grad_down[None]


def solution(mesh):
    placed = (P("expert", "dp", None),) * 9
    return jax.shard_map(
        body,
        mesh=mesh,
        in_specs=placed,
        out_specs=(P("expert", "dp", None),) * 3,
        check_vma=False,
    )
```

```python
import jax
import jax.numpy as jnp
from jax import lax
from jax.experimental import pallas as pl
from jax.experimental.pallas import tpu as pltpu
from jax.sharding import PartitionSpec as P

HALVES = 2
PAIR = 2
RING = 8
SIDE = 128
BF16 = jnp.bfloat16
F32 = jnp.float32


def dot_nn(a, b):
    return jnp.dot(a, b, preferred_element_type=F32)


def dot_nt(a, b):
    return lax.dot_general(a, b, (((1,), (1,)), ((), ())), preferred_element_type=F32)


def dot_tn(a, b):
    return lax.dot_general(a, b, (((0,), (0,)), ((), ())), preferred_element_type=F32)


def call(kernel, outs, args, mib=16):
    space = pl.BlockSpec(memory_space=pltpu.VMEM)
    return pl.pallas_call(
        kernel,
        out_shape=outs,
        in_specs=[space] * len(args),
        out_specs=[space] * len(outs),
        compiler_params=pltpu.CompilerParams(vmem_limit_bytes=mib * 1024 * 1024),
        cost_estimate=pl.CostEstimate(
            flops=0,
            bytes_accessed=sum(a.size * a.dtype.itemsize for a in args),
            transcendentals=0,
        ),
    )(*args)


def place():
    at = lax.axis_index("dp")
    return at // RING, at % RING


def pack_kernel(ids_ref, token_ref, weight_ref, out_ref):
    ranks, count = ids_ref.shape
    features = token_ref.shape[1]
    lane = lax.broadcasted_iota(jnp.int32, (ranks, SIDE), 1)
    rank = lax.broadcasted_iota(jnp.int32, (ranks, SIDE), 0)
    spread = jnp.where(lane == rank, 1.0, 0.0).astype(BF16)
    side = dot_tn(ids_ref[...].astype(F32).astype(BF16), spread)
    lane = lax.broadcasted_iota(jnp.int32, (count, SIDE), 1)
    weight = weight_ref[...].astype(F32)
    for k in range(ranks):
        side = jnp.where(lane == ranks + k, weight[:, k : k + 1], side)
    side = side.astype(BF16)
    tokens = token_ref[...]
    for i in range(out_ref.shape[0]):
        out_ref[i, :, :features] = tokens
        out_ref[i, :, features:] = side


def slots_kernel(ranks, capacity, group_ref, out_ref):
    half, _ = place()
    wide = group_ref.shape[1] - SIDE
    count = group_ref.shape[0]
    slots = out_ref.shape[0]
    side = group_ref[:, wide:].astype(F32)
    slot = lax.broadcasted_iota(jnp.int32, (count, slots), 1)
    column, inner = slot // (PAIR * capacity), slot % (PAIR * capacity)
    teacher = (column * HALVES * PAIR + half * PAIR + inner // capacity).astype(F32)
    position = (inner % capacity).astype(F32)
    hits = jnp.zeros((count, slots), F32)
    weight = jnp.zeros((count, slots), F32)
    for k in range(ranks):
        same = side[:, k : k + 1] == teacher
        hits = jnp.where(same, 1.0, hits)
        weight = jnp.where(same, side[:, ranks + k : ranks + k + 1], weight)
    later = lax.broadcasted_iota(jnp.int32, (count, count), 0)
    earlier = lax.broadcasted_iota(jnp.int32, (count, count), 1)
    below = jnp.where(earlier < later, 1.0, 0.0).astype(BF16)
    before = dot_nn(below, hits.astype(BF16))
    chosen = jnp.where((hits > 0.0) & (before == position), 1.0, 0.0)
    out_ref[:, :wide] = dot_tn(chosen.astype(BF16), group_ref[:, :wide]).astype(BF16)
    weights = dot_tn((chosen * weight).astype(BF16), jnp.ones((count, SIDE), BF16))
    out_ref[:, wide:] = weights.astype(BF16)


def by_teacher(count, capacity, source_axis):
    source = lax.broadcasted_iota(jnp.int32, (count, count), source_axis)
    target = lax.broadcasted_iota(jnp.int32, (count, count), 1 - source_axis)
    group, inner = source // (PAIR * capacity), source % (PAIR * capacity)
    goes = (inner // capacity) * (count // PAIR) + group * capacity + inner % capacity
    return jnp.where(goes == target, 1.0, 0.0).astype(BF16)


def silu_split(value):
    logistic = jax.nn.sigmoid(value)
    return value * logistic, logistic * (1.0 + value * (1.0 - logistic))


def hidden_kernel(
    capacity,
    rows_ref,
    t_gate_ref,
    t_up_ref,
    m_gate_ref,
    m_up_ref,
    come_ref,
    out_ref,
    silu_ref,
    slope_ref,
    weight_ref,
):
    half, _ = place()
    block = m_gate_ref.shape[1]
    units = 2 * block
    count = rows_ref.shape[0]
    features = rows_ref.shape[1] - SIDE
    span = count // PAIR
    places = out_ref.shape[0] // PAIR
    rows = rows_ref[:, :features]

    def gate_up(*parts):
        value = dot_nt(jnp.concatenate(parts, axis=0), rows)
        return value[:units], value[units:]

    gate, up = gate_up(m_gate_ref[0], come_ref[2 * PAIR], m_up_ref[0], come_ref[2 * PAIR + 1])
    silu, slope = silu_split(gate)
    silu_ref[...] = silu
    slope_ref[...] = up * slope
    hidden = [(silu * up).astype(BF16)]
    for m in range(PAIR):
        own = PAIR * half + m
        gate, up = gate_up(t_gate_ref[own], come_ref[m], t_up_ref[own], come_ref[PAIR + m])
        silu, _ = silu_split(gate)
        hidden.append((silu * up).astype(BF16))
    move = by_teacher(count, capacity, 0)
    hidden = dot_nn(jnp.concatenate(hidden, axis=0), move).astype(BF16)
    weight_ref[...] = dot_tn(move, rows_ref[:, features:]).astype(BF16)
    for m in range(PAIR):
        lanes = slice(m * span, (m + 1) * span)
        first = (1 + m) * units
        for i in range(places):
            at = m * places + i
            out_ref[at, 0] = hidden[:block, lanes]
            out_ref[at, 1] = hidden[block:units, lanes]
            out_ref[at, 2] = hidden[first : first + block, lanes]
            out_ref[at, 3] = hidden[first + block : first + units, lanes]


def share_kernel(down_ref, merged_ref, came_ref, merged_came_ref, *out_refs):
    half, at = place()
    block = merged_ref.shape[1]
    quarter = out_refs[0].shape[2]
    for k, out_ref in enumerate(out_refs):
        there = (at + k) % RING
        m = there // (RING // PAIR)
        span = pl.ds(pl.multiple_of(there % (RING // PAIR) * quarter, SIDE), quarter)
        out_ref[0, :block] = down_ref[PAIR * half + m, :, span]
        out_ref[0, block:] = came_ref[m, :, span]
        out_ref[1, :block] = merged_ref[0, :, span]
        out_ref[1, block:] = merged_came_ref[0, :, span]


def gap_kernel(hidden_ref, weight_ref, *refs):
    down_refs = refs[:RING]
    grad_ref, kept_ref, other_ref = refs[RING:]
    block = hidden_ref.shape[2]
    units = 2 * block
    span = hidden_ref.shape[3]
    _, at = place()
    back = [(at + RING - k) % RING for k in range(RING)]
    student = jnp.concatenate([hidden_ref[i, a] for i in back for a in (0, 1)], axis=0)
    teacher = jnp.concatenate([hidden_ref[i, a] for i in back for a in (2, 3)], axis=0)
    t_down = jnp.concatenate([down_ref[0] for down_ref in down_refs], axis=0)
    m_down = jnp.concatenate([down_ref[1] for down_ref in down_refs], axis=0)
    gap = dot_tn(student, m_down) - dot_tn(teacher, t_down)
    start = pl.multiple_of(at // (RING // PAIR) * span, span)
    weight = weight_ref[pl.ds(start, span), SIDE - 1 : SIDE].astype(F32)
    slot_grad = (weight * gap).astype(BF16)
    grad = dot_nt(m_down, slot_grad).astype(BF16)
    down_grad = dot_nn(student, slot_grad).astype(BF16)
    for k, i in enumerate(back):
        grad_ref[i] = grad[k * units : (k + 1) * units]
        kept_ref[i] = down_grad[k * units : k * units + block]
        other_ref[i] = down_grad[k * units + block : (k + 1) * units]


def grads_kernel(capacity, parts_ref, silu_ref, slope_ref, rows_ref, own_ref, other_ref):
    block = own_ref.shape[1]
    places = parts_ref.shape[0] // PAIR
    units = parts_ref.shape[1]
    count = rows_ref.shape[0]
    parts = jnp.concatenate(
        [
            jnp.concatenate([parts_ref[m * places + i] for i in range(places)], axis=0)
            for m in range(PAIR)
        ],
        axis=1,
    )
    parts = dot_nn(parts, by_teacher(count, capacity, 1))
    total = parts[:units]
    for i in range(1, places):
        total += parts[i * units : (i + 1) * units]
    gate = (total * slope_ref[...]).astype(BF16)
    up = (total * silu_ref[...]).astype(BF16)
    stack = jnp.concatenate([gate[:block], up[:block], gate[block:], up[block:]], axis=0)
    grads = dot_nn(stack, rows_ref[:, : own_ref.shape[2]])
    own_ref[0] = grads[:block]
    own_ref[1] = grads[block : 2 * block]
    other_ref[0] = grads[2 * block : 3 * block].astype(BF16)
    other_ref[1] = grads[3 * block :].astype(BF16)


def down_sum_kernel(parts_ref, out_ref):
    count, _, piece = parts_ref.shape
    quarters = out_ref.shape[1] // piece
    for q in range(quarters):
        total = parts_ref[q].astype(F32)
        for i in range(q + quarters, count, quarters):
            total += parts_ref[i].astype(F32)
        out_ref[:, q * piece : (q + 1) * piece] = total


def body(
    tokens,
    teacher_ids,
    route_weight,
    teacher_gate,
    teacher_up,
    teacher_down,
    merged_gate,
    merged_up,
    merged_down,
):
    n_dp = HALVES * RING
    experts = lax.axis_size("expert")
    features = tokens.shape[2]
    capacity = tokens.shape[1]
    ranks = teacher_ids.shape[2]
    block = merged_gate.shape[1]
    wide = features + SIDE
    quarter = features * PAIR // RING
    rows = experts * PAIR * capacity
    span = rows // PAIR
    half = lax.axis_index("dp") // RING
    rings = [[a * RING + i for i in range(RING)] for a in range(HALVES)]
    swap = [(a * RING + i, (1 - a) * RING + i) for a in range(HALVES) for i in range(RING)]

    turns = [
        [(a * RING + i, a * RING + (i + k) % RING) for a in range(HALVES) for i in range(RING)]
        for k in range(RING)
    ]

    def exchange(array, axis_name, groups=None):
        return lax.all_to_all(
            array, axis_name, split_axis=0, concat_axis=0, tiled=True, axis_index_groups=groups
        )

    def halves(array, which):
        return lax.dynamic_slice_in_dim(array, PAIR * which, PAIR, axis=0)

    (packets,) = call(
        pack_kernel,
        (jax.ShapeDtypeStruct((n_dp, capacity, wide), BF16),),
        (teacher_ids[0].T, tokens[0], route_weight[0]),
    )
    group = exchange(packets, "dp").reshape(n_dp * capacity, wide)

    came = lax.ppermute(halves(teacher_down, 1 - half), "dp", swap)
    group, came = lax.optimization_barrier((group, came))
    (slots,) = call(
        lambda *refs: slots_kernel(ranks, capacity, *refs),
        (jax.ShapeDtypeStruct((rows, wide), BF16),),
        (group,),
        mib=60,
    )
    slots = exchange(slots.reshape(experts, PAIR * capacity, wide), "expert").reshape(rows, wide)

    merged_came = lax.ppermute(merged_down, "dp", swap)
    down = call(
        share_kernel,
        tuple(jax.ShapeDtypeStruct((2, 2 * block, quarter), BF16) for _ in range(RING)),
        (teacher_down, merged_down, came, merged_came),
    )
    down = [down[k] if k == 0 else lax.ppermute(down[k], "dp", turns[k]) for k in range(RING)]

    parts = [halves(teacher_gate, 1 - half), halves(teacher_up, 1 - half), merged_gate, merged_up]
    come = jnp.concatenate(parts, axis=0)
    come, down[1] = lax.optimization_barrier((come, down[1]))
    come = lax.ppermute(come, "dp", swap)
    slots, come, down = lax.optimization_barrier((slots, come, down))

    hidden, silu, slope, weight = call(
        lambda *refs: hidden_kernel(capacity, *refs),
        (
            jax.ShapeDtypeStruct((RING, 4, block, span), BF16),
            jax.ShapeDtypeStruct((2 * block, rows), F32),
            jax.ShapeDtypeStruct((2 * block, rows), F32),
            jax.ShapeDtypeStruct((rows, SIDE), BF16),
        ),
        (slots, teacher_gate, teacher_up, merged_gate, merged_up, come),
        mib=60,
    )
    hidden = exchange(hidden, "dp", rings)
    hidden_grad, kept_down, other_down = call(
        gap_kernel,
        (
            jax.ShapeDtypeStruct((RING, 2 * block, span), BF16),
            jax.ShapeDtypeStruct((RING, block, quarter), BF16),
            jax.ShapeDtypeStruct((RING, block, quarter), BF16),
        ),
        (hidden, weight, *down),
    )
    parts = exchange(hidden_grad, "dp", rings)
    other_down = lax.ppermute(other_down, "dp", swap)
    down_grad = (kept_down.astype(F32) + other_down.astype(F32)).astype(BF16)
    own, other = call(
        lambda *refs: grads_kernel(capacity, *refs),
        (
            jax.ShapeDtypeStruct((2, block, features), F32),
            jax.ShapeDtypeStruct((2, block, features), BF16),
        ),
        (parts, silu, slope, slots),
    )
    other, down_grad = lax.optimization_barrier((other, down_grad))
    down_grad = exchange(down_grad, "dp", rings)
    other = lax.ppermute(other, "dp", swap)
    (grad_down,) = call(
        down_sum_kernel, (jax.ShapeDtypeStruct((block, features), F32),), (down_grad,)
    )
    grad_gate = own[:1] + other[:1].astype(F32)
    grad_up = own[1:] + other[1:].astype(F32)
    return grad_gate, grad_up, grad_down[None]


def solution(mesh):
    placed = (P("expert", "dp", None),) * 9
    return jax.shard_map(
        body,
        mesh=mesh,
        in_specs=placed,
        out_specs=(P("expert", "dp", None),) * 3,
        check_vma=False,
    )
```

```python
import jax
import jax.numpy as jnp
from jax import lax
from jax.experimental import pallas as pl
from jax.experimental.pallas import tpu as pltpu
from jax.sharding import PartitionSpec as P

HALVES = 2
PAIR = 2
EARLY = (1, 7, 2)
RING = 8
SIDE = 128
BF16 = jnp.bfloat16
F32 = jnp.float32


def dot_nn(a, b):
    return jnp.dot(a, b, preferred_element_type=F32)


def dot_nt(a, b):
    return lax.dot_general(a, b, (((1,), (1,)), ((), ())), preferred_element_type=F32)


def dot_tn(a, b):
    return lax.dot_general(a, b, (((0,), (0,)), ((), ())), preferred_element_type=F32)


def call(kernel, outs, args, far=(), scratch=(), mib=16):
    def space(i, alone):
        return pl.BlockSpec(memory_space=pltpu.HBM if i in alone else pltpu.VMEM)

    return pl.pallas_call(
        kernel,
        out_shape=outs,
        in_specs=[space(i, far) for i in range(len(args))],
        out_specs=[space(i, ()) for i in range(len(outs))],
        scratch_shapes=scratch,
        compiler_params=pltpu.CompilerParams(vmem_limit_bytes=mib * 1024 * 1024),
        cost_estimate=pl.CostEstimate(
            flops=0,
            bytes_accessed=sum(a.size * a.dtype.itemsize for a in args),
            transcendentals=0,
        ),
    )(*args)


def start_copies(pairs, sems, first=0):
    copies = [
        pltpu.make_async_copy(source, target, sems.at[first + i])
        for i, (source, target) in enumerate(pairs)
    ]
    for copy in copies:
        copy.start()
    return copies


def wait_copies(copies):
    for copy in copies:
        copy.wait()


def place():
    at = lax.axis_index("dp")
    return at // RING, at % RING


def pack_kernel(ids_ref, token_ref, weight_ref, out_ref):
    ranks, count = ids_ref.shape
    features = token_ref.shape[1]
    lane = lax.broadcasted_iota(jnp.int32, (ranks, SIDE), 1)
    rank = lax.broadcasted_iota(jnp.int32, (ranks, SIDE), 0)
    spread = jnp.where(lane == rank, 1.0, 0.0).astype(BF16)
    side = dot_tn(ids_ref[...].astype(F32).astype(BF16), spread)
    lane = lax.broadcasted_iota(jnp.int32, (count, SIDE), 1)
    weight = weight_ref[...].astype(F32)
    for k in range(ranks):
        side = jnp.where(lane == ranks + k, weight[:, k : k + 1], side)
    side = side.astype(BF16)
    tokens = token_ref[...]
    for i in range(out_ref.shape[0]):
        out_ref[i, :, :features] = tokens
        out_ref[i, :, features:] = side


def slots_kernel(ranks, capacity, group_ref, out_ref):
    half, _ = place()
    wide = group_ref.shape[1] - SIDE
    count = group_ref.shape[0]
    slots = out_ref.shape[0]
    side = group_ref[:, wide:].astype(F32)
    slot = lax.broadcasted_iota(jnp.int32, (count, slots), 1)
    column, inner = slot // (PAIR * capacity), slot % (PAIR * capacity)
    teacher = (column * HALVES * PAIR + half * PAIR + inner // capacity).astype(F32)
    position = (inner % capacity).astype(F32)
    hits = jnp.zeros((count, slots), F32)
    weight = jnp.zeros((count, slots), F32)
    for k in range(ranks):
        same = side[:, k : k + 1] == teacher
        hits = jnp.where(same, 1.0, hits)
        weight = jnp.where(same, side[:, ranks + k : ranks + k + 1], weight)
    later = lax.broadcasted_iota(jnp.int32, (count, count), 0)
    earlier = lax.broadcasted_iota(jnp.int32, (count, count), 1)
    below = jnp.where(earlier < later, 1.0, 0.0).astype(BF16)
    before = dot_nn(below, hits.astype(BF16))
    chosen = jnp.where((hits > 0.0) & (before == position), 1.0, 0.0)
    out_ref[:, :wide] = dot_tn(chosen.astype(BF16), group_ref[:, :wide]).astype(BF16)
    weights = dot_tn((chosen * weight).astype(BF16), jnp.ones((count, SIDE), BF16))
    out_ref[:, wide:] = weights.astype(BF16)


def by_teacher(count, capacity, source_axis):
    source = lax.broadcasted_iota(jnp.int32, (count, count), source_axis)
    target = lax.broadcasted_iota(jnp.int32, (count, count), 1 - source_axis)
    group, inner = source // (PAIR * capacity), source % (PAIR * capacity)
    goes = (inner // capacity) * (count // PAIR) + group * capacity + inner % capacity
    return jnp.where(goes == target, 1.0, 0.0).astype(BF16)


def silu_split(value):
    logistic = jax.nn.sigmoid(value)
    return value * logistic, logistic * (1.0 + value * (1.0 - logistic))


def hidden_kernel(
    capacity,
    rows_hbm,
    t_gate_hbm,
    t_up_hbm,
    m_gate_hbm,
    m_up_hbm,
    come_hbm,
    out_ref,
    silu_ref,
    slope_ref,
    weight_ref,
    row_buf,
    weight_buf,
    sems,
):
    half, _ = place()
    block = m_gate_hbm.shape[1]
    units = 2 * block
    count, wide = row_buf.shape
    features = wide - SIDE
    span = count // PAIR
    places = out_ref.shape[0] // PAIR

    def weights(at, *parts):
        pairs = [(part, weight_buf.at[at, pl.ds(i * block, block)]) for i, part in enumerate(parts)]
        return start_copies(pairs, sems, 4 * at)

    def gate_up(at):
        value = dot_nt(weight_buf[at], row_buf[:, :features])
        return value[:units], value[units:]

    first = start_copies([(rows_hbm, row_buf)], sems, 4 * PAIR + 4)
    first += weights(
        PAIR, m_gate_hbm.at[0], come_hbm.at[2 * PAIR], m_up_hbm.at[0], come_hbm.at[2 * PAIR + 1]
    )
    later = []
    for m in range(PAIR):
        own = PAIR * half + m
        later.append(
            weights(m, t_gate_hbm.at[own], come_hbm.at[m], t_up_hbm.at[own], come_hbm.at[PAIR + m])
        )
    move = by_teacher(count, capacity, 0)
    wait_copies(first)
    gate, up = gate_up(PAIR)
    silu, slope = silu_split(gate)
    silu_ref[...] = silu
    slope_ref[...] = up * slope
    hidden = [(silu * up).astype(BF16)]
    for m in range(PAIR):
        wait_copies(later[m])
        gate, up = gate_up(m)
        silu, _ = silu_split(gate)
        hidden.append((silu * up).astype(BF16))
    hidden = dot_nn(jnp.concatenate(hidden, axis=0), move).astype(BF16)
    weight_ref[...] = dot_tn(move, row_buf[:, features:]).astype(BF16)
    for m in range(PAIR):
        lanes = slice(m * span, (m + 1) * span)
        first = (1 + m) * units
        for i in range(places):
            at = m * places + i
            out_ref[at, 0] = hidden[:block, lanes]
            out_ref[at, 1] = hidden[block:units, lanes]
            out_ref[at, 2] = hidden[first : first + block, lanes]
            out_ref[at, 3] = hidden[first + block : first + units, lanes]


def share_kernel(down_ref, merged_ref, *out_refs):
    half, at = place()
    quarter = out_refs[0].shape[2]
    for k, out_ref in enumerate(out_refs):
        there = (at + k) % RING
        m = there // (RING // PAIR)
        span = pl.ds(pl.multiple_of(there % (RING // PAIR) * quarter, SIDE), quarter)
        out_ref[0] = down_ref[PAIR * half + m, :, span]
        out_ref[1] = down_ref[PAIR * (1 - half) + m, :, span]
        out_ref[2] = merged_ref[0, :, span]


def pass_kernel(*refs):
    out_ref = refs[-1]
    for k, down_ref in enumerate(refs[:-1]):
        out_ref[k] = down_ref[1:]


def gap_kernel(hidden_ref, weight_ref, came_ref, *refs):
    down_refs = refs[:RING]
    grad_ref, kept_ref, other_ref = refs[RING:]
    block = hidden_ref.shape[2]
    units = 2 * block
    span = hidden_ref.shape[3]
    _, at = place()
    back = [(at + RING - k) % RING for k in range(RING)]
    student = jnp.concatenate([hidden_ref[i, a] for i in back for a in (0, 1)], axis=0)
    teacher = jnp.concatenate([hidden_ref[i, a] for i in back for a in (2, 3)], axis=0)
    t_down = jnp.concatenate([x for k in range(RING) for x in (down_refs[k][0], came_ref[k, 0])], axis=0)
    m_down = jnp.concatenate([x for k in range(RING) for x in (down_refs[k][2], came_ref[k, 1])], axis=0)
    gap = dot_tn(student, m_down) - dot_tn(teacher, t_down)
    start = pl.multiple_of(at // (RING // PAIR) * span, span)
    weight = weight_ref[pl.ds(start, span), SIDE - 1 : SIDE].astype(F32)
    slot_grad = (weight * gap).astype(BF16)
    grad = dot_nt(m_down, slot_grad).astype(BF16)
    down_grad = dot_nn(student, slot_grad).astype(BF16)
    for k, i in enumerate(back):
        grad_ref[i] = grad[k * units : (k + 1) * units]
        kept_ref[i] = down_grad[k * units : k * units + block]
        other_ref[i] = down_grad[k * units + block : (k + 1) * units]


def grads_kernel(capacity, parts_ref, silu_ref, slope_ref, rows_ref, own_ref, other_ref):
    block = own_ref.shape[1]
    places = parts_ref.shape[0] // PAIR
    units = parts_ref.shape[1]
    count = rows_ref.shape[0]
    parts = jnp.concatenate(
        [
            jnp.concatenate([parts_ref[m * places + i] for i in range(places)], axis=0)
            for m in range(PAIR)
        ],
        axis=1,
    )
    parts = dot_nn(parts, by_teacher(count, capacity, 1))
    total = parts[:units]
    for i in range(1, places):
        total += parts[i * units : (i + 1) * units]
    gate = (total * slope_ref[...]).astype(BF16)
    up = (total * silu_ref[...]).astype(BF16)
    stack = jnp.concatenate([gate[:block], up[:block], gate[block:], up[block:]], axis=0)
    grads = dot_nn(stack, rows_ref[:, : own_ref.shape[2]])
    own_ref[0] = grads[:block]
    own_ref[1] = grads[block : 2 * block]
    other_ref[0] = grads[2 * block : 3 * block].astype(BF16)
    other_ref[1] = grads[3 * block :].astype(BF16)


def down_sum_kernel(parts_ref, out_ref):
    count, _, piece = parts_ref.shape
    quarters = out_ref.shape[1] // piece
    for q in range(quarters):
        total = parts_ref[q].astype(F32)
        for i in range(q + quarters, count, quarters):
            total += parts_ref[i].astype(F32)
        out_ref[:, q * piece : (q + 1) * piece] = total


def body(
    tokens,
    teacher_ids,
    route_weight,
    teacher_gate,
    teacher_up,
    teacher_down,
    merged_gate,
    merged_up,
    merged_down,
):
    n_dp = HALVES * RING
    experts = lax.axis_size("expert")
    features = tokens.shape[2]
    capacity = tokens.shape[1]
    ranks = teacher_ids.shape[2]
    block = merged_gate.shape[1]
    wide = features + SIDE
    quarter = features * PAIR // RING
    rows = experts * PAIR * capacity
    span = rows // PAIR
    half = lax.axis_index("dp") // RING
    rings = [[a * RING + i for i in range(RING)] for a in range(HALVES)]
    swap = [(a * RING + i, (1 - a) * RING + i) for a in range(HALVES) for i in range(RING)]

    turns = [
        [(a * RING + i, a * RING + (i + k) % RING) for a in range(HALVES) for i in range(RING)]
        for k in range(RING)
    ]

    def exchange(array, axis_name, groups=None):
        return lax.all_to_all(
            array, axis_name, split_axis=0, concat_axis=0, tiled=True, axis_index_groups=groups
        )

    def halves(array, which):
        return lax.dynamic_slice_in_dim(array, PAIR * which, PAIR, axis=0)

    (packets,) = call(
        pack_kernel,
        (jax.ShapeDtypeStruct((n_dp, capacity, wide), BF16),),
        (teacher_ids[0].T, tokens[0], route_weight[0]),
    )
    group = exchange(packets, "dp").reshape(n_dp * capacity, wide)

    down = call(
        share_kernel,
        tuple(jax.ShapeDtypeStruct((PAIR + 1, block, quarter), BF16) for _ in range(RING)),
        (teacher_down, merged_down),
    )
    down = [down[k] if k == 0 else lax.ppermute(down[k], "dp", turns[k]) for k in range(RING)]
    early = [down[k] for k in EARLY]
    group, early = lax.optimization_barrier((group, early))
    for k, array in zip(EARLY, early):
        down[k] = array

    (slots,) = call(
        lambda *refs: slots_kernel(ranks, capacity, *refs),
        (jax.ShapeDtypeStruct((rows, wide), BF16),),
        (group,),
        mib=60,
    )
    slots = exchange(slots.reshape(experts, PAIR * capacity, wide), "expert").reshape(rows, wide)

    sent = [halves(teacher_gate, 1 - half), halves(teacher_up, 1 - half), merged_gate, merged_up]
    come = lax.ppermute(jnp.concatenate(sent, axis=0), "dp", swap)
    slots, come, down = lax.optimization_barrier((slots, come, down))

    (passed,) = call(
        pass_kernel, (jax.ShapeDtypeStruct((RING, PAIR, block, quarter), BF16),), tuple(down), mib=60
    )
    came = lax.ppermute(passed, "dp", swap)

    hidden, silu, slope, weight = call(
        lambda *refs: hidden_kernel(capacity, *refs),
        (
            jax.ShapeDtypeStruct((RING, 4, block, span), BF16),
            jax.ShapeDtypeStruct((2 * block, rows), F32),
            jax.ShapeDtypeStruct((2 * block, rows), F32),
            jax.ShapeDtypeStruct((rows, SIDE), BF16),
        ),
        (slots, teacher_gate, teacher_up, merged_gate, merged_up, come),
        far=range(6),
        scratch=[
            pltpu.VMEM((rows, wide), BF16),
            pltpu.VMEM((PAIR + 1, 4 * block, features), BF16),
            pltpu.SemaphoreType.DMA((4 * PAIR + 5,)),
        ],
        mib=60,
    )
    hidden = exchange(hidden, "dp", rings)
    hidden_grad, kept_down, other_down = call(
        gap_kernel,
        (
            jax.ShapeDtypeStruct((RING, 2 * block, span), BF16),
            jax.ShapeDtypeStruct((RING, block, quarter), BF16),
            jax.ShapeDtypeStruct((RING, block, quarter), BF16),
        ),
        (hidden, weight, came, *down),
        mib=60,
    )
    parts = exchange(hidden_grad, "dp", rings)
    other_down = lax.ppermute(other_down, "dp", swap)
    down_grad = (kept_down.astype(F32) + other_down.astype(F32)).astype(BF16)
    own, other = call(
        lambda *refs: grads_kernel(capacity, *refs),
        (
            jax.ShapeDtypeStruct((2, block, features), F32),
            jax.ShapeDtypeStruct((2, block, features), BF16),
        ),
        (parts, silu, slope, slots),
    )
    other, down_grad = lax.optimization_barrier((other, down_grad))
    down_grad = exchange(down_grad, "dp", rings)
    other = lax.ppermute(other, "dp", swap)
    (grad_down,) = call(
        down_sum_kernel, (jax.ShapeDtypeStruct((block, features), F32),), (down_grad,)
    )
    grad_gate = own[:1] + other[:1].astype(F32)
    grad_up = own[1:] + other[1:].astype(F32)
    return grad_gate, grad_up, grad_down[None]


def solution(mesh):
    placed = (P("expert", "dp", None),) * 9
    return jax.shard_map(
        body,
        mesh=mesh,
        in_specs=placed,
        out_specs=(P("expert", "dp", None),) * 3,
        check_vma=False,
    )
```

```python
import jax
import jax.numpy as jnp
from jax import lax
from jax.experimental import pallas as pl
from jax.experimental.pallas import tpu as pltpu
from jax.sharding import PartitionSpec as P

HALVES = 2
PAIR = 2
EARLY = (1,)
RING = 8
SIDE = 128
BF16 = jnp.bfloat16
F32 = jnp.float32


def dot_nn(a, b):
    return jnp.dot(a, b, preferred_element_type=F32)


def dot_nt(a, b):
    return lax.dot_general(a, b, (((1,), (1,)), ((), ())), preferred_element_type=F32)


def dot_tn(a, b):
    return lax.dot_general(a, b, (((0,), (0,)), ((), ())), preferred_element_type=F32)


def call(kernel, outs, args, far=(), scratch=(), mib=16):
    def space(i, alone):
        return pl.BlockSpec(memory_space=pltpu.HBM if i in alone else pltpu.VMEM)

    return pl.pallas_call(
        kernel,
        out_shape=outs,
        in_specs=[space(i, far) for i in range(len(args))],
        out_specs=[space(i, ()) for i in range(len(outs))],
        scratch_shapes=scratch,
        compiler_params=pltpu.CompilerParams(vmem_limit_bytes=mib * 1024 * 1024),
        cost_estimate=pl.CostEstimate(
            flops=0,
            bytes_accessed=sum(a.size * a.dtype.itemsize for a in args),
            transcendentals=0,
        ),
    )(*args)


def start_copies(pairs, sems, first=0):
    copies = [
        pltpu.make_async_copy(source, target, sems.at[first + i])
        for i, (source, target) in enumerate(pairs)
    ]
    for copy in copies:
        copy.start()
    return copies


def wait_copies(copies):
    for copy in copies:
        copy.wait()


def place():
    at = lax.axis_index("dp")
    return at // RING, at % RING


def pack_kernel(ids_ref, token_ref, weight_ref, out_ref):
    ranks, count = ids_ref.shape
    features = token_ref.shape[1]
    lane = lax.broadcasted_iota(jnp.int32, (ranks, SIDE), 1)
    rank = lax.broadcasted_iota(jnp.int32, (ranks, SIDE), 0)
    spread = jnp.where(lane == rank, 1.0, 0.0).astype(BF16)
    side = dot_tn(ids_ref[...].astype(F32).astype(BF16), spread)
    lane = lax.broadcasted_iota(jnp.int32, (count, SIDE), 1)
    weight = weight_ref[...].astype(F32)
    for k in range(ranks):
        side = jnp.where(lane == ranks + k, weight[:, k : k + 1], side)
    side = side.astype(BF16)
    tokens = token_ref[...]
    for i in range(out_ref.shape[0]):
        out_ref[i, :, :features] = tokens
        out_ref[i, :, features:] = side


def slots_kernel(ranks, capacity, group_ref, out_ref):
    half, _ = place()
    wide = group_ref.shape[1] - SIDE
    count = group_ref.shape[0]
    slots = out_ref.shape[0]
    side = group_ref[:, wide:].astype(F32)
    slot = lax.broadcasted_iota(jnp.int32, (count, slots), 1)
    column, inner = slot // (PAIR * capacity), slot % (PAIR * capacity)
    teacher = (column * HALVES * PAIR + half * PAIR + inner // capacity).astype(F32)
    position = (inner % capacity).astype(F32)
    hits = jnp.zeros((count, slots), F32)
    weight = jnp.zeros((count, slots), F32)
    for k in range(ranks):
        same = side[:, k : k + 1] == teacher
        hits = jnp.where(same, 1.0, hits)
        weight = jnp.where(same, side[:, ranks + k : ranks + k + 1], weight)
    later = lax.broadcasted_iota(jnp.int32, (count, count), 0)
    earlier = lax.broadcasted_iota(jnp.int32, (count, count), 1)
    below = jnp.where(earlier < later, 1.0, 0.0).astype(BF16)
    before = dot_nn(below, hits.astype(BF16))
    chosen = jnp.where((hits > 0.0) & (before == position), 1.0, 0.0)
    out_ref[:, :wide] = dot_tn(chosen.astype(BF16), group_ref[:, :wide]).astype(BF16)
    weights = dot_tn((chosen * weight).astype(BF16), jnp.ones((count, SIDE), BF16))
    out_ref[:, wide:] = weights.astype(BF16)


def by_teacher(count, capacity, source_axis):
    source = lax.broadcasted_iota(jnp.int32, (count, count), source_axis)
    target = lax.broadcasted_iota(jnp.int32, (count, count), 1 - source_axis)
    group, inner = source // (PAIR * capacity), source % (PAIR * capacity)
    goes = (inner // capacity) * (count // PAIR) + group * capacity + inner % capacity
    return jnp.where(goes == target, 1.0, 0.0).astype(BF16)


def silu_split(value):
    logistic = jax.nn.sigmoid(value)
    return value * logistic, logistic * (1.0 + value * (1.0 - logistic))


def hidden_kernel(
    capacity,
    rows_hbm,
    t_gate_hbm,
    t_up_hbm,
    m_gate_hbm,
    m_up_hbm,
    t_come_hbm,
    m_come_hbm,
    out_ref,
    silu_ref,
    slope_ref,
    weight_ref,
    row_buf,
    weight_buf,
    sems,
):
    half, _ = place()
    block = m_gate_hbm.shape[1]
    units = 2 * block
    count, wide = row_buf.shape
    features = wide - SIDE
    span = count // PAIR
    places = out_ref.shape[0] // PAIR

    def weights(at, *parts):
        pairs = [(part, weight_buf.at[at, pl.ds(i * block, block)]) for i, part in enumerate(parts)]
        return start_copies(pairs, sems, 4 * at)

    def gate_up(at):
        value = dot_nt(weight_buf[at], row_buf[:, :features])
        return value[:units], value[units:]

    first = start_copies([(rows_hbm, row_buf)], sems, 4 * PAIR + 4)
    first += weights(
        PAIR, m_gate_hbm.at[0], m_come_hbm.at[0], m_up_hbm.at[0], m_come_hbm.at[1]
    )
    later = []
    for m in range(PAIR):
        own = PAIR * half + m
        later.append(
            weights(m, t_gate_hbm.at[own], t_come_hbm.at[m], t_up_hbm.at[own], t_come_hbm.at[PAIR + m])
        )
    move = by_teacher(count, capacity, 0)
    wait_copies(first)
    gate, up = gate_up(PAIR)
    silu, slope = silu_split(gate)
    silu_ref[...] = silu
    slope_ref[...] = up * slope
    hidden = [(silu * up).astype(BF16)]
    for m in range(PAIR):
        wait_copies(later[m])
        gate, up = gate_up(m)
        silu, _ = silu_split(gate)
        hidden.append((silu * up).astype(BF16))
    hidden = dot_nn(jnp.concatenate(hidden, axis=0), move).astype(BF16)
    weight_ref[...] = dot_tn(move, row_buf[:, features:]).astype(BF16)
    for m in range(PAIR):
        lanes = slice(m * span, (m + 1) * span)
        first = (1 + m) * units
        for i in range(places):
            at = m * places + i
            out_ref[at, 0] = hidden[:block, lanes]
            out_ref[at, 1] = hidden[block:units, lanes]
            out_ref[at, 2] = hidden[first : first + block, lanes]
            out_ref[at, 3] = hidden[first + block : first + units, lanes]


def share_kernel(down_ref, merged_ref, *out_refs):
    half, at = place()
    quarter = out_refs[0].shape[2]
    for k, out_ref in enumerate(out_refs):
        there = (at + k) % RING
        m = there // (RING // PAIR)
        span = pl.ds(pl.multiple_of(there % (RING // PAIR) * quarter, SIDE), quarter)
        out_ref[0] = down_ref[PAIR * half + m, :, span]
        out_ref[1] = down_ref[PAIR * (1 - half) + m, :, span]
        out_ref[2] = merged_ref[0, :, span]


def pass_kernel(*refs):
    out_ref = refs[-1]
    for k, down_ref in enumerate(refs[:-1]):
        out_ref[k] = down_ref[1:]


def gap_kernel(hidden_ref, weight_ref, came_ref, *refs):
    down_refs = refs[:RING]
    grad_ref, kept_ref, other_ref = refs[RING:]
    block = hidden_ref.shape[2]
    units = 2 * block
    span = hidden_ref.shape[3]
    _, at = place()
    back = [(at + RING - k) % RING for k in range(RING)]
    student = jnp.concatenate([hidden_ref[i, a] for i in back for a in (0, 1)], axis=0)
    teacher = jnp.concatenate([hidden_ref[i, a] for i in back for a in (2, 3)], axis=0)
    t_down = jnp.concatenate([x for k in range(RING) for x in (down_refs[k][0], came_ref[k, 0])], axis=0)
    m_down = jnp.concatenate([x for k in range(RING) for x in (down_refs[k][2], came_ref[k, 1])], axis=0)
    gap = dot_tn(student, m_down) - dot_tn(teacher, t_down)
    start = pl.multiple_of(at // (RING // PAIR) * span, span)
    weight = weight_ref[pl.ds(start, span), SIDE - 1 : SIDE].astype(F32)
    slot_grad = (weight * gap).astype(BF16)
    grad = dot_nt(m_down, slot_grad).astype(BF16)
    down_grad = dot_nn(student, slot_grad).astype(BF16)
    for k, i in enumerate(back):
        grad_ref[i] = grad[k * units : (k + 1) * units]
        kept_ref[i] = down_grad[k * units : k * units + block]
        other_ref[i] = down_grad[k * units + block : (k + 1) * units]


def grads_kernel(capacity, parts_ref, silu_ref, slope_ref, rows_ref, own_ref, other_ref):
    block = own_ref.shape[1]
    places = parts_ref.shape[0] // PAIR
    units = parts_ref.shape[1]
    count = rows_ref.shape[0]
    parts = jnp.concatenate(
        [
            jnp.concatenate([parts_ref[m * places + i] for i in range(places)], axis=0)
            for m in range(PAIR)
        ],
        axis=1,
    )
    parts = dot_nn(parts, by_teacher(count, capacity, 1))
    total = parts[:units]
    for i in range(1, places):
        total += parts[i * units : (i + 1) * units]
    gate = (total * slope_ref[...]).astype(BF16)
    up = (total * silu_ref[...]).astype(BF16)
    stack = jnp.concatenate([gate[:block], up[:block], gate[block:], up[block:]], axis=0)
    grads = dot_nn(stack, rows_ref[:, : own_ref.shape[2]])
    own_ref[0] = grads[:block]
    own_ref[1] = grads[block : 2 * block]
    other_ref[0] = grads[2 * block : 3 * block].astype(BF16)
    other_ref[1] = grads[3 * block :].astype(BF16)


def down_sum_kernel(parts_ref, out_ref):
    count, _, piece = parts_ref.shape
    quarters = out_ref.shape[1] // piece
    for q in range(quarters):
        total = parts_ref[q].astype(F32)
        for i in range(q + quarters, count, quarters):
            total += parts_ref[i].astype(F32)
        out_ref[:, q * piece : (q + 1) * piece] = total


def body(
    tokens,
    teacher_ids,
    route_weight,
    teacher_gate,
    teacher_up,
    teacher_down,
    merged_gate,
    merged_up,
    merged_down,
):
    n_dp = HALVES * RING
    experts = lax.axis_size("expert")
    features = tokens.shape[2]
    capacity = tokens.shape[1]
    ranks = teacher_ids.shape[2]
    block = merged_gate.shape[1]
    wide = features + SIDE
    quarter = features * PAIR // RING
    rows = experts * PAIR * capacity
    span = rows // PAIR
    half = lax.axis_index("dp") // RING
    rings = [[a * RING + i for i in range(RING)] for a in range(HALVES)]
    swap = [(a * RING + i, (1 - a) * RING + i) for a in range(HALVES) for i in range(RING)]

    turns = [
        [(a * RING + i, a * RING + (i + k) % RING) for a in range(HALVES) for i in range(RING)]
        for k in range(RING)
    ]

    def exchange(array, axis_name, groups=None):
        return lax.all_to_all(
            array, axis_name, split_axis=0, concat_axis=0, tiled=True, axis_index_groups=groups
        )

    def halves(array, which):
        return lax.dynamic_slice_in_dim(array, PAIR * which, PAIR, axis=0)

    (packets,) = call(
        pack_kernel,
        (jax.ShapeDtypeStruct((n_dp, capacity, wide), BF16),),
        (teacher_ids[0].T, tokens[0], route_weight[0]),
        mib=60,
    )
    group = exchange(packets, "dp").reshape(n_dp * capacity, wide)

    down = call(
        share_kernel,
        tuple(jax.ShapeDtypeStruct((PAIR + 1, block, quarter), BF16) for _ in range(RING)),
        (teacher_down, merged_down),
    )
    down = [down[k] if k == 0 else lax.ppermute(down[k], "dp", turns[k]) for k in range(RING)]
    early = [down[k] for k in EARLY]
    m_come = lax.ppermute(jnp.concatenate([merged_gate, merged_up], axis=0), "dp", swap)
    group, early, m_come = lax.optimization_barrier((group, early, m_come))
    for k, array in zip(EARLY, early):
        down[k] = array

    (slots,) = call(
        lambda *refs: slots_kernel(ranks, capacity, *refs),
        (jax.ShapeDtypeStruct((rows, wide), BF16),),
        (group,),
        mib=60,
    )
    slots = exchange(slots.reshape(experts, PAIR * capacity, wide), "expert").reshape(rows, wide)

    sent = [halves(teacher_gate, 1 - half), halves(teacher_up, 1 - half)]
    t_come = lax.ppermute(jnp.concatenate(sent, axis=0), "dp", swap)
    (passed,) = call(
        pass_kernel, (jax.ShapeDtypeStruct((RING, PAIR, block, quarter), BF16),), tuple(down), mib=60
    )
    slots, t_come, passed = lax.optimization_barrier((slots, t_come, passed))
    came = lax.ppermute(passed, "dp", swap)

    hidden, silu, slope, weight = call(
        lambda *refs: hidden_kernel(capacity, *refs),
        (
            jax.ShapeDtypeStruct((RING, 4, block, span), BF16),
            jax.ShapeDtypeStruct((2 * block, rows), F32),
            jax.ShapeDtypeStruct((2 * block, rows), F32),
            jax.ShapeDtypeStruct((rows, SIDE), BF16),
        ),
        (slots, teacher_gate, teacher_up, merged_gate, merged_up, t_come, m_come),
        far=range(7),
        scratch=[
            pltpu.VMEM((rows, wide), BF16),
            pltpu.VMEM((PAIR + 1, 4 * block, features), BF16),
            pltpu.SemaphoreType.DMA((4 * PAIR + 5,)),
        ],
        mib=60,
    )
    hidden = exchange(hidden, "dp", rings)
    hidden_grad, kept_down, other_down = call(
        gap_kernel,
        (
            jax.ShapeDtypeStruct((RING, 2 * block, span), BF16),
            jax.ShapeDtypeStruct((RING, block, quarter), BF16),
            jax.ShapeDtypeStruct((RING, block, quarter), BF16),
        ),
        (hidden, weight, came, *down),
        mib=60,
    )
    parts = exchange(hidden_grad, "dp", rings)
    other_down = lax.ppermute(other_down, "dp", swap)
    down_grad = (kept_down.astype(F32) + other_down.astype(F32)).astype(BF16)
    own, other = call(
        lambda *refs: grads_kernel(capacity, *refs),
        (
            jax.ShapeDtypeStruct((2, block, features), F32),
            jax.ShapeDtypeStruct((2, block, features), BF16),
        ),
        (parts, silu, slope, slots),
    )
    other = lax.ppermute(other, "dp", swap)
    down_grad = exchange(down_grad, "dp", rings)
    (grad_down,) = call(
        down_sum_kernel, (jax.ShapeDtypeStruct((block, features), F32),), (down_grad,)
    )
    grad_gate = own[:1] + other[:1].astype(F32)
    grad_up = own[1:] + other[1:].astype(F32)
    return grad_gate, grad_up, grad_down[None]


def solution(mesh):
    placed = (P("expert", "dp", None),) * 9
    return jax.shard_map(
        body,
        mesh=mesh,
        in_specs=placed,
        out_specs=(P("expert", "dp", None),) * 3,
        check_vma=False,
    )
```

```python
import jax
import jax.numpy as jnp
from jax import lax
from jax.experimental import pallas as pl
from jax.experimental.pallas import tpu as pltpu
from jax.sharding import PartitionSpec as P

HALVES = 2
PAIR = 2
EARLY = (1, 7)
PARTS = ((0, 1, 7), (2, 3, 4, 5, 6))
RING = 8
SIDE = 128
BF16 = jnp.bfloat16
F32 = jnp.float32


def dot_nn(a, b):
    return jnp.dot(a, b, preferred_element_type=F32)


def dot_nt(a, b):
    return lax.dot_general(a, b, (((1,), (1,)), ((), ())), preferred_element_type=F32)


def dot_tn(a, b):
    return lax.dot_general(a, b, (((0,), (0,)), ((), ())), preferred_element_type=F32)


def call(kernel, outs, args, far=(), scratch=(), mib=16):
    def space(i, alone):
        return pl.BlockSpec(memory_space=pltpu.HBM if i in alone else pltpu.VMEM)

    return pl.pallas_call(
        kernel,
        out_shape=outs,
        in_specs=[space(i, far) for i in range(len(args))],
        out_specs=[space(i, ()) for i in range(len(outs))],
        scratch_shapes=scratch,
        compiler_params=pltpu.CompilerParams(vmem_limit_bytes=mib * 1024 * 1024),
        cost_estimate=pl.CostEstimate(
            flops=0,
            bytes_accessed=sum(a.size * a.dtype.itemsize for a in args),
            transcendentals=0,
        ),
    )(*args)


def start_copies(pairs, sems, first=0):
    copies = [
        pltpu.make_async_copy(source, target, sems.at[first + i])
        for i, (source, target) in enumerate(pairs)
    ]
    for copy in copies:
        copy.start()
    return copies


def wait_copies(copies):
    for copy in copies:
        copy.wait()


def place():
    at = lax.axis_index("dp")
    return at // RING, at % RING


def pack_kernel(ids_ref, token_ref, weight_ref, out_ref):
    ranks, count = ids_ref.shape
    features = token_ref.shape[1]
    lane = lax.broadcasted_iota(jnp.int32, (ranks, SIDE), 1)
    rank = lax.broadcasted_iota(jnp.int32, (ranks, SIDE), 0)
    spread = jnp.where(lane == rank, 1.0, 0.0).astype(BF16)
    side = dot_tn(ids_ref[...].astype(F32).astype(BF16), spread)
    lane = lax.broadcasted_iota(jnp.int32, (count, SIDE), 1)
    weight = weight_ref[...].astype(F32)
    for k in range(ranks):
        side = jnp.where(lane == ranks + k, weight[:, k : k + 1], side)
    side = side.astype(BF16)
    tokens = token_ref[...]
    for i in range(out_ref.shape[0]):
        out_ref[i, :, :features] = tokens
        out_ref[i, :, features:] = side


def slots_kernel(ranks, capacity, group_ref, out_ref):
    half, _ = place()
    wide = group_ref.shape[1] - SIDE
    count = group_ref.shape[0]
    slots = out_ref.shape[0]
    side = group_ref[:, wide:].astype(F32)
    slot = lax.broadcasted_iota(jnp.int32, (count, slots), 1)
    column, inner = slot // (PAIR * capacity), slot % (PAIR * capacity)
    teacher = (column * HALVES * PAIR + half * PAIR + inner // capacity).astype(F32)
    position = (inner % capacity).astype(F32)
    hits = jnp.zeros((count, slots), F32)
    weight = jnp.zeros((count, slots), F32)
    for k in range(ranks):
        same = side[:, k : k + 1] == teacher
        hits = jnp.where(same, 1.0, hits)
        weight = jnp.where(same, side[:, ranks + k : ranks + k + 1], weight)
    later = lax.broadcasted_iota(jnp.int32, (count, count), 0)
    earlier = lax.broadcasted_iota(jnp.int32, (count, count), 1)
    below = jnp.where(earlier < later, 1.0, 0.0).astype(BF16)
    before = dot_nn(below, hits.astype(BF16))
    chosen = jnp.where((hits > 0.0) & (before == position), 1.0, 0.0)
    out_ref[:, :wide] = dot_tn(chosen.astype(BF16), group_ref[:, :wide]).astype(BF16)
    weights = dot_tn((chosen * weight).astype(BF16), jnp.ones((count, SIDE), BF16))
    out_ref[:, wide:] = weights.astype(BF16)


def by_teacher(count, capacity, source_axis):
    source = lax.broadcasted_iota(jnp.int32, (count, count), source_axis)
    target = lax.broadcasted_iota(jnp.int32, (count, count), 1 - source_axis)
    group, inner = source // (PAIR * capacity), source % (PAIR * capacity)
    goes = (inner // capacity) * (count // PAIR) + group * capacity + inner % capacity
    return jnp.where(goes == target, 1.0, 0.0).astype(BF16)


def silu_split(value):
    logistic = jax.nn.sigmoid(value)
    return value * logistic, logistic * (1.0 + value * (1.0 - logistic))


def hidden_kernel(
    capacity,
    rows_hbm,
    t_gate_hbm,
    t_up_hbm,
    m_gate_hbm,
    m_up_hbm,
    t_come_hbm,
    m_come_hbm,
    out_ref,
    silu_ref,
    slope_ref,
    weight_ref,
    row_buf,
    weight_buf,
    sems,
):
    half, _ = place()
    block = m_gate_hbm.shape[1]
    units = 2 * block
    count, wide = row_buf.shape
    features = wide - SIDE
    span = count // PAIR
    places = out_ref.shape[0] // PAIR

    def weights(at, *parts):
        pairs = [(part, weight_buf.at[at, pl.ds(i * block, block)]) for i, part in enumerate(parts)]
        return start_copies(pairs, sems, 4 * at)

    def gate_up(at):
        value = dot_nt(weight_buf[at], row_buf[:, :features])
        return value[:units], value[units:]

    first = start_copies([(rows_hbm, row_buf)], sems, 4 * PAIR + 4)
    first += weights(
        PAIR, m_gate_hbm.at[0], m_come_hbm.at[0], m_up_hbm.at[0], m_come_hbm.at[1]
    )
    later = []
    for m in range(PAIR):
        own = PAIR * half + m
        later.append(
            weights(m, t_gate_hbm.at[own], t_come_hbm.at[m], t_up_hbm.at[own], t_come_hbm.at[PAIR + m])
        )
    move = by_teacher(count, capacity, 0)
    wait_copies(first)
    gate, up = gate_up(PAIR)
    silu, slope = silu_split(gate)
    silu_ref[...] = silu
    slope_ref[...] = up * slope
    hidden = [(silu * up).astype(BF16)]
    for m in range(PAIR):
        wait_copies(later[m])
        gate, up = gate_up(m)
        silu, _ = silu_split(gate)
        hidden.append((silu * up).astype(BF16))
    hidden = dot_nn(jnp.concatenate(hidden, axis=0), move).astype(BF16)
    weight_ref[...] = dot_tn(move, row_buf[:, features:]).astype(BF16)
    for m in range(PAIR):
        lanes = slice(m * span, (m + 1) * span)
        first = (1 + m) * units
        for i in range(places):
            at = m * places + i
            out_ref[at, 0] = hidden[:block, lanes]
            out_ref[at, 1] = hidden[block:units, lanes]
            out_ref[at, 2] = hidden[first : first + block, lanes]
            out_ref[at, 3] = hidden[first + block : first + units, lanes]


def share_kernel(down_ref, merged_ref, *out_refs):
    half, at = place()
    quarter = out_refs[0].shape[2]
    for k, out_ref in enumerate(out_refs):
        there = (at + k) % RING
        m = there // (RING // PAIR)
        span = pl.ds(pl.multiple_of(there % (RING // PAIR) * quarter, SIDE), quarter)
        out_ref[0] = down_ref[PAIR * half + m, :, span]
        out_ref[1] = down_ref[PAIR * (1 - half) + m, :, span]
        out_ref[2] = merged_ref[0, :, span]


def pass_kernel(*refs):
    out_ref = refs[-1]
    for k, down_ref in enumerate(refs[:-1]):
        out_ref[k] = down_ref[1:]


def gap_kernel(hidden_ref, weight_ref, *refs):
    came_refs, down_refs = refs[:2], refs[2 : 2 + RING]
    grad_ref, kept_ref, other_ref = refs[2 + RING :]
    came = {
        k: came_ref.at[i] for came_ref, part in zip(came_refs, PARTS) for i, k in enumerate(part)
    }
    block = hidden_ref.shape[2]
    units = 2 * block
    span = hidden_ref.shape[3]
    _, at = place()
    back = [(at + RING - k) % RING for k in range(RING)]
    student = jnp.concatenate([hidden_ref[i, a] for i in back for a in (0, 1)], axis=0)
    teacher = jnp.concatenate([hidden_ref[i, a] for i in back for a in (2, 3)], axis=0)
    t_down = jnp.concatenate([x for k in range(RING) for x in (down_refs[k][0], came[k][0])], axis=0)
    m_down = jnp.concatenate([x for k in range(RING) for x in (down_refs[k][2], came[k][1])], axis=0)
    gap = dot_tn(student, m_down) - dot_tn(teacher, t_down)
    start = pl.multiple_of(at // (RING // PAIR) * span, span)
    weight = weight_ref[pl.ds(start, span), SIDE - 1 : SIDE].astype(F32)
    slot_grad = (weight * gap).astype(BF16)
    grad = dot_nt(m_down, slot_grad).astype(BF16)
    down_grad = dot_nn(student, slot_grad).astype(BF16)
    for k, i in enumerate(back):
        grad_ref[i] = grad[k * units : (k + 1) * units]
        kept_ref[i] = down_grad[k * units : k * units + block]
        other_ref[i] = down_grad[k * units + block : (k + 1) * units]


def grads_kernel(capacity, parts_ref, silu_ref, slope_ref, rows_ref, own_ref, other_ref):
    block = own_ref.shape[1]
    places = parts_ref.shape[0] // PAIR
    units = parts_ref.shape[1]
    count = rows_ref.shape[0]
    parts = jnp.concatenate(
        [
            jnp.concatenate([parts_ref[m * places + i] for i in range(places)], axis=0)
            for m in range(PAIR)
        ],
        axis=1,
    )
    parts = dot_nn(parts, by_teacher(count, capacity, 1))
    total = parts[:units]
    for i in range(1, places):
        total += parts[i * units : (i + 1) * units]
    gate = (total * slope_ref[...]).astype(BF16)
    up = (total * silu_ref[...]).astype(BF16)
    stack = jnp.concatenate([gate[:block], up[:block], gate[block:], up[block:]], axis=0)
    grads = dot_nn(stack, rows_ref[:, : own_ref.shape[2]])
    own_ref[0] = grads[:block]
    own_ref[1] = grads[block : 2 * block]
    other_ref[0] = grads[2 * block : 3 * block].astype(BF16)
    other_ref[1] = grads[3 * block :].astype(BF16)


def down_sum_kernel(parts_ref, out_ref):
    count, _, piece = parts_ref.shape
    quarters = out_ref.shape[1] // piece
    for q in range(quarters):
        total = parts_ref[q].astype(F32)
        for i in range(q + quarters, count, quarters):
            total += parts_ref[i].astype(F32)
        out_ref[:, q * piece : (q + 1) * piece] = total


def body(
    tokens,
    teacher_ids,
    route_weight,
    teacher_gate,
    teacher_up,
    teacher_down,
    merged_gate,
    merged_up,
    merged_down,
):
    n_dp = HALVES * RING
    experts = lax.axis_size("expert")
    features = tokens.shape[2]
    capacity = tokens.shape[1]
    ranks = teacher_ids.shape[2]
    block = merged_gate.shape[1]
    wide = features + SIDE
    quarter = features * PAIR // RING
    rows = experts * PAIR * capacity
    span = rows // PAIR
    half = lax.axis_index("dp") // RING
    rings = [[a * RING + i for i in range(RING)] for a in range(HALVES)]
    swap = [(a * RING + i, (1 - a) * RING + i) for a in range(HALVES) for i in range(RING)]

    turns = [
        [(a * RING + i, a * RING + (i + k) % RING) for a in range(HALVES) for i in range(RING)]
        for k in range(RING)
    ]

    def exchange(array, axis_name, groups=None):
        return lax.all_to_all(
            array, axis_name, split_axis=0, concat_axis=0, tiled=True, axis_index_groups=groups
        )

    def halves(array, which):
        return lax.dynamic_slice_in_dim(array, PAIR * which, PAIR, axis=0)

    (packets,) = call(
        pack_kernel,
        (jax.ShapeDtypeStruct((n_dp, capacity, wide), BF16),),
        (teacher_ids[0].T, tokens[0], route_weight[0]),
        mib=60,
    )
    group = exchange(packets, "dp").reshape(n_dp * capacity, wide)

    down = call(
        share_kernel,
        tuple(jax.ShapeDtypeStruct((PAIR + 1, block, quarter), BF16) for _ in range(RING)),
        (teacher_down, merged_down),
    )
    down = [down[k] if k == 0 else lax.ppermute(down[k], "dp", turns[k]) for k in range(RING)]
    early = [down[k] for k in EARLY]
    m_come = lax.ppermute(jnp.concatenate([merged_gate, merged_up], axis=0), "dp", swap)
    group, early, m_come = lax.optimization_barrier((group, early, m_come))
    for k, array in zip(EARLY, early):
        down[k] = array

    (slots,) = call(
        lambda *refs: slots_kernel(ranks, capacity, *refs),
        (jax.ShapeDtypeStruct((rows, wide), BF16),),
        (group,),
        mib=60,
    )
    slots = exchange(slots.reshape(experts, PAIR * capacity, wide), "expert").reshape(rows, wide)

    sent = [halves(teacher_gate, 1 - half), halves(teacher_up, 1 - half)]
    t_come = lax.ppermute(jnp.concatenate(sent, axis=0), "dp", swap)
    first, second = [
        call(
            pass_kernel,
            (jax.ShapeDtypeStruct((len(part), PAIR, block, quarter), BF16),),
            tuple(down[k] for k in part),
            mib=60,
        )[0]
        for part in PARTS
    ]
    first = lax.ppermute(first, "dp", swap)
    slots, t_come, first, second = lax.optimization_barrier((slots, t_come, first, second))
    second = lax.ppermute(second, "dp", swap)

    hidden, silu, slope, weight = call(
        lambda *refs: hidden_kernel(capacity, *refs),
        (
            jax.ShapeDtypeStruct((RING, 4, block, span), BF16),
            jax.ShapeDtypeStruct((2 * block, rows), F32),
            jax.ShapeDtypeStruct((2 * block, rows), F32),
            jax.ShapeDtypeStruct((rows, SIDE), BF16),
        ),
        (slots, teacher_gate, teacher_up, merged_gate, merged_up, t_come, m_come),
        far=range(7),
        scratch=[
            pltpu.VMEM((rows, wide), BF16),
            pltpu.VMEM((PAIR + 1, 4 * block, features), BF16),
            pltpu.SemaphoreType.DMA((4 * PAIR + 5,)),
        ],
        mib=60,
    )
    hidden = exchange(hidden, "dp", rings)
    hidden_grad, kept_down, other_down = call(
        gap_kernel,
        (
            jax.ShapeDtypeStruct((RING, 2 * block, span), BF16),
            jax.ShapeDtypeStruct((RING, block, quarter), BF16),
            jax.ShapeDtypeStruct((RING, block, quarter), BF16),
        ),
        (hidden, weight, first, second, *down),
        mib=60,
    )
    parts = exchange(hidden_grad, "dp", rings)
    other_down = lax.ppermute(other_down, "dp", swap)
    down_grad = (kept_down.astype(F32) + other_down.astype(F32)).astype(BF16)
    own, other = call(
        lambda *refs: grads_kernel(capacity, *refs),
        (
            jax.ShapeDtypeStruct((2, block, features), F32),
            jax.ShapeDtypeStruct((2, block, features), BF16),
        ),
        (parts, silu, slope, slots),
    )
    other = lax.ppermute(other, "dp", swap)
    down_grad = exchange(down_grad, "dp", rings)
    (grad_down,) = call(
        down_sum_kernel, (jax.ShapeDtypeStruct((block, features), F32),), (down_grad,)
    )
    grad_gate = own[:1] + other[:1].astype(F32)
    grad_up = own[1:] + other[1:].astype(F32)
    return grad_gate, grad_up, grad_down[None]


def solution(mesh):
    placed = (P("expert", "dp", None),) * 9
    return jax.shard_map(
        body,
        mesh=mesh,
        in_specs=placed,
        out_specs=(P("expert", "dp", None),) * 3,
        check_vma=False,
    )
```

```python
import jax
import jax.numpy as jnp
from jax import lax
from jax.experimental import pallas as pl
from jax.experimental.pallas import tpu as pltpu
from jax.sharding import PartitionSpec as P

HALVES = 2
PAIR = 2
EARLY = (1, 7)
PARTS = ((0, 1, 7), (2, 3, 4, 5, 6))
RING = 8
SIDE = 128
BF16 = jnp.bfloat16
F32 = jnp.float32


def dot_nn(a, b):
    return jnp.dot(a, b, preferred_element_type=F32)


def dot_nt(a, b):
    return lax.dot_general(a, b, (((1,), (1,)), ((), ())), preferred_element_type=F32)


def dot_tn(a, b):
    return lax.dot_general(a, b, (((0,), (0,)), ((), ())), preferred_element_type=F32)


def call(kernel, outs, args, far=(), far_outs=(), scratch=(), mib=16):
    def space(i, alone):
        return pl.BlockSpec(memory_space=pltpu.HBM if i in alone else pltpu.VMEM)

    return pl.pallas_call(
        kernel,
        out_shape=outs,
        in_specs=[space(i, far) for i in range(len(args))],
        out_specs=[space(i, far_outs) for i in range(len(outs))],
        scratch_shapes=scratch,
        compiler_params=pltpu.CompilerParams(vmem_limit_bytes=mib * 1024 * 1024),
        cost_estimate=pl.CostEstimate(
            flops=0,
            bytes_accessed=sum(a.size * a.dtype.itemsize for a in args),
            transcendentals=0,
        ),
    )(*args)


def start_copies(pairs, sems, first=0):
    copies = [
        pltpu.make_async_copy(source, target, sems.at[first + i])
        for i, (source, target) in enumerate(pairs)
    ]
    for copy in copies:
        copy.start()
    return copies


def wait_copies(copies):
    for copy in copies:
        copy.wait()


def place():
    at = lax.axis_index("dp")
    return at // RING, at % RING


def pack_kernel(ids_ref, token_ref, weight_ref, out_ref):
    ranks, _, count = ids_ref.shape
    features = token_ref.shape[1]
    lane = lax.broadcasted_iota(jnp.int32, (ranks, SIDE), 1)
    rank = lax.broadcasted_iota(jnp.int32, (ranks, SIDE), 0)
    spread = jnp.where(lane == rank, 1.0, 0.0).astype(BF16)
    ids = jnp.concatenate([ids_ref[k] for k in range(ranks)], axis=0)
    side = dot_tn(ids.astype(F32).astype(BF16), spread)
    lane = lax.broadcasted_iota(jnp.int32, (count, SIDE), 1)
    weight = weight_ref[...].astype(F32)
    for k in range(ranks):
        side = jnp.where(lane == ranks + k, weight[:, k : k + 1], side)
    side = side.astype(BF16)
    tokens = token_ref[...]
    for i in range(out_ref.shape[0]):
        out_ref[i, :, :features] = tokens
        out_ref[i, :, features:] = side


def slots_kernel(ranks, capacity, group_ref, out_hbm, out_ref, sems):
    half, _ = place()
    wide = group_ref.shape[1] - SIDE
    count = group_ref.shape[0]
    slots = out_ref.shape[0]
    side = group_ref[:, wide:].astype(F32)
    slot = lax.broadcasted_iota(jnp.int32, (count, slots), 1)
    column, inner = slot // (PAIR * capacity), slot % (PAIR * capacity)
    teacher = (column * HALVES * PAIR + half * PAIR + inner // capacity).astype(F32)
    position = (inner % capacity).astype(F32)
    hits = jnp.zeros((count, slots), F32)
    weight = jnp.zeros((count, slots), F32)
    for k in range(ranks):
        same = side[:, k : k + 1] == teacher
        hits = jnp.where(same, 1.0, hits)
        weight = jnp.where(same, side[:, ranks + k : ranks + k + 1], weight)
    later = lax.broadcasted_iota(jnp.int32, (count, count), 0)
    earlier = lax.broadcasted_iota(jnp.int32, (count, count), 1)
    below = jnp.where(earlier < later, 1.0, 0.0).astype(BF16)
    before = dot_nn(below, hits.astype(BF16))
    chosen = jnp.where((hits > 0.0) & (before == position), 1.0, 0.0)
    pick = chosen.astype(BF16)
    weights = dot_tn((chosen * weight).astype(BF16), jnp.ones((count, SIDE), BF16))
    out_ref[:, wide:] = weights.astype(BF16)
    tile = 7 * SIDE
    copies = []
    for n, start in enumerate(range(0, wide + SIDE, tile)):
        stop = min(start + tile, wide)
        out_ref[:, start:stop] = dot_tn(pick, group_ref[:, start:stop]).astype(BF16)
        span = (slice(None), pl.ds(start, tile))
        copies += start_copies([(out_ref.at[span], out_hbm.at[span])], sems, n)
    wait_copies(copies)


def by_teacher(count, capacity, source_axis):
    source = lax.broadcasted_iota(jnp.int32, (count, count), source_axis)
    target = lax.broadcasted_iota(jnp.int32, (count, count), 1 - source_axis)
    group, inner = source // (PAIR * capacity), source % (PAIR * capacity)
    goes = (inner // capacity) * (count // PAIR) + group * capacity + inner % capacity
    return jnp.where(goes == target, 1.0, 0.0).astype(BF16)


def silu_split(value):
    logistic = jax.nn.sigmoid(value)
    return value * logistic, logistic * (1.0 + value * (1.0 - logistic))


def hidden_kernel(
    capacity,
    rows_hbm,
    t_gate_hbm,
    t_up_hbm,
    m_gate_hbm,
    m_up_hbm,
    t_come_hbm,
    m_come_hbm,
    out_ref,
    silu_ref,
    slope_ref,
    weight_ref,
    row_buf,
    weight_buf,
    sems,
):
    half, _ = place()
    block = m_gate_hbm.shape[1]
    units = 2 * block
    count, wide = row_buf.shape
    features = wide - SIDE
    span = count // PAIR
    places = out_ref.shape[0] // PAIR

    def weights(at, *parts):
        pairs = [(part, weight_buf.at[at, pl.ds(i * block, block)]) for i, part in enumerate(parts)]
        return start_copies(pairs, sems, 4 * at)

    def gate_up(at):
        value = dot_nt(weight_buf[at], row_buf[:, :features])
        return value[:units], value[units:]

    first = start_copies([(rows_hbm, row_buf)], sems, 4 * PAIR + 4)
    first += weights(
        PAIR, m_gate_hbm.at[0], m_come_hbm.at[0], m_up_hbm.at[0], m_come_hbm.at[1]
    )
    later = []
    for m in range(PAIR):
        own = PAIR * half + m
        later.append(
            weights(m, t_gate_hbm.at[own], t_come_hbm.at[m], t_up_hbm.at[own], t_come_hbm.at[PAIR + m])
        )
    move = by_teacher(count, capacity, 0)
    wait_copies(first)
    gate, up = gate_up(PAIR)
    silu, slope = silu_split(gate)
    silu_ref[...] = silu
    slope_ref[...] = up * slope
    hidden = [(silu * up).astype(BF16)]
    for m in range(PAIR):
        wait_copies(later[m])
        gate, up = gate_up(m)
        silu, _ = silu_split(gate)
        hidden.append((silu * up).astype(BF16))
    hidden = dot_nn(jnp.concatenate(hidden, axis=0), move).astype(BF16)
    weight_ref[...] = dot_tn(move, row_buf[:, features:]).astype(BF16)
    for m in range(PAIR):
        lanes = slice(m * span, (m + 1) * span)
        first = (1 + m) * units
        for i in range(places):
            at = m * places + i
            out_ref[at, 0] = hidden[:block, lanes]
            out_ref[at, 1] = hidden[block:units, lanes]
            out_ref[at, 2] = hidden[first : first + block, lanes]
            out_ref[at, 3] = hidden[first + block : first + units, lanes]


def share_kernel(down_ref, merged_ref, *out_refs):
    half, at = place()
    quarter = out_refs[0].shape[2]
    for k, out_ref in enumerate(out_refs):
        there = (at + k) % RING
        m = there // (RING // PAIR)
        span = pl.ds(pl.multiple_of(there % (RING // PAIR) * quarter, SIDE), quarter)
        out_ref[0] = down_ref[PAIR * half + m, :, span]
        out_ref[1] = down_ref[PAIR * (1 - half) + m, :, span]
        out_ref[2] = merged_ref[0, :, span]


def pass_kernel(*refs):
    out_ref = refs[-1]
    for k, down_ref in enumerate(refs[:-1]):
        out_ref[k] = down_ref[1:]


def gap_kernel(hidden_ref, weight_ref, *refs):
    came_refs, down_refs = refs[:2], refs[2 : 2 + RING]
    grad_ref, kept_ref, other_ref = refs[2 + RING :]
    came = {
        k: came_ref.at[i] for came_ref, part in zip(came_refs, PARTS) for i, k in enumerate(part)
    }
    block = hidden_ref.shape[2]
    units = 2 * block
    span = hidden_ref.shape[3]
    _, at = place()
    back = [(at + RING - k) % RING for k in range(RING)]
    student = jnp.concatenate([hidden_ref[i, a] for i in back for a in (0, 1)], axis=0)
    teacher = jnp.concatenate([hidden_ref[i, a] for i in back for a in (2, 3)], axis=0)
    t_down = jnp.concatenate([x for k in range(RING) for x in (down_refs[k][0], came[k][0])], axis=0)
    m_down = jnp.concatenate([x for k in range(RING) for x in (down_refs[k][2], came[k][1])], axis=0)
    gap = dot_tn(student, m_down) - dot_tn(teacher, t_down)
    start = pl.multiple_of(at // (RING // PAIR) * span, span)
    weight = weight_ref[pl.ds(start, span), SIDE - 1 : SIDE].astype(F32)
    slot_grad = (weight * gap).astype(BF16)
    grad = dot_nt(m_down, slot_grad).astype(BF16)
    down_grad = dot_nn(student, slot_grad).astype(BF16)
    for k, i in enumerate(back):
        grad_ref[i] = grad[k * units : (k + 1) * units]
        kept_ref[i] = down_grad[k * units : k * units + block]
        other_ref[i] = down_grad[k * units + block : (k + 1) * units]


def other_kernel(capacity, parts_ref, silu_ref, slope_ref, rows_ref, other_ref, stack_ref):
    block = other_ref.shape[1]
    places = parts_ref.shape[0] // PAIR
    units = parts_ref.shape[1]
    count = rows_ref.shape[0]
    parts = jnp.concatenate(
        [
            jnp.concatenate([parts_ref[m * places + i] for i in range(places)], axis=0)
            for m in range(PAIR)
        ],
        axis=1,
    )
    parts = dot_nn(parts, by_teacher(count, capacity, 1))
    total = parts[:units]
    for i in range(1, places):
        total += parts[i * units : (i + 1) * units]
    gate = (total * slope_ref[...]).astype(BF16)
    up = (total * silu_ref[...]).astype(BF16)
    stack_ref[...] = jnp.concatenate([gate[:block], up[:block]], axis=0)
    stack = jnp.concatenate([gate[block:], up[block:]], axis=0)
    grads = dot_nn(stack, rows_ref[:, : other_ref.shape[2]])
    other_ref[0] = grads[:block].astype(BF16)
    other_ref[1] = grads[block:].astype(BF16)


def own_kernel(stack_ref, rows_ref, own_ref):
    block = own_ref.shape[1]
    grads = dot_nn(stack_ref[...], rows_ref[:, : own_ref.shape[2]])
    own_ref[0] = grads[:block]
    own_ref[1] = grads[block:]


def down_sum_kernel(parts_ref, out_ref):
    count, _, piece = parts_ref.shape
    quarters = out_ref.shape[1] // piece
    for q in range(quarters):
        total = parts_ref[q].astype(F32)
        for i in range(q + quarters, count, quarters):
            total += parts_ref[i].astype(F32)
        out_ref[:, q * piece : (q + 1) * piece] = total


def body(
    tokens,
    teacher_ids,
    route_weight,
    teacher_gate,
    teacher_up,
    teacher_down,
    merged_gate,
    merged_up,
    merged_down,
):
    n_dp = HALVES * RING
    experts = lax.axis_size("expert")
    features = tokens.shape[2]
    capacity = tokens.shape[1]
    ranks = teacher_ids.shape[2]
    block = merged_gate.shape[1]
    wide = features + SIDE
    quarter = features * PAIR // RING
    rows = experts * PAIR * capacity
    span = rows // PAIR
    half = lax.axis_index("dp") // RING
    rings = [[a * RING + i for i in range(RING)] for a in range(HALVES)]
    swap = [(a * RING + i, (1 - a) * RING + i) for a in range(HALVES) for i in range(RING)]

    turns = [
        [(a * RING + i, a * RING + (i + k) % RING) for a in range(HALVES) for i in range(RING)]
        for k in range(RING)
    ]

    def exchange(array, axis_name, groups=None):
        return lax.all_to_all(
            array, axis_name, split_axis=0, concat_axis=0, tiled=True, axis_index_groups=groups
        )

    def halves(array, which):
        return lax.dynamic_slice_in_dim(array, PAIR * which, PAIR, axis=0)

    (packets,) = call(
        pack_kernel,
        (jax.ShapeDtypeStruct((n_dp, capacity, wide), BF16),),
        (teacher_ids.transpose(2, 0, 1), tokens[0], route_weight[0]),
        mib=60,
    )
    group = exchange(packets, "dp").reshape(n_dp * capacity, wide)

    down = call(
        share_kernel,
        tuple(jax.ShapeDtypeStruct((PAIR + 1, block, quarter), BF16) for _ in range(RING)),
        (teacher_down, merged_down),
    )
    down = [down[k] if k == 0 else lax.ppermute(down[k], "dp", turns[k]) for k in range(RING)]
    early = [down[k] for k in EARLY]
    m_come = lax.ppermute(jnp.concatenate([merged_gate, merged_up], axis=0), "dp", swap)
    group, early, m_come = lax.optimization_barrier((group, early, m_come))
    for k, array in zip(EARLY, early):
        down[k] = array

    (slots,) = call(
        lambda *refs: slots_kernel(ranks, capacity, *refs),
        (jax.ShapeDtypeStruct((rows, wide), BF16),),
        (group,),
        far_outs=(0,),
        scratch=[pltpu.VMEM((rows, wide), BF16), pltpu.SemaphoreType.DMA((8,))],
        mib=60,
    )
    slots = exchange(slots.reshape(experts, PAIR * capacity, wide), "expert").reshape(rows, wide)

    sent = [halves(teacher_gate, 1 - half), halves(teacher_up, 1 - half)]
    t_come = lax.ppermute(jnp.concatenate(sent, axis=0), "dp", swap)
    first, second = [
        call(
            pass_kernel,
            (jax.ShapeDtypeStruct((len(part), PAIR, block, quarter), BF16),),
            tuple(down[k] for k in part),
            mib=60,
        )[0]
        for part in PARTS
    ]
    first = lax.ppermute(first, "dp", swap)
    slots, t_come, first, second = lax.optimization_barrier((slots, t_come, first, second))
    second = lax.ppermute(second, "dp", swap)

    hidden, silu, slope, weight = call(
        lambda *refs: hidden_kernel(capacity, *refs),
        (
            jax.ShapeDtypeStruct((RING, 4, block, span), BF16),
            jax.ShapeDtypeStruct((2 * block, rows), F32),
            jax.ShapeDtypeStruct((2 * block, rows), F32),
            jax.ShapeDtypeStruct((rows, SIDE), BF16),
        ),
        (slots, teacher_gate, teacher_up, merged_gate, merged_up, t_come, m_come),
        far=range(7),
        scratch=[
            pltpu.VMEM((rows, wide), BF16),
            pltpu.VMEM((PAIR + 1, 4 * block, features), BF16),
            pltpu.SemaphoreType.DMA((4 * PAIR + 5,)),
        ],
        mib=60,
    )
    hidden = exchange(hidden, "dp", rings)
    hidden_grad, kept_down, other_down = call(
        gap_kernel,
        (
            jax.ShapeDtypeStruct((RING, 2 * block, span), BF16),
            jax.ShapeDtypeStruct((RING, block, quarter), BF16),
            jax.ShapeDtypeStruct((RING, block, quarter), BF16),
        ),
        (hidden, weight, first, second, *down),
        mib=60,
    )
    parts = exchange(hidden_grad, "dp", rings)
    other_down = lax.ppermute(other_down, "dp", swap)
    down_grad = (kept_down.astype(F32) + other_down.astype(F32)).astype(BF16)
    other, stack = call(
        lambda *refs: other_kernel(capacity, *refs),
        (
            jax.ShapeDtypeStruct((2, block, features), BF16),
            jax.ShapeDtypeStruct((2 * block, rows), BF16),
        ),
        (parts, silu, slope, slots),
    )
    (own,) = call(
        own_kernel, (jax.ShapeDtypeStruct((2, block, features), F32),), (stack, slots)
    )
    other = lax.ppermute(other, "dp", swap)
    down_grad = exchange(down_grad, "dp", rings)
    (grad_down,) = call(
        down_sum_kernel, (jax.ShapeDtypeStruct((block, features), F32),), (down_grad,)
    )
    grad_gate = own[:1] + other[:1].astype(F32)
    grad_up = own[1:] + other[1:].astype(F32)
    return grad_gate, grad_up, grad_down[None]


def solution(mesh):
    placed = (P("expert", "dp", None),) * 9
    return jax.shard_map(
        body,
        mesh=mesh,
        in_specs=placed,
        out_specs=(P("expert", "dp", None),) * 3,
        check_vma=False,
    )
```

```python
import jax
import jax.numpy as jnp
from jax import lax
from jax.experimental import pallas as pl
from jax.experimental.pallas import tpu as pltpu
from jax.sharding import PartitionSpec as P

HALVES = 2
PAIR = 2
EARLY = (1, 7)
PARTS = ((0, 1, 7), (2, 3, 4, 5, 6))
RING = 8
SUM_COST = 2_000_000_000
SIDE = 128
BF16 = jnp.bfloat16
F32 = jnp.float32


def dot_nn(a, b):
    return jnp.dot(a, b, preferred_element_type=F32)


def dot_nt(a, b):
    return lax.dot_general(a, b, (((1,), (1,)), ((), ())), preferred_element_type=F32)


def dot_tn(a, b):
    return lax.dot_general(a, b, (((0,), (0,)), ((), ())), preferred_element_type=F32)


def call(kernel, outs, args, far=(), far_outs=(), scratch=(), mib=16, flops=0):
    def space(i, alone):
        return pl.BlockSpec(memory_space=pltpu.HBM if i in alone else pltpu.VMEM)

    return pl.pallas_call(
        kernel,
        out_shape=outs,
        in_specs=[space(i, far) for i in range(len(args))],
        out_specs=[space(i, far_outs) for i in range(len(outs))],
        scratch_shapes=scratch,
        compiler_params=pltpu.CompilerParams(vmem_limit_bytes=mib * 1024 * 1024),
        cost_estimate=pl.CostEstimate(
            flops=flops,
            bytes_accessed=sum(a.size * a.dtype.itemsize for a in args),
            transcendentals=0,
        ),
    )(*args)


def start_copies(pairs, sems, first=0):
    copies = [
        pltpu.make_async_copy(source, target, sems.at[first + i])
        for i, (source, target) in enumerate(pairs)
    ]
    for copy in copies:
        copy.start()
    return copies


def wait_copies(copies):
    for copy in copies:
        copy.wait()


def place():
    at = lax.axis_index("dp")
    return at // RING, at % RING


def pack_kernel(ids_ref, token_ref, weight_ref, out_ref):
    ranks, _, count = ids_ref.shape
    features = token_ref.shape[1]
    lane = lax.broadcasted_iota(jnp.int32, (ranks, SIDE), 1)
    rank = lax.broadcasted_iota(jnp.int32, (ranks, SIDE), 0)
    spread = jnp.where(lane == rank, 1.0, 0.0).astype(BF16)
    ids = jnp.concatenate([ids_ref[k] for k in range(ranks)], axis=0)
    side = dot_tn(ids.astype(F32).astype(BF16), spread)
    lane = lax.broadcasted_iota(jnp.int32, (count, SIDE), 1)
    weight = weight_ref[...].astype(F32)
    for k in range(ranks):
        side = jnp.where(lane == ranks + k, weight[:, k : k + 1], side)
    side = side.astype(BF16)
    tokens = token_ref[...]
    for i in range(out_ref.shape[0]):
        out_ref[i, :, :features] = tokens
        out_ref[i, :, features:] = side


def slots_kernel(ranks, capacity, group_ref, out_hbm, out_ref, sems):
    half, _ = place()
    wide = group_ref.shape[1] - SIDE
    count = group_ref.shape[0]
    slots = out_ref.shape[0]
    side = group_ref[:, wide:].astype(F32)
    slot = lax.broadcasted_iota(jnp.int32, (count, slots), 1)
    column, inner = slot // (PAIR * capacity), slot % (PAIR * capacity)
    teacher = (column * HALVES * PAIR + half * PAIR + inner // capacity).astype(F32)
    position = (inner % capacity).astype(F32)
    hits = jnp.zeros((count, slots), F32)
    weight = jnp.zeros((count, slots), F32)
    for k in range(ranks):
        same = side[:, k : k + 1] == teacher
        hits = jnp.where(same, 1.0, hits)
        weight = jnp.where(same, side[:, ranks + k : ranks + k + 1], weight)
    later = lax.broadcasted_iota(jnp.int32, (count, count), 0)
    earlier = lax.broadcasted_iota(jnp.int32, (count, count), 1)
    below = jnp.where(earlier < later, 1.0, 0.0).astype(BF16)
    before = dot_nn(below, hits.astype(BF16))
    chosen = jnp.where((hits > 0.0) & (before == position), 1.0, 0.0)
    pick = chosen.astype(BF16)
    weights = dot_tn((chosen * weight).astype(BF16), jnp.ones((count, SIDE), BF16))
    out_ref[:, wide:] = weights.astype(BF16)
    tile = 7 * SIDE
    copies = []
    for n, start in enumerate(range(0, wide + SIDE, tile)):
        stop = min(start + tile, wide)
        out_ref[:, start:stop] = dot_tn(pick, group_ref[:, start:stop]).astype(BF16)
        span = (slice(None), pl.ds(start, tile))
        copies += start_copies([(out_ref.at[span], out_hbm.at[span])], sems, n)
    wait_copies(copies)


def by_teacher(count, capacity, source_axis):
    source = lax.broadcasted_iota(jnp.int32, (count, count), source_axis)
    target = lax.broadcasted_iota(jnp.int32, (count, count), 1 - source_axis)
    group, inner = source // (PAIR * capacity), source % (PAIR * capacity)
    goes = (inner // capacity) * (count // PAIR) + group * capacity + inner % capacity
    return jnp.where(goes == target, 1.0, 0.0).astype(BF16)


def silu_split(value):
    logistic = jax.nn.sigmoid(value)
    return value * logistic, logistic * (1.0 + value * (1.0 - logistic))


def hidden_kernel(
    capacity,
    rows_hbm,
    t_gate_hbm,
    t_up_hbm,
    m_gate_hbm,
    m_up_hbm,
    t_come_hbm,
    m_come_hbm,
    out_ref,
    silu_ref,
    slope_ref,
    weight_ref,
    row_buf,
    weight_buf,
    sems,
):
    half, _ = place()
    block = m_gate_hbm.shape[1]
    units = 2 * block
    count, wide = row_buf.shape
    features = wide - SIDE
    span = count // PAIR
    places = out_ref.shape[0] // PAIR

    def weights(at, *parts):
        pairs = [(part, weight_buf.at[at, pl.ds(i * block, block)]) for i, part in enumerate(parts)]
        return start_copies(pairs, sems, 4 * at)

    def gate_up(at):
        value = dot_nt(weight_buf[at], row_buf[:, :features])
        return value[:units], value[units:]

    first = start_copies([(rows_hbm, row_buf)], sems, 4 * PAIR + 4)
    first += weights(
        PAIR, m_gate_hbm.at[0], m_come_hbm.at[0], m_up_hbm.at[0], m_come_hbm.at[1]
    )
    later = []
    for m in range(PAIR):
        own = PAIR * half + m
        later.append(
            weights(m, t_gate_hbm.at[own], t_come_hbm.at[m], t_up_hbm.at[own], t_come_hbm.at[PAIR + m])
        )
    move = by_teacher(count, capacity, 0)
    wait_copies(first)
    gate, up = gate_up(PAIR)
    silu, slope = silu_split(gate)
    silu_ref[...] = silu
    slope_ref[...] = up * slope
    hidden = [(silu * up).astype(BF16)]
    for m in range(PAIR):
        wait_copies(later[m])
        gate, up = gate_up(m)
        silu, _ = silu_split(gate)
        hidden.append((silu * up).astype(BF16))
    hidden = dot_nn(jnp.concatenate(hidden, axis=0), move).astype(BF16)
    weight_ref[...] = dot_tn(move, row_buf[:, features:]).astype(BF16)
    for m in range(PAIR):
        lanes = slice(m * span, (m + 1) * span)
        first = (1 + m) * units
        for i in range(places):
            at = m * places + i
            out_ref[at, 0] = hidden[:block, lanes]
            out_ref[at, 1] = hidden[block:units, lanes]
            out_ref[at, 2] = hidden[first : first + block, lanes]
            out_ref[at, 3] = hidden[first + block : first + units, lanes]


def share_kernel(down_ref, merged_ref, *out_refs):
    half, at = place()
    quarter = out_refs[0].shape[2]
    for k, out_ref in enumerate(out_refs):
        there = (at + k) % RING
        m = there // (RING // PAIR)
        span = pl.ds(pl.multiple_of(there % (RING // PAIR) * quarter, SIDE), quarter)
        out_ref[0] = down_ref[PAIR * half + m, :, span]
        out_ref[1] = down_ref[PAIR * (1 - half) + m, :, span]
        out_ref[2] = merged_ref[0, :, span]


def pass_kernel(*refs):
    out_ref = refs[-1]
    for k, down_ref in enumerate(refs[:-1]):
        out_ref[k] = down_ref[1:]


def gap_kernel(hidden_ref, weight_ref, *refs):
    came_refs, down_refs = refs[:2], refs[2 : 2 + RING]
    grad_ref, kept_ref, other_ref = refs[2 + RING :]
    came = {
        k: came_ref.at[i] for came_ref, part in zip(came_refs, PARTS) for i, k in enumerate(part)
    }
    block = hidden_ref.shape[2]
    units = 2 * block
    span = hidden_ref.shape[3]
    _, at = place()
    back = [(at + RING - k) % RING for k in range(RING)]
    student = jnp.concatenate([hidden_ref[i, a] for i in back for a in (0, 1)], axis=0)
    teacher = jnp.concatenate([hidden_ref[i, a] for i in back for a in (2, 3)], axis=0)
    t_down = jnp.concatenate([x for k in range(RING) for x in (down_refs[k][0], came[k][0])], axis=0)
    m_down = jnp.concatenate([x for k in range(RING) for x in (down_refs[k][2], came[k][1])], axis=0)
    gap = dot_tn(student, m_down) - dot_tn(teacher, t_down)
    start = pl.multiple_of(at // (RING // PAIR) * span, span)
    weight = weight_ref[pl.ds(start, span), SIDE - 1 : SIDE].astype(F32)
    slot_grad = (weight * gap).astype(BF16)
    grad = dot_nt(m_down, slot_grad).astype(BF16)
    down_grad = dot_nn(student, slot_grad).astype(BF16)
    for k, i in enumerate(back):
        grad_ref[i] = grad[k * units : (k + 1) * units]
        kept_ref[i] = down_grad[k * units : k * units + block]
        other_ref[i] = down_grad[k * units + block : (k + 1) * units]


def other_kernel(capacity, parts_ref, silu_ref, slope_ref, rows_ref, other_ref, stack_ref):
    block = other_ref.shape[1]
    places = parts_ref.shape[0] // PAIR
    units = parts_ref.shape[1]
    count = rows_ref.shape[0]
    parts = jnp.concatenate(
        [
            jnp.concatenate([parts_ref[m * places + i] for i in range(places)], axis=0)
            for m in range(PAIR)
        ],
        axis=1,
    )
    parts = dot_nn(parts, by_teacher(count, capacity, 1))
    total = parts[:units]
    for i in range(1, places):
        total += parts[i * units : (i + 1) * units]
    gate = (total * slope_ref[...]).astype(BF16)
    up = (total * silu_ref[...]).astype(BF16)
    stack_ref[...] = jnp.concatenate([gate[:block], up[:block]], axis=0)
    stack = jnp.concatenate([gate[block:], up[block:]], axis=0)
    grads = dot_nn(stack, rows_ref[:, : other_ref.shape[2]])
    other_ref[0] = grads[:block].astype(BF16)
    other_ref[1] = grads[block:].astype(BF16)


def own_kernel(stack_ref, rows_ref, own_ref):
    block = own_ref.shape[1]
    grads = dot_nn(stack_ref[...], rows_ref[:, : own_ref.shape[2]])
    own_ref[0] = grads[:block]
    own_ref[1] = grads[block:]


def add_kernel(own_ref, other_ref, gate_ref, up_ref):
    gate_ref[...] = own_ref[:1] + other_ref[:1].astype(F32)
    up_ref[...] = own_ref[1:] + other_ref[1:].astype(F32)


def down_add_kernel(kept_ref, other_ref, out_ref):
    out_ref[...] = (kept_ref[...].astype(F32) + other_ref[...].astype(F32)).astype(BF16)


def down_sum_kernel(parts_ref, out_ref):
    count, _, piece = parts_ref.shape
    quarters = out_ref.shape[1] // piece
    for q in range(quarters):
        total = parts_ref[q].astype(F32)
        for i in range(q + quarters, count, quarters):
            total += parts_ref[i].astype(F32)
        out_ref[:, q * piece : (q + 1) * piece] = total


def body(
    tokens,
    teacher_ids,
    route_weight,
    teacher_gate,
    teacher_up,
    teacher_down,
    merged_gate,
    merged_up,
    merged_down,
):
    n_dp = HALVES * RING
    experts = lax.axis_size("expert")
    features = tokens.shape[2]
    capacity = tokens.shape[1]
    ranks = teacher_ids.shape[2]
    block = merged_gate.shape[1]
    wide = features + SIDE
    quarter = features * PAIR // RING
    rows = experts * PAIR * capacity
    span = rows // PAIR
    half = lax.axis_index("dp") // RING
    rings = [[a * RING + i for i in range(RING)] for a in range(HALVES)]
    swap = [(a * RING + i, (1 - a) * RING + i) for a in range(HALVES) for i in range(RING)]

    turns = [
        [(a * RING + i, a * RING + (i + k) % RING) for a in range(HALVES) for i in range(RING)]
        for k in range(RING)
    ]

    def exchange(array, axis_name, groups=None):
        return lax.all_to_all(
            array, axis_name, split_axis=0, concat_axis=0, tiled=True, axis_index_groups=groups
        )

    def halves(array, which):
        return lax.dynamic_slice_in_dim(array, PAIR * which, PAIR, axis=0)

    (packets,) = call(
        pack_kernel,
        (jax.ShapeDtypeStruct((n_dp, capacity, wide), BF16),),
        (teacher_ids.transpose(2, 0, 1), tokens[0], route_weight[0]),
        mib=60,
    )
    group = exchange(packets, "dp").reshape(n_dp * capacity, wide)

    down = call(
        share_kernel,
        tuple(jax.ShapeDtypeStruct((PAIR + 1, block, quarter), BF16) for _ in range(RING)),
        (teacher_down, merged_down),
    )
    down = [down[k] if k == 0 else lax.ppermute(down[k], "dp", turns[k]) for k in range(RING)]
    early = [down[k] for k in EARLY]
    m_come = lax.ppermute(jnp.concatenate([merged_gate, merged_up], axis=0), "dp", swap)
    group, early, m_come = lax.optimization_barrier((group, early, m_come))
    for k, array in zip(EARLY, early):
        down[k] = array

    (slots,) = call(
        lambda *refs: slots_kernel(ranks, capacity, *refs),
        (jax.ShapeDtypeStruct((rows, wide), BF16),),
        (group,),
        far_outs=(0,),
        scratch=[pltpu.VMEM((rows, wide), BF16), pltpu.SemaphoreType.DMA((8,))],
        mib=60,
    )
    slots = exchange(slots.reshape(experts, PAIR * capacity, wide), "expert").reshape(rows, wide)

    sent = [halves(teacher_gate, 1 - half), halves(teacher_up, 1 - half)]
    t_come = lax.ppermute(jnp.concatenate(sent, axis=0), "dp", swap)
    first, second = [
        call(
            pass_kernel,
            (jax.ShapeDtypeStruct((len(part), PAIR, block, quarter), BF16),),
            tuple(down[k] for k in part),
            mib=60,
        )[0]
        for part in PARTS
    ]
    first = lax.ppermute(first, "dp", swap)
    slots, t_come, first, second = lax.optimization_barrier((slots, t_come, first, second))
    second = lax.ppermute(second, "dp", swap)

    hidden, silu, slope, weight = call(
        lambda *refs: hidden_kernel(capacity, *refs),
        (
            jax.ShapeDtypeStruct((RING, 4, block, span), BF16),
            jax.ShapeDtypeStruct((2 * block, rows), F32),
            jax.ShapeDtypeStruct((2 * block, rows), F32),
            jax.ShapeDtypeStruct((rows, SIDE), BF16),
        ),
        (slots, teacher_gate, teacher_up, merged_gate, merged_up, t_come, m_come),
        far=range(7),
        scratch=[
            pltpu.VMEM((rows, wide), BF16),
            pltpu.VMEM((PAIR + 1, 4 * block, features), BF16),
            pltpu.SemaphoreType.DMA((4 * PAIR + 5,)),
        ],
        mib=60,
    )
    hidden = exchange(hidden, "dp", rings)
    hidden_grad, kept_down, other_down = call(
        gap_kernel,
        (
            jax.ShapeDtypeStruct((RING, 2 * block, span), BF16),
            jax.ShapeDtypeStruct((RING, block, quarter), BF16),
            jax.ShapeDtypeStruct((RING, block, quarter), BF16),
        ),
        (hidden, weight, first, second, *down),
        mib=60,
    )
    parts = exchange(hidden_grad, "dp", rings)
    other_down = lax.ppermute(other_down, "dp", swap)
    (down_grad,) = call(
        down_add_kernel,
        (jax.ShapeDtypeStruct((RING, block, quarter), BF16),),
        (kept_down, other_down),
        mib=16,
        flops=0,
    )
    other, stack = call(
        lambda *refs: other_kernel(capacity, *refs),
        (
            jax.ShapeDtypeStruct((2, block, features), BF16),
            jax.ShapeDtypeStruct((2 * block, rows), BF16),
        ),
        (parts, silu, slope, slots),
    )
    (own,) = call(
        own_kernel, (jax.ShapeDtypeStruct((2, block, features), F32),), (stack, slots)
    )
    other = lax.ppermute(other, "dp", swap)
    down_grad = exchange(down_grad, "dp", rings)
    (grad_down,) = call(
        down_sum_kernel, (jax.ShapeDtypeStruct((block, features), F32),), (down_grad,), flops=SUM_COST
    )
    shape = jax.ShapeDtypeStruct((1, block, features), F32)
    grad_gate, grad_up = call(add_kernel, (shape, shape), (own, other))
    return grad_gate, grad_up, grad_down[None]


def solution(mesh):
    placed = (P("expert", "dp", None),) * 9
    return jax.shard_map(
        body,
        mesh=mesh,
        in_specs=placed,
        out_specs=(P("expert", "dp", None),) * 3,
        check_vma=False,
    )
```

```python
import jax
import jax.numpy as jnp
from jax import lax
from jax.experimental import pallas as pl
from jax.experimental.pallas import tpu as pltpu
from jax.sharding import PartitionSpec as P

HALVES = 2
PAIR = 2
EARLY = (1, 7)
PARTS = ((0, 1, 7), (2, 3, 4, 5, 6))
RING = 8
SIDE = 128
BF16 = jnp.bfloat16
F32 = jnp.float32


def dot_nn(a, b):
    return jnp.dot(a, b, preferred_element_type=F32)


def dot_nt(a, b):
    return lax.dot_general(a, b, (((1,), (1,)), ((), ())), preferred_element_type=F32)


def dot_tn(a, b):
    return lax.dot_general(a, b, (((0,), (0,)), ((), ())), preferred_element_type=F32)


def call(kernel, outs, args, far=(), far_outs=(), scratch=(), mib=16):
    def space(i, alone):
        return pl.BlockSpec(memory_space=pltpu.HBM if i in alone else pltpu.VMEM)

    return pl.pallas_call(
        kernel,
        out_shape=outs,
        in_specs=[space(i, far) for i in range(len(args))],
        out_specs=[space(i, far_outs) for i in range(len(outs))],
        scratch_shapes=scratch,
        compiler_params=pltpu.CompilerParams(vmem_limit_bytes=mib * 1024 * 1024),
        cost_estimate=pl.CostEstimate(
            flops=0,
            bytes_accessed=sum(a.size * a.dtype.itemsize for a in args),
            transcendentals=0,
        ),
    )(*args)


def start_copies(pairs, sems, first=0):
    copies = [
        pltpu.make_async_copy(source, target, sems.at[first + i])
        for i, (source, target) in enumerate(pairs)
    ]
    for copy in copies:
        copy.start()
    return copies


def wait_copies(copies):
    for copy in copies:
        copy.wait()


def place():
    at = lax.axis_index("dp")
    return at // RING, at % RING


def pack_kernel(ids_ref, token_ref, weight_ref, out_ref):
    ranks, _, count = ids_ref.shape
    features = token_ref.shape[1]
    lane = lax.broadcasted_iota(jnp.int32, (ranks, SIDE), 1)
    rank = lax.broadcasted_iota(jnp.int32, (ranks, SIDE), 0)
    spread = jnp.where(lane == rank, 1.0, 0.0).astype(BF16)
    ids = jnp.concatenate([ids_ref[k] for k in range(ranks)], axis=0)
    side = dot_tn(ids.astype(F32).astype(BF16), spread)
    lane = lax.broadcasted_iota(jnp.int32, (count, SIDE), 1)
    weight = weight_ref[...].astype(F32)
    for k in range(ranks):
        side = jnp.where(lane == ranks + k, weight[:, k : k + 1], side)
    side = side.astype(BF16)
    tokens = token_ref[...]
    for i in range(out_ref.shape[0]):
        out_ref[i, :, :features] = tokens
        out_ref[i, :, features:] = side


def slots_kernel(ranks, capacity, group_ref, out_hbm, out_ref, sems):
    half, _ = place()
    wide = group_ref.shape[1] - SIDE
    count = group_ref.shape[0]
    slots = out_ref.shape[0]
    side = group_ref[:, wide:].astype(F32)
    slot = lax.broadcasted_iota(jnp.int32, (count, slots), 1)
    column, inner = slot // (PAIR * capacity), slot % (PAIR * capacity)
    teacher = (column * HALVES * PAIR + half * PAIR + inner // capacity).astype(F32)
    position = (inner % capacity).astype(F32)
    hits = jnp.zeros((count, slots), F32)
    weight = jnp.zeros((count, slots), F32)
    for k in range(ranks):
        same = side[:, k : k + 1] == teacher
        hits = jnp.where(same, 1.0, hits)
        weight = jnp.where(same, side[:, ranks + k : ranks + k + 1], weight)
    later = lax.broadcasted_iota(jnp.int32, (count, count), 0)
    earlier = lax.broadcasted_iota(jnp.int32, (count, count), 1)
    below = jnp.where(earlier < later, 1.0, 0.0).astype(BF16)
    before = dot_nn(below, hits.astype(BF16))
    chosen = jnp.where((hits > 0.0) & (before == position), 1.0, 0.0)
    pick = chosen.astype(BF16)
    weights = dot_tn((chosen * weight).astype(BF16), jnp.ones((count, SIDE), BF16))
    out_ref[:, wide:] = weights.astype(BF16)
    tile = 7 * SIDE
    copies = []
    for n, start in enumerate(range(0, wide + SIDE, tile)):
        stop = min(start + tile, wide)
        out_ref[:, start:stop] = dot_tn(pick, group_ref[:, start:stop]).astype(BF16)
        span = (slice(None), pl.ds(start, tile))
        copies += start_copies([(out_ref.at[span], out_hbm.at[span])], sems, n)
    wait_copies(copies)


def by_teacher(count, capacity, source_axis):
    source = lax.broadcasted_iota(jnp.int32, (count, count), source_axis)
    target = lax.broadcasted_iota(jnp.int32, (count, count), 1 - source_axis)
    group, inner = source // (PAIR * capacity), source % (PAIR * capacity)
    goes = (inner // capacity) * (count // PAIR) + group * capacity + inner % capacity
    return jnp.where(goes == target, 1.0, 0.0).astype(BF16)


def silu_split(value):
    logistic = jax.nn.sigmoid(value)
    return value * logistic, logistic * (1.0 + value * (1.0 - logistic))


def weights_kernel(t_gate_ref, t_up_ref, m_gate_ref, m_up_ref, t_come_ref, m_come_ref, out_ref):
    half, _ = place()
    block = m_gate_ref.shape[1]

    def put(at, *parts):
        for i, part in enumerate(parts):
            out_ref[at, i * block : (i + 1) * block] = part

    for m in range(PAIR):
        own = PAIR * half + m
        put(m, t_gate_ref[own], t_come_ref[m], t_up_ref[own], t_come_ref[PAIR + m])
    put(PAIR, m_gate_ref[0], m_come_ref[0], m_up_ref[0], m_come_ref[1])


def hidden_kernel(capacity, rows_ref, weights_ref, out_ref, slopes_ref, weight_ref):
    units = weights_ref.shape[1] // 2
    block = units // 2
    count, wide = rows_ref.shape
    features = wide - SIDE
    span = count // PAIR
    places = out_ref.shape[0] // PAIR
    rows = rows_ref[:, :features]
    move = by_teacher(count, capacity, 0)
    hidden = []
    for at in range(PAIR + 1):
        value = dot_nt(weights_ref[at], rows)
        gate, up = value[:units], value[units:]
        silu, slope = silu_split(gate)
        hidden.append((silu * up).astype(BF16))
        if at == PAIR:
            slopes_ref[0] = silu
            slopes_ref[1] = up * slope
    hidden = dot_nn(jnp.concatenate(hidden, axis=0), move).astype(BF16)
    weight_ref[...] = dot_tn(move, rows_ref[:, features:]).astype(BF16)
    student = hidden[PAIR * units :]
    for m in range(PAIR):
        lanes = slice(m * span, (m + 1) * span)
        teacher = hidden[m * units : (m + 1) * units]
        for i in range(places):
            at = m * places + i
            out_ref[at, 0] = student[:block, lanes]
            out_ref[at, 1] = student[block:, lanes]
            out_ref[at, 2] = teacher[:block, lanes]
            out_ref[at, 3] = teacher[block:, lanes]


def share_kernel(down_ref, merged_ref, *out_refs):
    half, at = place()
    quarter = out_refs[0].shape[2]
    for k, out_ref in enumerate(out_refs):
        there = (at + k) % RING
        m = there // (RING // PAIR)
        span = pl.ds(pl.multiple_of(there % (RING // PAIR) * quarter, SIDE), quarter)
        out_ref[0] = down_ref[PAIR * half + m, :, span]
        out_ref[1] = down_ref[PAIR * (1 - half) + m, :, span]
        out_ref[2] = merged_ref[0, :, span]


def pass_kernel(*refs):
    out_ref = refs[-1]
    for k, down_ref in enumerate(refs[:-1]):
        out_ref[k] = down_ref[1:]


def gap_kernel(hidden_ref, weight_ref, *refs):
    came_refs, down_refs = refs[:2], refs[2 : 2 + RING]
    grad_ref, kept_ref, other_ref = refs[2 + RING :]
    came = {
        k: came_ref.at[i] for came_ref, part in zip(came_refs, PARTS) for i, k in enumerate(part)
    }
    block = hidden_ref.shape[2]
    units = 2 * block
    span = hidden_ref.shape[3]
    _, at = place()
    back = [(at + RING - k) % RING for k in range(RING)]
    student = jnp.concatenate([hidden_ref[i, a] for i in back for a in (0, 1)], axis=0)
    teacher = jnp.concatenate([hidden_ref[i, a] for i in back for a in (2, 3)], axis=0)
    t_down = jnp.concatenate([x for k in range(RING) for x in (down_refs[k][0], came[k][0])], axis=0)
    m_down = jnp.concatenate([x for k in range(RING) for x in (down_refs[k][2], came[k][1])], axis=0)
    gap = dot_tn(student, m_down) - dot_tn(teacher, t_down)
    start = pl.multiple_of(at // (RING // PAIR) * span, span)
    weight = weight_ref[pl.ds(start, span), SIDE - 1 : SIDE].astype(F32)
    slot_grad = (weight * gap).astype(BF16)
    grad = dot_nt(m_down, slot_grad).astype(BF16)
    down_grad = dot_nn(student, slot_grad).astype(BF16)
    for k, i in enumerate(back):
        grad_ref[i] = grad[k * units : (k + 1) * units]
        kept_ref[i] = down_grad[k * units : k * units + block]
        other_ref[i] = down_grad[k * units + block : (k + 1) * units]


def other_kernel(capacity, parts_ref, slopes_ref, rows_ref, other_ref, stack_ref):
    block = other_ref.shape[1]
    places = parts_ref.shape[0] // PAIR
    units = parts_ref.shape[1]
    count = rows_ref.shape[0]
    parts = jnp.concatenate(
        [
            jnp.concatenate([parts_ref[m * places + i] for i in range(places)], axis=0)
            for m in range(PAIR)
        ],
        axis=1,
    )
    parts = dot_nn(parts, by_teacher(count, capacity, 1))
    total = parts[:units]
    for i in range(1, places):
        total += parts[i * units : (i + 1) * units]
    gate = (total * slopes_ref[1]).astype(BF16)
    up = (total * slopes_ref[0]).astype(BF16)
    stack_ref[...] = jnp.concatenate([gate[:block], up[:block]], axis=0)
    stack = jnp.concatenate([gate[block:], up[block:]], axis=0)
    grads = dot_nn(stack, rows_ref[:, : other_ref.shape[2]])
    other_ref[0] = grads[:block].astype(BF16)
    other_ref[1] = grads[block:].astype(BF16)


def own_kernel(stack_ref, rows_ref, own_ref):
    block = own_ref.shape[1]
    grads = dot_nn(stack_ref[...], rows_ref[:, : own_ref.shape[2]])
    own_ref[0] = grads[:block]
    own_ref[1] = grads[block:]


def down_sum_kernel(parts_ref, out_ref):
    count, _, piece = parts_ref.shape
    quarters = out_ref.shape[1] // piece
    for q in range(quarters):
        total = parts_ref[q].astype(F32)
        for i in range(q + quarters, count, quarters):
            total += parts_ref[i].astype(F32)
        out_ref[:, q * piece : (q + 1) * piece] = total


def body(
    tokens,
    teacher_ids,
    route_weight,
    teacher_gate,
    teacher_up,
    teacher_down,
    merged_gate,
    merged_up,
    merged_down,
):
    n_dp = HALVES * RING
    experts = lax.axis_size("expert")
    features = tokens.shape[2]
    capacity = tokens.shape[1]
    ranks = teacher_ids.shape[2]
    block = merged_gate.shape[1]
    wide = features + SIDE
    quarter = features * PAIR // RING
    rows = experts * PAIR * capacity
    span = rows // PAIR
    half = lax.axis_index("dp") // RING
    rings = [[a * RING + i for i in range(RING)] for a in range(HALVES)]
    swap = [(a * RING + i, (1 - a) * RING + i) for a in range(HALVES) for i in range(RING)]

    turns = [
        [(a * RING + i, a * RING + (i + k) % RING) for a in range(HALVES) for i in range(RING)]
        for k in range(RING)
    ]

    def exchange(array, axis_name, groups=None):
        return lax.all_to_all(
            array, axis_name, split_axis=0, concat_axis=0, tiled=True, axis_index_groups=groups
        )

    def halves(array, which):
        return lax.dynamic_slice_in_dim(array, PAIR * which, PAIR, axis=0)

    (packets,) = call(
        pack_kernel,
        (jax.ShapeDtypeStruct((n_dp, capacity, wide), BF16),),
        (teacher_ids.transpose(2, 0, 1), tokens[0], route_weight[0]),
        mib=60,
    )
    group = exchange(packets, "dp").reshape(n_dp * capacity, wide)

    down = call(
        share_kernel,
        tuple(jax.ShapeDtypeStruct((PAIR + 1, block, quarter), BF16) for _ in range(RING)),
        (teacher_down, merged_down),
    )
    down = [down[k] if k == 0 else lax.ppermute(down[k], "dp", turns[k]) for k in range(RING)]
    early = [down[k] for k in EARLY]
    m_come = lax.ppermute(jnp.concatenate([merged_gate, merged_up], axis=0), "dp", swap)
    group, early, m_come = lax.optimization_barrier((group, early, m_come))
    for k, array in zip(EARLY, early):
        down[k] = array

    (slots,) = call(
        lambda *refs: slots_kernel(ranks, capacity, *refs),
        (jax.ShapeDtypeStruct((rows, wide), BF16),),
        (group,),
        far_outs=(0,),
        scratch=[pltpu.VMEM((rows, wide), BF16), pltpu.SemaphoreType.DMA((8,))],
        mib=52,
    )
    slots = exchange(slots.reshape(experts, PAIR * capacity, wide), "expert").reshape(rows, wide)

    sent = [halves(teacher_gate, 1 - half), halves(teacher_up, 1 - half)]
    t_come = lax.ppermute(jnp.concatenate(sent, axis=0), "dp", swap)
    first, second = [
        call(
            pass_kernel,
            (jax.ShapeDtypeStruct((len(part), PAIR, block, quarter), BF16),),
            tuple(down[k] for k in part),
            mib=60,
        )[0]
        for part in PARTS
    ]
    first = lax.ppermute(first, "dp", swap)
    (weights,) = call(
        weights_kernel,
        (jax.ShapeDtypeStruct((PAIR + 1, 4 * block, features), BF16),),
        (teacher_gate, teacher_up, merged_gate, merged_up, t_come, m_come),
        mib=60,
    )
    slots, weights, first, second = lax.optimization_barrier((slots, weights, first, second))
    second = lax.ppermute(second, "dp", swap)

    hidden, slopes, weight = call(
        lambda *refs: hidden_kernel(capacity, *refs),
        (
            jax.ShapeDtypeStruct((RING, 4, block, span), BF16),
            jax.ShapeDtypeStruct((2, 2 * block, rows), F32),
            jax.ShapeDtypeStruct((rows, SIDE), BF16),
        ),
        (slots, weights),
        mib=32,
    )
    hidden = exchange(hidden, "dp", rings)
    hidden_grad, kept_down, other_down = call(
        gap_kernel,
        (
            jax.ShapeDtypeStruct((RING, 2 * block, span), BF16),
            jax.ShapeDtypeStruct((RING, block, quarter), BF16),
            jax.ShapeDtypeStruct((RING, block, quarter), BF16),
        ),
        (hidden, weight, first, second, *down),
        mib=60,
    )
    parts = exchange(hidden_grad, "dp", rings)
    other_down = lax.ppermute(other_down, "dp", swap)
    down_grad = (kept_down.astype(F32) + other_down.astype(F32)).astype(BF16)
    other, stack = call(
        lambda *refs: other_kernel(capacity, *refs),
        (
            jax.ShapeDtypeStruct((2, block, features), BF16),
            jax.ShapeDtypeStruct((2 * block, rows), BF16),
        ),
        (parts, slopes, slots),
    )
    (own,) = call(
        own_kernel, (jax.ShapeDtypeStruct((2, block, features), F32),), (stack, slots)
    )
    other = lax.ppermute(other, "dp", swap)
    down_grad = exchange(down_grad, "dp", rings)
    (grad_down,) = call(
        down_sum_kernel, (jax.ShapeDtypeStruct((block, features), F32),), (down_grad,)
    )
    grad_gate = own[:1] + other[:1].astype(F32)
    grad_up = own[1:] + other[1:].astype(F32)
    return grad_gate, grad_up, grad_down[None]


def solution(mesh):
    placed = (P("expert", "dp", None),) * 9
    return jax.shard_map(
        body,
        mesh=mesh,
        in_specs=placed,
        out_specs=(P("expert", "dp", None),) * 3,
        check_vma=False,
    )
```

```python
import jax
import jax.numpy as jnp
from jax import lax
from jax.experimental import pallas as pl
from jax.experimental.pallas import tpu as pltpu
from jax.sharding import PartitionSpec as P

HALVES = 2
PAIR = 2
EARLY = (1, 7)
PARTS = ((0, 1, 7), (2, 3, 4, 5, 6))
RING = 8
SIDE = 128
BF16 = jnp.bfloat16
F32 = jnp.float32


def dot_nn(a, b):
    return jnp.dot(a, b, preferred_element_type=F32)


def dot_nt(a, b):
    return lax.dot_general(a, b, (((1,), (1,)), ((), ())), preferred_element_type=F32)


def dot_tn(a, b):
    return lax.dot_general(a, b, (((0,), (0,)), ((), ())), preferred_element_type=F32)


def call(kernel, outs, args, far=(), far_outs=(), scratch=(), mib=16):
    def space(i, alone):
        return pl.BlockSpec(memory_space=pltpu.HBM if i in alone else pltpu.VMEM)

    return pl.pallas_call(
        kernel,
        out_shape=outs,
        in_specs=[space(i, far) for i in range(len(args))],
        out_specs=[space(i, far_outs) for i in range(len(outs))],
        scratch_shapes=scratch,
        compiler_params=pltpu.CompilerParams(vmem_limit_bytes=mib * 1024 * 1024),
        cost_estimate=pl.CostEstimate(
            flops=0,
            bytes_accessed=sum(a.size * a.dtype.itemsize for a in args),
            transcendentals=0,
        ),
    )(*args)


def start_copies(pairs, sems, first=0):
    copies = [
        pltpu.make_async_copy(source, target, sems.at[first + i])
        for i, (source, target) in enumerate(pairs)
    ]
    for copy in copies:
        copy.start()
    return copies


def wait_copies(copies):
    for copy in copies:
        copy.wait()


def place():
    at = lax.axis_index("dp")
    return at // RING, at % RING


def pack_kernel(ids_ref, token_ref, weight_ref, out_ref):
    ranks, _, count = ids_ref.shape
    features = token_ref.shape[1]
    lane = lax.broadcasted_iota(jnp.int32, (ranks, SIDE), 1)
    rank = lax.broadcasted_iota(jnp.int32, (ranks, SIDE), 0)
    spread = jnp.where(lane == rank, 1.0, 0.0).astype(BF16)
    ids = jnp.concatenate([ids_ref[k] for k in range(ranks)], axis=0)
    side = dot_tn(ids.astype(F32).astype(BF16), spread)
    lane = lax.broadcasted_iota(jnp.int32, (count, SIDE), 1)
    weight = weight_ref[...].astype(F32)
    for k in range(ranks):
        side = jnp.where(lane == ranks + k, weight[:, k : k + 1], side)
    side = side.astype(BF16)
    tokens = token_ref[...]
    for i in range(out_ref.shape[0]):
        out_ref[i, :, :features] = tokens
        out_ref[i, :, features:] = side


def slots_kernel(ranks, capacity, group_ref, out_hbm, out_ref, sems):
    half, _ = place()
    wide = group_ref.shape[1] - SIDE
    count = group_ref.shape[0]
    slots = out_ref.shape[0]
    side = group_ref[:, wide:].astype(F32)
    slot = lax.broadcasted_iota(jnp.int32, (count, slots), 1)
    column, inner = slot // (PAIR * capacity), slot % (PAIR * capacity)
    teacher = (column * HALVES * PAIR + half * PAIR + inner // capacity).astype(F32)
    position = (inner % capacity).astype(F32)
    hits = jnp.zeros((count, slots), F32)
    weight = jnp.zeros((count, slots), F32)
    for k in range(ranks):
        same = side[:, k : k + 1] == teacher
        hits = jnp.where(same, 1.0, hits)
        weight = jnp.where(same, side[:, ranks + k : ranks + k + 1], weight)
    later = lax.broadcasted_iota(jnp.int32, (count, count), 0)
    earlier = lax.broadcasted_iota(jnp.int32, (count, count), 1)
    below = jnp.where(earlier < later, 1.0, 0.0).astype(BF16)
    before = dot_nn(below, hits.astype(BF16))
    chosen = jnp.where((hits > 0.0) & (before == position), 1.0, 0.0)
    pick = chosen.astype(BF16)
    weights = dot_tn((chosen * weight).astype(BF16), jnp.ones((count, SIDE), BF16))
    out_ref[:, wide:] = weights.astype(BF16)
    tile = 7 * SIDE
    copies = []
    for n, start in enumerate(range(0, wide + SIDE, tile)):
        stop = min(start + tile, wide)
        out_ref[:, start:stop] = dot_tn(pick, group_ref[:, start:stop]).astype(BF16)
        span = (slice(None), pl.ds(start, tile))
        copies += start_copies([(out_ref.at[span], out_hbm.at[span])], sems, n)
    wait_copies(copies)


def by_teacher(count, capacity, source_axis):
    source = lax.broadcasted_iota(jnp.int32, (count, count), source_axis)
    target = lax.broadcasted_iota(jnp.int32, (count, count), 1 - source_axis)
    group, inner = source // (PAIR * capacity), source % (PAIR * capacity)
    goes = (inner // capacity) * (count // PAIR) + group * capacity + inner % capacity
    return jnp.where(goes == target, 1.0, 0.0).astype(BF16)


def silu_split(value):
    logistic = jax.nn.sigmoid(value)
    return value * logistic, logistic * (1.0 + value * (1.0 - logistic))


def weights_kernel(t_gate_ref, t_up_ref, m_gate_ref, m_up_ref, t_come_ref, m_come_ref, out_ref):
    half, _ = place()
    block = m_gate_ref.shape[1]

    def put(at, *parts):
        for i, part in enumerate(parts):
            out_ref[at, i * block : (i + 1) * block] = part

    for m in range(PAIR):
        own = PAIR * half + m
        put(m, t_gate_ref[own], t_come_ref[m], t_up_ref[own], t_come_ref[PAIR + m])
    put(PAIR, m_gate_ref[0], m_come_ref[0], m_up_ref[0], m_come_ref[1])


def hidden_kernel(
    capacity, rows_ref, weights_hbm, out_ref, slopes_ref, weight_ref, weights_ref, sems
):
    copies = start_copies(
        [(weights_hbm.at[at], weights_ref.at[at]) for at in (2, 0, 1)], sems
    )
    units = weights_ref.shape[1] // 2
    block = units // 2
    count, wide = rows_ref.shape
    features = wide - SIDE
    span = count // PAIR
    places = out_ref.shape[0] // PAIR
    rows = rows_ref[:, :features]
    move = by_teacher(count, capacity, 0)
    hidden = [None] * (PAIR + 1)
    for at, copy in zip((2, 0, 1), copies):
        copy.wait()
        value = dot_nt(weights_ref[at], rows)
        gate, up = value[:units], value[units:]
        silu, slope = silu_split(gate)
        hidden[at] = (silu * up).astype(BF16)
        if at == PAIR:
            slopes_ref[0] = silu
            slopes_ref[1] = up * slope
    hidden = dot_nn(jnp.concatenate(hidden, axis=0), move).astype(BF16)
    weight_ref[...] = dot_tn(move, rows_ref[:, features:]).astype(BF16)
    student = hidden[PAIR * units :]
    for m in range(PAIR):
        lanes = slice(m * span, (m + 1) * span)
        teacher = hidden[m * units : (m + 1) * units]
        for i in range(places):
            at = m * places + i
            out_ref[at, 0] = student[:block, lanes]
            out_ref[at, 1] = student[block:, lanes]
            out_ref[at, 2] = teacher[:block, lanes]
            out_ref[at, 3] = teacher[block:, lanes]


def share_kernel(down_ref, merged_ref, *out_refs):
    half, at = place()
    quarter = out_refs[0].shape[2]
    for k, out_ref in enumerate(out_refs):
        there = (at + k) % RING
        m = there // (RING // PAIR)
        span = pl.ds(pl.multiple_of(there % (RING // PAIR) * quarter, SIDE), quarter)
        out_ref[0] = down_ref[PAIR * half + m, :, span]
        out_ref[1] = down_ref[PAIR * (1 - half) + m, :, span]
        out_ref[2] = merged_ref[0, :, span]


def pass_kernel(*refs):
    out_ref = refs[-1]
    for k, down_ref in enumerate(refs[:-1]):
        out_ref[k] = down_ref[1:]


def gap_kernel(hidden_ref, weight_ref, *refs):
    came_refs, down_refs = refs[:2], refs[2 : 2 + RING]
    grad_ref, kept_ref, other_ref = refs[2 + RING :]
    came = {
        k: came_ref.at[i] for came_ref, part in zip(came_refs, PARTS) for i, k in enumerate(part)
    }
    block = hidden_ref.shape[2]
    units = 2 * block
    span = hidden_ref.shape[3]
    _, at = place()
    back = [(at + RING - k) % RING for k in range(RING)]
    student = jnp.concatenate([hidden_ref[i, a] for i in back for a in (0, 1)], axis=0)
    teacher = jnp.concatenate([hidden_ref[i, a] for i in back for a in (2, 3)], axis=0)
    t_down = jnp.concatenate([x for k in range(RING) for x in (down_refs[k][0], came[k][0])], axis=0)
    m_down = jnp.concatenate([x for k in range(RING) for x in (down_refs[k][2], came[k][1])], axis=0)
    gap = dot_tn(student, m_down) - dot_tn(teacher, t_down)
    start = pl.multiple_of(at // (RING // PAIR) * span, span)
    weight = weight_ref[pl.ds(start, span), SIDE - 1 : SIDE].astype(F32)
    slot_grad = (weight * gap).astype(BF16)
    grad = dot_nt(m_down, slot_grad).astype(BF16)
    down_grad = dot_nn(student, slot_grad).astype(BF16)
    for k, i in enumerate(back):
        grad_ref[i] = grad[k * units : (k + 1) * units]
        kept_ref[i] = down_grad[k * units : k * units + block]
        other_ref[i] = down_grad[k * units + block : (k + 1) * units]


def other_kernel(capacity, parts_ref, slopes_ref, rows_ref, other_ref, stack_ref):
    block = other_ref.shape[1]
    places = parts_ref.shape[0] // PAIR
    units = parts_ref.shape[1]
    count = rows_ref.shape[0]
    parts = jnp.concatenate(
        [
            jnp.concatenate([parts_ref[m * places + i] for i in range(places)], axis=0)
            for m in range(PAIR)
        ],
        axis=1,
    )
    parts = dot_nn(parts, by_teacher(count, capacity, 1))
    total = parts[:units]
    for i in range(1, places):
        total += parts[i * units : (i + 1) * units]
    gate = (total * slopes_ref[1]).astype(BF16)
    up = (total * slopes_ref[0]).astype(BF16)
    stack_ref[...] = jnp.concatenate([gate[:block], up[:block]], axis=0)
    stack = jnp.concatenate([gate[block:], up[block:]], axis=0)
    grads = dot_nn(stack, rows_ref[:, : other_ref.shape[2]])
    other_ref[0] = grads[:block].astype(BF16)
    other_ref[1] = grads[block:].astype(BF16)


def own_kernel(stack_ref, rows_ref, own_ref):
    block = own_ref.shape[1]
    grads = dot_nn(stack_ref[...], rows_ref[:, : own_ref.shape[2]])
    own_ref[0] = grads[:block]
    own_ref[1] = grads[block:]


def down_sum_kernel(parts_ref, out_ref):
    count, _, piece = parts_ref.shape
    quarters = out_ref.shape[1] // piece
    for q in range(quarters):
        total = parts_ref[q].astype(F32)
        for i in range(q + quarters, count, quarters):
            total += parts_ref[i].astype(F32)
        out_ref[:, q * piece : (q + 1) * piece] = total


def body(
    tokens,
    teacher_ids,
    route_weight,
    teacher_gate,
    teacher_up,
    teacher_down,
    merged_gate,
    merged_up,
    merged_down,
):
    n_dp = HALVES * RING
    experts = lax.axis_size("expert")
    features = tokens.shape[2]
    capacity = tokens.shape[1]
    ranks = teacher_ids.shape[2]
    block = merged_gate.shape[1]
    wide = features + SIDE
    quarter = features * PAIR // RING
    rows = experts * PAIR * capacity
    span = rows // PAIR
    half = lax.axis_index("dp") // RING
    rings = [[a * RING + i for i in range(RING)] for a in range(HALVES)]
    swap = [(a * RING + i, (1 - a) * RING + i) for a in range(HALVES) for i in range(RING)]

    turns = [
        [(a * RING + i, a * RING + (i + k) % RING) for a in range(HALVES) for i in range(RING)]
        for k in range(RING)
    ]

    def exchange(array, axis_name, groups=None):
        return lax.all_to_all(
            array, axis_name, split_axis=0, concat_axis=0, tiled=True, axis_index_groups=groups
        )

    def halves(array, which):
        return lax.dynamic_slice_in_dim(array, PAIR * which, PAIR, axis=0)

    (packets,) = call(
        pack_kernel,
        (jax.ShapeDtypeStruct((n_dp, capacity, wide), BF16),),
        (teacher_ids.transpose(2, 0, 1), tokens[0], route_weight[0]),
        mib=60,
    )
    group = exchange(packets, "dp").reshape(n_dp * capacity, wide)

    down = call(
        share_kernel,
        tuple(jax.ShapeDtypeStruct((PAIR + 1, block, quarter), BF16) for _ in range(RING)),
        (teacher_down, merged_down),
    )
    down = [down[k] if k == 0 else lax.ppermute(down[k], "dp", turns[k]) for k in range(RING)]
    early = [down[k] for k in EARLY]
    m_come = lax.ppermute(jnp.concatenate([merged_gate, merged_up], axis=0), "dp", swap)
    group, early, m_come = lax.optimization_barrier((group, early, m_come))
    for k, array in zip(EARLY, early):
        down[k] = array

    (slots,) = call(
        lambda *refs: slots_kernel(ranks, capacity, *refs),
        (jax.ShapeDtypeStruct((rows, wide), BF16),),
        (group,),
        far_outs=(0,),
        scratch=[pltpu.VMEM((rows, wide), BF16), pltpu.SemaphoreType.DMA((8,))],
        mib=52,
    )
    slots = exchange(slots.reshape(experts, PAIR * capacity, wide), "expert").reshape(rows, wide)

    sent = [halves(teacher_gate, 1 - half), halves(teacher_up, 1 - half)]
    t_come = lax.ppermute(jnp.concatenate(sent, axis=0), "dp", swap)
    first, second = [
        call(
            pass_kernel,
            (jax.ShapeDtypeStruct((len(part), PAIR, block, quarter), BF16),),
            tuple(down[k] for k in part),
            mib=60,
        )[0]
        for part in PARTS
    ]
    first = lax.ppermute(first, "dp", swap)
    (weights,) = call(
        weights_kernel,
        (jax.ShapeDtypeStruct((PAIR + 1, 4 * block, features), BF16),),
        (teacher_gate, teacher_up, merged_gate, merged_up, t_come, m_come),
        mib=60,
    )
    slots, weights, first, second = lax.optimization_barrier((slots, weights, first, second))
    second = lax.ppermute(second, "dp", swap)

    hidden, slopes, weight = call(
        lambda *refs: hidden_kernel(capacity, *refs),
        (
            jax.ShapeDtypeStruct((RING, 4, block, span), BF16),
            jax.ShapeDtypeStruct((2, 2 * block, rows), F32),
            jax.ShapeDtypeStruct((rows, SIDE), BF16),
        ),
        (slots, weights),
        far=(1,),
        scratch=[
            pltpu.VMEM((PAIR + 1, 4 * block, features), BF16),
            pltpu.SemaphoreType.DMA((PAIR + 1,)),
        ],
        mib=48,
    )
    hidden = exchange(hidden, "dp", rings)
    hidden_grad, kept_down, other_down = call(
        gap_kernel,
        (
            jax.ShapeDtypeStruct((RING, 2 * block, span), BF16),
            jax.ShapeDtypeStruct((RING, block, quarter), BF16),
            jax.ShapeDtypeStruct((RING, block, quarter), BF16),
        ),
        (hidden, weight, first, second, *down),
        mib=60,
    )
    parts = exchange(hidden_grad, "dp", rings)
    other_down = lax.ppermute(other_down, "dp", swap)
    down_grad = (kept_down.astype(F32) + other_down.astype(F32)).astype(BF16)
    other, stack = call(
        lambda *refs: other_kernel(capacity, *refs),
        (
            jax.ShapeDtypeStruct((2, block, features), BF16),
            jax.ShapeDtypeStruct((2 * block, rows), BF16),
        ),
        (parts, slopes, slots),
    )
    (own,) = call(
        own_kernel, (jax.ShapeDtypeStruct((2, block, features), F32),), (stack, slots)
    )
    other = lax.ppermute(other, "dp", swap)
    down_grad = exchange(down_grad, "dp", rings)
    (grad_down,) = call(
        down_sum_kernel, (jax.ShapeDtypeStruct((block, features), F32),), (down_grad,)
    )
    grad_gate = own[:1] + other[:1].astype(F32)
    grad_up = own[1:] + other[1:].astype(F32)
    return grad_gate, grad_up, grad_down[None]


def solution(mesh):
    placed = (P("expert", "dp", None),) * 9
    return jax.shard_map(
        body,
        mesh=mesh,
        in_specs=placed,
        out_specs=(P("expert", "dp", None),) * 3,
        check_vma=False,
    )
```
